32 devices in a mesh: seq: 8 (over y, x, core), tp: 4 (over z).
Axes of the slice: x: 2, y: 2, z: 4, core: 2. Of those that a mesh axis runs over, the one named last changes fastest.
Arguments:
- patches: bfloat16 [16384, 1280], P('seq', 'tp'), may hold values from -6 to 6
- route: int32 [256, 1], P('seq'), may hold values from 0 to 7; in each aligned block of 32 rows (0 to 31, 32 to 63, ...) at most 4 rows name the same one
- order: int32 [8, 32], P('seq'), may hold values from 0 to 31, each once within a row
- tiles: int32 [16], P('seq'), may hold values from 1 to 4
- w_qkv: bfloat16 [1280, 3840], P(None, 'tp'), may hold values from -0.15625 to 0.15625
- w_proj: bfloat16 [1280, 1280], P('tp'), may hold values from -0.15625 to 0.15625
- vit_gain: float32 [1280], replicated, may hold values from 0.1 to 1.9
- merge_gain: float32 [1280], replicated, may hold values from 0.1 to 1.9
- w_merge: bfloat16 [5120, 8192], P('seq', 'tp'), may hold values from -0.078125 to 0.078125
- llm_gain: float32 [8192], P('tp'), may hold values from 0.1 to 1.9
- w_cache: bfloat16 [8192, 2048], P('tp'), may hold values from -0.0625 to 0.0625
Outputs:
- kv_cache: bfloat16 [4096, 2048], P(('seq', 'tp'))
The draws below stay inside these ranges and needn't reach their ends.
Inputs may be any that keep to these rules, and one draw needn't show every extreme that they name: `route`: each seq index's 32 windows send exactly 4 windows to every seq index. `order`: each row is a permutation of 0 to 31.
All inputs are finite; a program needn't handle non-finite values.
Results may differ from the reference program's by a relative error of at most 0.019.
Values may be sent and summed in bfloat16 or wider, within the bound.
No kernel may reach another device: no remote copies, remote signals or barrier semaphores. Data moves between devices by JAX's collectives and lax.ppermute only.
A program may use at most 192 MiB of HBM per device.

```python
import math
import jax
import jax.numpy as jnp
import numpy as np
from jax import lax

DV = 1280
HV = 16
D = 8192
KVW = 2048
WIN = 64
MERGE = 4
TILE_WIN = 4
TILE_SLOTS = 4
FRAMES_DEV = 2
WIN_DEV = 32
CAP = 4
FRAMES = 16
ROWS = 16384
N_SEQ = 8
N_TP = 4


def with_ends(array, own_key, least, largest):
    longest = array.shape.index(max(array.shape))
    spots = []
    for shift in (0, 1):
        where = [jax.random.randint(jax.random.fold_in(own_key, axis), (), 0, length) for axis, length in enumerate(array.shape)]
        where[longest] = (where[longest] + shift) % array.shape[longest]
        spots.append(tuple(where))
    return array.at[spots[0]].set(least).at[spots[1]].set(largest)


def level_of(rng, shape, shards, least, largest):
    def one(position, shards_of):
        heights = jax.random.uniform(jax.random.fold_in(jax.random.fold_in(rng, 6), position), (shards_of,), jnp.float32, least / len(shards), largest / len(shards))
        return jnp.repeat(jnp.exp(heights), shape[position] // shards_of).reshape((-1,) + (1,) * (len(shape) - position - 1))

    gain = one(*shards[0])
    for cut in shards[1:]:
        gain = gain * one(*cut)
    return gain


def routed_block(rng, own, number, rows, amount, top, reach, skew):
    ranking = jax.random.permutation(rng, amount)
    crowded, common = portions_of(amount, rows * top, reach, skew, True), portions_of(amount, rows * top, reach, skew, False)
    places = jnp.arange(amount)

    def named(lengths, turn):
        used = int((lengths > 0).sum())
        fixed = max(1, used // 4)
        moved = fixed + (places - fixed + turn * (used - fixed)) % max(1, amount - fixed)
        return jnp.zeros((amount,), jnp.int32).at[ranking[jnp.where(places < fixed, places, moved)]].set(jnp.asarray(lengths, jnp.int32))

    lengths = jnp.where(number % 4 == 0, named(crowded, number // 4), named(common, number - number // 4 - 1))
    mixed = jax.random.permutation(jax.random.fold_in(own, 3), amount)
    source_of, receiver = mixed[0:amount // 2 * 2:2], mixed[1:amount // 2 * 2:2]
    margin = jnp.minimum(lengths[source_of] - 1, reach - lengths[receiver]) // 2
    margin = jnp.where((source_of == ranking[0]) | (receiver == ranking[0]) | (lengths[receiver] == 0), 0, jnp.maximum(margin, 0))
    moved = jax.random.randint(jax.random.fold_in(own, 4), (amount // 2,), 0, 1 << 20) % (margin + 1)
    lengths = lengths.at[source_of].add(-moved).at[receiver].add(moved)
    members = jnp.searchsorted(jnp.cumsum(lengths), jnp.arange(rows * top), side="right").astype(jnp.int32)
    grid = members.reshape(top, rows).T
    grid = grid[jax.random.permutation(jax.random.fold_in(own, 1), rows)]
    turn = jax.random.randint(jax.random.fold_in(own, 2), (rows, 1), 0, top)
    return jnp.take_along_axis(grid, (jnp.arange(top)[None, :] + turn) % top, axis=1)


def portions_of(count, total, most, slope, full):
    portions = [(1 << 20) // math.isqrt(grade ** slope) + 1 for grade in range(1, count + 1)]
    largest = most if full else min(most, max(-(-total // count), total * portions[0] // sum(portions)))
    least = 1 if total - largest >= count - 1 else 0
    holding, surplus = [largest] + [least] * (count - 1), total - largest - least * (count - 1)
    while surplus > 0:
        movable = [i for i in range(1, count) if holding[i] < largest] or [i for i in range(1, count) if holding[i] < most]
        mass, remaining = sum([portions[i] for i in movable]), surplus
        for i in movable:
            addition = min(most - holding[i], max(1, remaining * portions[i] // mass), surplus)
            holding[i] = holding[i] + addition
            surplus = surplus - addition
    return np.array(holding)


def noise(own_key, shape, spread, limit, shards=(), kind=jnp.bfloat16):
    loudness = level_of(own_key, shape, shards, -0.22, 0.18) if shards else 1.0
    drawn = jax.random.normal(own_key, shape, jnp.float32) * spread * loudness
    return jnp.minimum(jnp.maximum(drawn, -limit), limit).astype(kind)


def setup_inputs(seed: int = 0) -> dict:
    key_list = jax.random.split(jax.random.key(seed), 12)
    patches = noise(key_list[0], (ROWS, DV), 1.0, 6.0, ((0, 8), (1, 4)))
    route_keys = jax.random.split(jax.random.fold_in(key_list[1], 1), (N_SEQ * WIN_DEV) // WIN_DEV)
    route_turns = jax.random.permutation(jax.random.fold_in(key_list[1], 3), (N_SEQ * WIN_DEV) // WIN_DEV)
    route = jax.vmap(lambda own, number: routed_block(jax.random.fold_in(key_list[1], 2), own, number, WIN_DEV, N_SEQ, 1, CAP, 0))(route_keys, route_turns).reshape((N_SEQ * WIN_DEV, 1))
    order = jax.vmap(lambda own: jax.random.permutation(own, WIN_DEV))(jax.random.split(key_list[2], N_SEQ)).reshape((N_SEQ, WIN_DEV)).astype(jnp.int32)
    tiles = with_ends(jax.random.randint(key_list[3], (FRAMES,), 1, 5), jax.random.fold_in(key_list[3], 1), 1, 4).astype(jnp.int32)
    w_qkv = noise(key_list[4], (DV, 3 * DV), DV ** -0.5, 0.15625, ((1, 4),))
    w_proj = noise(key_list[5], (DV, DV), DV ** -0.5, 0.15625, ((0, 4),))
    vit_gain = jnp.clip(1.0 + 0.18 * jax.random.normal(key_list[6], (DV,), jnp.float32), 0.1, 1.9)
    merge_gain = jnp.clip(1.0 + 0.18 * jax.random.normal(key_list[7], (DV,), jnp.float32), 0.1, 1.9)
    w_merge = noise(key_list[8], (MERGE * DV, D), (MERGE * DV) ** -0.5, 0.078125, ((0, 8), (1, 4)))
    llm_gain = jnp.clip(1.0 + 0.18 * jax.random.normal(key_list[9], (D,), jnp.float32), 0.1, 1.9)
    w_cache = noise(key_list[10], (D, KVW), D ** -0.5, 0.0625, ((0, 4),))
    return {"patches": patches, "route": route, "order": order, "tiles": tiles, "w_qkv": w_qkv, "w_proj": w_proj, "vit_gain": vit_gain, "merge_gain": merge_gain, "w_merge": w_merge, "llm_gain": llm_gain, "w_cache": w_cache}


def encode_device(windows, live, w_qkv, w_proj, vit_gain, merge_gain, w_merge, llm_gain, w_cache):
    head_size = DV // HV
    rows = windows.reshape(-1, DV).astype(jnp.float32)
    scale_rows = lax.rsqrt(lax.optimization_barrier(jnp.mean(rows * rows, axis=1, keepdims=True)) + 1e-06)
    normed = (rows * scale_rows * vit_gain).astype(jnp.bfloat16)
    packed = jnp.dot(normed, w_qkv, preferred_element_type=jnp.float32).astype(jnp.bfloat16)
    packed = packed.reshape(WIN_DEV, WIN, HV, 3, head_size).astype(jnp.float32)
    query = packed[:, :, :, 0, :]
    keys = packed[:, :, :, 1, :]
    values = packed[:, :, :, 2, :]
    scores = jnp.einsum('wqhd,wkhd->whqk', query, keys) / jnp.sqrt(jnp.float32(head_size))
    probs = jax.nn.softmax(scores, axis=-1).astype(jnp.bfloat16).astype(jnp.float32)
    mixed = jnp.einsum('whqk,wkhd->wqhd', probs, values).astype(jnp.bfloat16)
    group = DV // N_TP
    mixed = mixed.reshape(-1, N_TP, group).astype(jnp.float32)
    proj_parts = jnp.einsum('rtg,tgo->tro', mixed, w_proj.reshape(N_TP, group, DV).astype(jnp.float32))
    proj = lax.optimization_barrier(jnp.sum(proj_parts.astype(jnp.bfloat16).astype(jnp.float32), axis=0))
    vit_out = (rows + proj).astype(jnp.bfloat16)
    patch_rows = vit_out.reshape(-1, MERGE, DV).astype(jnp.float32)
    patch_scale = lax.rsqrt(lax.optimization_barrier(jnp.mean(patch_rows * patch_rows, axis=2, keepdims=True)) + 1e-06)
    merged = (patch_rows * patch_scale * merge_gain).astype(jnp.bfloat16).reshape(-1, MERGE * DV)
    hidden = jnp.dot(merged, w_merge, preferred_element_type=jnp.float32).astype(jnp.bfloat16)
    wide = hidden.astype(jnp.float32)
    scaled = (wide * llm_gain).astype(jnp.bfloat16)
    cache = jnp.dot(scaled, w_cache, preferred_element_type=jnp.float32)
    squares = lax.optimization_barrier(jnp.sum(wide * wide, axis=1, keepdims=True))
    live_tokens = jnp.repeat(live, WIN // MERGE).astype(jnp.float32)
    return (cache * lax.rsqrt(squares / D + 1e-06) * live_tokens[:, None]).astype(jnp.bfloat16)

def reference(patches, route, order, tiles, w_qkv, w_proj, vit_gain, merge_gain, w_merge, llm_gain, w_cache):
    windows = patches.reshape(N_SEQ, WIN_DEV, WIN, DV)
    ordered = jnp.take_along_axis(windows, order[:, :, None, None], axis=1)
    tile_index = order // TILE_WIN
    frame = tile_index // TILE_SLOTS
    slot = tile_index % TILE_SLOTS
    counts = jnp.take_along_axis(tiles.reshape(N_SEQ, FRAMES_DEV), frame, axis=1)
    live = (slot < counts).astype(jnp.int32).reshape(-1)
    flat = ordered.reshape(N_SEQ * WIN_DEV, WIN, DV)
    arrange = jnp.argsort(route[:, 0], stable=True).astype(jnp.int32).reshape(N_SEQ, WIN_DEV)

    def one_device(picks):
        return encode_device(jnp.take(flat, picks, axis=0), jnp.take(live, picks), w_qkv, w_proj, vit_gain, merge_gain, w_merge, llm_gain, w_cache)
    return lax.map(one_device, arrange).reshape(-1, KVW)
```

```python
import functools

import jax
import jax.numpy as jnp
from jax import lax
from jax.experimental import pallas as pl
from jax.experimental.pallas import tpu as pltpu
from jax.sharding import PartitionSpec as P

DV = 1280
HV = 16
HS = DV // HV
D = 8192
WIN = 64
MERGE = 4
TILE_WIN = 4
TILE_SLOTS = 4
GROUP = 4
F32 = jnp.float32
BF = jnp.bfloat16
MIB = 1024 * 1024


def attend_kernel(tp, moves, nw, aliased, info, *refs):
    own = refs[0]
    right = refs[1:tp]
    left = refs[tp : 2 * tp - 1]
    at = 2 * tp - 1
    w_refs = refs[at : at + nw]
    vit_gain, merge_gain = refs[at + nw : at + nw + 2]
    at += nw + 2 + int(aliased)
    out = refs[at]
    w, xs, nrm, packed, mixed, vit, bias, sem = refs[at + 1 :]
    t = info[0]
    feats = own.shape[1]
    heads = HV // tp
    rows = packed.shape[0]
    first_proj = 3 * DV
    cols = xs.shape[1]
    step = pl.program_id(0)

    @pl.when(step == 0)
    def _():
        for copy in moves(info, w_refs, w, sem):
            copy.start()
        key = lax.broadcasted_iota(jnp.int32, (cols, cols), 0) // (WIN // MERGE) % GROUP
        query = lax.broadcasted_iota(jnp.int32, (cols, cols), 1) // (WIN // MERGE) % GROUP
        bias[...] = jnp.where(key == query, 0.0, -1e30).astype(F32)

    for j in range(tp):
        spot = pl.ds(pl.multiple_of(lax.rem(t + j, tp) * feats, feats), feats)
        if j == 0:
            xs[spot, :] = own[0]
        else:

            @pl.when(t + j < tp)
            def _():
                xs[spot, :] = right[j - 1][0]

            @pl.when(t + j >= tp)
            def _():
                xs[spot, :] = left[tp - j - 1][0]

    xf = xs[...].astype(F32)
    scale = lax.rsqrt(jnp.mean(xf * xf, axis=0, keepdims=True) + 1e-6)
    nrm[...] = (xf * scale * vit_gain[...]).astype(BF)

    @pl.when(step == 0)
    def _():
        for copy in moves(info, w_refs, w, sem):
            copy.wait()

    fold = (HS**-0.5) * 1.4426950408889634

    def group(g, carry):
        mine = w[pl.ds(pl.multiple_of(g * rows, rows), rows), :]
        packed[...] = jnp.dot(mine, nrm[...], preferred_element_type=F32).astype(BF)
        for h in range(heads):
            q, k, v = (packed[(3 * h + i) * HS : (3 * h + i + 1) * HS, :] for i in range(3))
            s = lax.dot_general(k, q, (((0,), (0,)), ((), ())), preferred_element_type=F32)
            s = s * fold + bias[...]
            p = jnp.exp2(s - jnp.max(s, axis=0, keepdims=True))
            total = jnp.sum(p, axis=0, keepdims=True)
            p = (p * (1.0 / total)).astype(BF)
            m = jnp.dot(v, p, preferred_element_type=F32).astype(BF)
            mixed[pl.ds(pl.multiple_of(g * heads * HS, heads * HS) + h * HS, HS), :] = m
        return carry

    lax.fori_loop(0, tp, group, 0)

    width = 256
    sums = jnp.zeros((cols, 1), F32)
    for n in range(DV // width):
        part = slice(n * width, (n + 1) * width)
        proj = lax.dot_general(
            mixed[...],
            w[first_proj : first_proj + DV, part],
            (((0,), (0,)), ((), ())),
            preferred_element_type=F32,
        )
        y = (xs[part, :].T.astype(F32) + proj).astype(BF)
        vit[:, part] = y
        yf = y.astype(F32)
        sums = sums + jnp.sum(yf * yf, axis=1, keepdims=True)
    scale = lax.rsqrt(sums * (1.0 / DV) + 1e-6)
    merged = (vit[...].astype(F32) * scale * merge_gain[...]).astype(BF)
    per = cols // MERGE
    for c in range(MERGE):
        out[c, 0] = merged[c * per : (c + 1) * per, :]


def attend(tp, info, own, right, left, weights, moves, count, vit_gain, merge_gain, blocks, buf):
    nb, feats, cols = own.shape
    per = cols // MERGE
    x_spec = pl.BlockSpec((1, feats, cols), lambda i, s: (i, 0, 0))
    anywhere = pl.BlockSpec(memory_space=pl.ANY)
    ins = [own, *right, *left, *weights, vit_gain, merge_gain]
    specs = [x_spec] * (2 * tp - 1) + [anywhere] * len(weights)
    specs += [pl.BlockSpec((DV, 1), lambda i, s: (0, 0)), pl.BlockSpec((1, DV), lambda i, s: (0, 0))]
    alias = {}
    if buf is not None:
        ins.append(buf)
        specs.append(anywhere)
        alias = {len(ins): 0}
    return pl.pallas_call(
        functools.partial(attend_kernel, tp, moves, len(weights), buf is not None),
        out_shape=jax.ShapeDtypeStruct((MERGE, blocks, per, DV), BF),
        grid_spec=pltpu.PrefetchScalarGridSpec(
            num_scalar_prefetch=1,
            grid=(nb,),
            in_specs=specs,
            out_specs=pl.BlockSpec((MERGE, 1, per, DV), lambda i, s: (0, s[2 + i], 0, 0)),
            scratch_shapes=[
                pltpu.VMEM((4 * DV, DV), BF),
                pltpu.VMEM((DV, cols), BF),
                pltpu.VMEM((DV, cols), BF),
                pltpu.VMEM((3 * DV // tp, cols), BF),
                pltpu.VMEM((DV, cols), BF),
                pltpu.VMEM((cols, DV), BF),
                pltpu.VMEM((cols, cols), F32),
                pltpu.SemaphoreType.DMA((count,)),
            ],
        ),
        input_output_aliases=alias,
        compiler_params=pltpu.CompilerParams(
            vmem_limit_bytes=48 * MIB, dimension_semantics=("arbitrary",)
        ),
        cost_estimate=pl.CostEstimate(
            flops=nb * cols * DV * DV * 10,
            bytes_accessed=14 * MIB,
            transcendentals=nb * cols * cols * HV,
        ),
        name="attend",
    )(info, *ins)


def project_kernel(moves, position, nw, info, *refs):
    merged = refs[0]
    w_refs = refs[1 : 1 + nw]
    w_cache, llm_gain, out = refs[1 + nw : 4 + nw]
    held, slots, cache, acc, scaled, held_sem, slot_sem, cache_sem = refs[4 + nw :]
    units = scaled.shape[1]
    half = units // 2
    rows = held.shape[1]
    depth = slots.shape[0]
    width = min(256, half)
    chunks = [(h, i) for h in range(2) for i in range(MERGE)]

    def bring(n):
        return moves(info, w_refs, *chunks[n], slots.at[n % depth], slot_sem.at[n % depth])

    def bring_merged(i):
        c = position(info, i)
        return pltpu.make_async_copy(merged.at[c], held.at[c], held_sem.at[i])

    load_cache = pltpu.make_async_copy(w_cache, cache, cache_sem)
    for n in range(depth):
        bring_merged(n).start()
        for copy in bring(n):
            copy.start()
    for n in range(depth, MERGE):
        bring_merged(n).start()
    load_cache.start()
    total = jnp.zeros((rows, 1), F32)
    for n, (h, i) in enumerate(chunks):
        c = position(info, i)
        if h == 0:
            bring_merged(i).wait()
        for copy in bring(n):
            copy.wait()
        slot = n % depth

        def tile(j, carry):
            spot = pl.ds(pl.multiple_of(j * width, width), width)
            d = jnp.dot(held[c], slots[slot, :, spot], preferred_element_type=F32)
            if i == 0:
                acc[:, spot] = d
            else:
                acc[:, spot] += d
            return carry

        lax.fori_loop(0, half // width, tile, 0)
        if n + depth < len(chunks):
            for copy in bring(n + depth):
                copy.start()
        if i == MERGE - 1:
            hidden = acc[...].astype(BF).astype(F32)
            total = total + jnp.sum(hidden * hidden, axis=1, keepdims=True)
            part = slice(h * half, (h + 1) * half)
            scaled[:, part] = (hidden * llm_gain[:, part]).astype(BF)
    load_cache.wait()
    kvw = cache.shape[1]

    def kv_tile(j, carry):
        spot = pl.ds(pl.multiple_of(j * 256, 256), 256)
        out[:, spot] = jnp.dot(scaled[...], cache[:, spot], preferred_element_type=F32).astype(BF)
        return carry

    lax.fori_loop(0, kvw // 256, kv_tile, 0)
    out[:, kvw:] = jnp.broadcast_to(total, (rows, 128)).astype(BF)


def project(info, merged, weights, moves, position, w_cache, llm_gain):
    units, kvw = w_cache.shape
    rows = merged.shape[1] * merged.shape[2]
    anywhere = pl.BlockSpec(memory_space=pl.ANY)
    return pl.pallas_call(
        functools.partial(project_kernel, moves, position, len(weights)),
        out_shape=jax.ShapeDtypeStruct((rows, kvw + 128), BF),
        grid_spec=pltpu.PrefetchScalarGridSpec(
            num_scalar_prefetch=1,
            grid=(1,),
            in_specs=[anywhere] * (len(weights) + 2)
            + [pl.BlockSpec((1, units), lambda i, s: (0, 0))],
            out_specs=pl.BlockSpec((rows, kvw + 128), lambda i, s: (0, 0)),
            scratch_shapes=[
                pltpu.VMEM((MERGE, rows, DV), BF),
                pltpu.VMEM((3, DV, units // 2), BF),
                pltpu.VMEM((units, kvw), BF),
                pltpu.VMEM((rows, units // 2), F32),
                pltpu.VMEM((rows, units), BF),
                pltpu.SemaphoreType.DMA((MERGE,)),
                pltpu.SemaphoreType.DMA((3, 2)),
                pltpu.SemaphoreType.DMA,
            ],
        ),
        compiler_params=pltpu.CompilerParams(
            vmem_limit_bytes=48 * MIB, dimension_semantics=("arbitrary",)
        ),
        cost_estimate=pl.CostEstimate(
            flops=2 * rows * units * (MERGE * DV + kvw),
            bytes_accessed=36 * MIB,
            transcendentals=0,
        ),
        name="project",
    )(info, merged.reshape(MERGE, rows, DV), *weights, w_cache, llm_gain)


def shards(
    patches, route, order, tiles, w_qkv, w_proj, vit_gain, merge_gain, w_merge, llm_gain, w_cache
):
    seq_count = lax.axis_size("seq")
    tp = lax.axis_size("tp")
    s = lax.axis_index("seq").astype(jnp.int32)
    t = lax.axis_index("tp").astype(jnp.int32)
    win_dev = order.shape[1]
    feats = patches.shape[1]
    per_peer = win_dev // seq_count
    tokens = WIN // MERGE
    blocks = win_dev // GROUP
    picks = order[0]
    tile_index = picks // TILE_WIN
    counts = jnp.take(tiles, tile_index // TILE_SLOTS)
    live = (tile_index % TILE_SLOTS < counts).astype(jnp.int32)
    arrange = jnp.argsort(route[:, 0], stable=True)
    live_send = jnp.take(live, arrange).reshape(seq_count, per_peer)
    live_here = lax.all_to_all(live_send, "seq", split_axis=0, concat_axis=0, tiled=True)
    window = jnp.take(picks, arrange).reshape(seq_count, per_peer)

    def xor(x, d):
        return lax.ppermute(x, "seq", [(i, i ^ d) for i in range(seq_count)])

    def along(x, k):
        return lax.ppermute(x, "tp", [(i, i + k) for i in range(tp) if 0 <= i + k < tp])

    def spread(x):
        right, left = [], []
        for _ in range(tp - 1):
            right.append(along(right[-1] if right else x, -1))
            left.append(along(left[-1] if left else x, 1))
        return right, left

    paired = per_peer == GROUP and seq_count == 8
    peers = jnp.arange(seq_count, dtype=jnp.int32)
    if paired:
        window = jnp.take(window, s ^ peers, axis=0)
    source = (
        window[:, None, :, None] * WIN
        + jnp.arange(tokens)[None, None, None, :] * MERGE
        + jnp.arange(MERGE)[None, :, None, None]
    ).reshape(-1)
    pick = (jnp.arange(patches.shape[0])[:, None] == source[None, :]).astype(BF)
    sent = lax.dot_general(
        patches, pick, (((0,), (0,)), ((), ())), preferred_element_type=F32
    ).astype(BF)
    step = per_peer * WIN
    wq_t = w_qkv.T

    if paired:
        parts = [sent[:, d * step : (d + 1) * step] for d in range(seq_count)]
        parts = [p if d == 0 else xor(p, d) for d, p in enumerate(parts)]
        groups = [jnp.stack(parts[:4]), jnp.stack(parts[4:])]
        places = [s ^ peers[:4], s ^ peers[4:]]

        share = (wq_t.shape[0] + w_proj.shape[0]) // seq_count
        q_parts = wq_t.shape[0] // share
        mine = jnp.where(
            s < q_parts,
            lax.dynamic_slice_in_dim(wq_t, jnp.minimum(s, q_parts - 1) * share, share),
            lax.dynamic_slice_in_dim(w_proj, jnp.maximum(s - q_parts, 0) * share, share),
        )
        right, left = spread(mine)
        others = jnp.concatenate(
            [jnp.where(t + j < tp, right[j - 1], left[tp - j - 1]) for j in range(1, tp)]
        )

        def plane(x):
            mid = x.shape[1] // 2
            halves = []
            for piece, bits in ((x[:, :mid], (2, 4)), (x[:, mid:], (4, 2))):
                held = {0: piece}
                for b in bits:
                    held.update({k ^ b: xor(v, b) for k, v in list(held.items())})
                held.update({k ^ 1: xor(v, 1) for k, v in list(held.items())})
                halves.append([held[d] for d in range(seq_count)])
            return halves

        vit_halves = plane(others)
        merge_halves = plane(w_merge)
        vit_weights = [wq_t, w_proj] + vit_halves[0] + vit_halves[1]
        merge_weights = merge_halves[0] + merge_halves[1]
        q_rows, p_rows = wq_t.shape[0], w_proj.shape[0]
        vit_count = 2 + 2 * seq_count * (tp - 1)

        def vit_moves(info, refs, w, sem):
            t, s = info[0], info[1]
            copies = [
                pltpu.make_async_copy(
                    refs[0], w.at[pl.ds(pl.multiple_of(t * q_rows, 16), q_rows)], sem.at[0]
                ),
                pltpu.make_async_copy(
                    refs[1], w.at[pl.ds(pl.multiple_of(3 * DV + t * p_rows, 16), p_rows)], sem.at[1]
                ),
            ]
            for h in range(2):
                for d in range(seq_count):
                    part = s ^ d
                    for j in range(1, tp):
                        q = lax.rem(t + j, tp)
                        row = jnp.where(
                            part < q_parts,
                            q * q_rows + part * share,
                            3 * DV + q * p_rows + (part - q_parts) * share,
                        )
                        copies.append(
                            pltpu.make_async_copy(
                                refs[2 + h * seq_count + d].at[(j - 1) * share : j * share],
                                w.at[
                                    pl.ds(pl.multiple_of(row, 16), share),
                                    h * (DV // 2) : (h + 1) * (DV // 2),
                                ],
                                sem.at[len(copies)],
                            )
                        )
            return copies

        def merge_moves(info, refs, h, i, slot, sem):
            s = info[1]
            rows = refs[0].shape[0]
            copies = []
            for e in range(2):
                at = pl.multiple_of(((s & 1) ^ e) * rows, 16)
                copies.append(
                    pltpu.make_async_copy(
                        refs[h * seq_count + 2 * i + e], slot.at[pl.ds(at, rows)], sem.at[e]
                    )
                )
            return copies

        def position(info, i):
            return (info[1] // 2) ^ i

    else:
        full = lax.all_to_all(
            sent.reshape(feats, seq_count, step).transpose(1, 0, 2),
            "seq",
            split_axis=0,
            concat_axis=0,
            tiled=True,
        )
        full = full.reshape(blocks, GROUP // per_peer, feats, MERGE, per_peer, tokens)
        groups = [full.transpose(0, 2, 3, 1, 4, 5).reshape(blocks, feats, GROUP * WIN)]
        places = [jnp.arange(blocks, dtype=jnp.int32)]
        vit_weights = [
            lax.all_gather(wq_t, "tp", axis=0, tiled=True),
            lax.all_gather(w_proj, "tp", axis=0, tiled=True),
        ]
        merge_weights = [lax.all_gather(w_merge, "seq", axis=0, tiled=True)]
        vit_count = 2

        def vit_moves(info, refs, w, sem):
            return [
                pltpu.make_async_copy(refs[0], w.at[0 : 3 * DV], sem.at[0]),
                pltpu.make_async_copy(refs[1], w.at[3 * DV : 4 * DV], sem.at[1]),
            ]

        def merge_moves(info, refs, h, i, slot, sem):
            wide = slot.shape[1]
            part = refs[0].at[i * DV : (i + 1) * DV, h * wide : (h + 1) * wide]
            return [pltpu.make_async_copy(part, slot, sem.at[0])]

        def position(info, i):
            return i

    merged = None
    for own, place in zip(groups, places):
        info = jnp.concatenate([jnp.stack([t, s]), place])
        right, left = spread(own)
        merged = attend(
            tp, info, own, right, left, vit_weights, vit_moves, vit_count,
            vit_gain[:, None], merge_gain[None, :], blocks, merged,
        )
    partial_value = project(
        jnp.stack([t, s]), merged, merge_weights, merge_moves, position, w_cache, llm_gain[None, :]
    )
    summed = lax.psum_scatter(partial_value, "tp", scatter_dimension=0, tiled=True).astype(F32)
    kvw = w_cache.shape[1]
    cache, total_squares = summed[:, :kvw], summed[:, kvw : kvw + 1]
    share = cache.shape[0]
    live_tokens = jnp.repeat(live_here.reshape(-1), tokens)
    mine = lax.dynamic_slice_in_dim(live_tokens, t * share, share).astype(F32)
    return (cache * lax.rsqrt(total_squares / D + 1e-6) * mine[:, None]).astype(BF)


def solution(mesh):
    return jax.shard_map(
        shards,
        mesh=mesh,
        in_specs=(
            P("seq", "tp"),
            P("seq", None),
            P("seq", None),
            P("seq"),
            P(None, "tp"),
            P("tp", None),
            P(),
            P(),
            P("seq", "tp"),
            P("tp"),
            P("tp", None),
        ),
        out_specs=P(("seq", "tp"), None),
        check_vma=False,
    )
```

```python
import functools

import jax
import jax.numpy as jnp
from jax import lax
from jax.experimental import pallas as pl
from jax.experimental.pallas import tpu as pltpu
from jax.sharding import PartitionSpec as P

DV = 1280
HV = 16
HS = DV // HV
D = 8192
WIN = 64
MERGE = 4
TILE_WIN = 4
TILE_SLOTS = 4
GROUP = 4
F32 = jnp.float32
BF = jnp.bfloat16
MIB = 1024 * 1024


def attend_kernel(tp, moves, nw, aliased, info, *refs):
    pieces = refs[:tp]
    at = tp
    w_refs = refs[at : at + nw]
    vit_gain, merge_gain = refs[at + nw : at + nw + 2]
    at += nw + 2 + int(aliased)
    out = refs[at]
    w, xs, nrm, packed, mixed, vit, bias, sem = refs[at + 1 :]
    t = info[0]
    feats = pieces[0].shape[1]
    heads = HV // tp
    rows = packed.shape[0]
    first_proj = 3 * DV
    cols = xs.shape[1]
    step = pl.program_id(0)

    @pl.when(step == 0)
    def _():
        for copy in moves(info, w_refs, w, sem):
            copy.start()
        key = lax.broadcasted_iota(jnp.int32, (cols, cols), 0) // (WIN // MERGE) % GROUP
        query = lax.broadcasted_iota(jnp.int32, (cols, cols), 1) // (WIN // MERGE) % GROUP
        bias[...] = jnp.where(key == query, 0.0, -1e30).astype(F32)

    for d, piece in enumerate(pieces):
        xs[pl.ds(pl.multiple_of((t ^ d) * feats, feats), feats), :] = piece[0]

    xf = xs[...].astype(F32)
    scale = lax.rsqrt(jnp.mean(xf * xf, axis=0, keepdims=True) + 1e-6)
    nrm[...] = (xf * scale * vit_gain[...]).astype(BF)

    @pl.when(step == 0)
    def _():
        for copy in moves(info, w_refs, w, sem):
            copy.wait()

    fold = (HS**-0.5) * 1.4426950408889634

    def group(g, carry):
        mine = w[pl.ds(pl.multiple_of(g * rows, rows), rows), :]
        packed[...] = jnp.dot(mine, nrm[...], preferred_element_type=F32).astype(BF)
        for h in range(heads):
            q, k, v = (packed[(3 * h + i) * HS : (3 * h + i + 1) * HS, :] for i in range(3))
            s = lax.dot_general(k, q, (((0,), (0,)), ((), ())), preferred_element_type=F32)
            s = s * fold + bias[...]
            p = jnp.exp2(s - jnp.max(s, axis=0, keepdims=True))
            total = jnp.sum(p, axis=0, keepdims=True)
            p = (p * (1.0 / total)).astype(BF)
            m = jnp.dot(v, p, preferred_element_type=F32).astype(BF)
            mixed[pl.ds(pl.multiple_of(g * heads * HS, heads * HS) + h * HS, HS), :] = m
        return carry

    lax.fori_loop(0, tp, group, 0)

    width = 256
    sums = jnp.zeros((cols, 1), F32)
    for n in range(DV // width):
        part = slice(n * width, (n + 1) * width)
        proj = lax.dot_general(
            mixed[...],
            w[first_proj : first_proj + DV, part],
            (((0,), (0,)), ((), ())),
            preferred_element_type=F32,
        )
        y = (xs[part, :].T.astype(F32) + proj).astype(BF)
        vit[:, part] = y
        yf = y.astype(F32)
        sums = sums + jnp.sum(yf * yf, axis=1, keepdims=True)
    scale = lax.rsqrt(sums * (1.0 / DV) + 1e-6)
    merged = (vit[...].astype(F32) * scale * merge_gain[...]).astype(BF)
    per = cols // MERGE
    for c in range(MERGE):
        out[c, 0] = merged[c * per : (c + 1) * per, :]


def attend(tp, info, pieces, weights, moves, count, vit_gain, merge_gain, blocks, buf):
    nb, feats, cols = pieces[0].shape
    per = cols // MERGE
    x_spec = pl.BlockSpec((1, feats, cols), lambda i, s: (i, 0, 0))
    anywhere = pl.BlockSpec(memory_space=pl.ANY)
    ins = [*pieces, *weights, vit_gain, merge_gain]
    specs = [x_spec] * tp + [anywhere] * len(weights)
    specs += [pl.BlockSpec((DV, 1), lambda i, s: (0, 0)), pl.BlockSpec((1, DV), lambda i, s: (0, 0))]
    alias = {}
    if buf is not None:
        ins.append(buf)
        specs.append(anywhere)
        alias = {len(ins): 0}
    return pl.pallas_call(
        functools.partial(attend_kernel, tp, moves, len(weights), buf is not None),
        out_shape=jax.ShapeDtypeStruct((MERGE, blocks, per, DV), BF),
        grid_spec=pltpu.PrefetchScalarGridSpec(
            num_scalar_prefetch=1,
            grid=(nb,),
            in_specs=specs,
            out_specs=pl.BlockSpec((MERGE, 1, per, DV), lambda i, s: (0, s[2 + i], 0, 0)),
            scratch_shapes=[
                pltpu.VMEM((4 * DV, DV), BF),
                pltpu.VMEM((DV, cols), BF),
                pltpu.VMEM((DV, cols), BF),
                pltpu.VMEM((3 * DV // tp, cols), BF),
                pltpu.VMEM((DV, cols), BF),
                pltpu.VMEM((cols, DV), BF),
                pltpu.VMEM((cols, cols), F32),
                pltpu.SemaphoreType.DMA((count,)),
            ],
        ),
        input_output_aliases=alias,
        compiler_params=pltpu.CompilerParams(
            vmem_limit_bytes=48 * MIB, dimension_semantics=("arbitrary",)
        ),
        cost_estimate=pl.CostEstimate(
            flops=nb * cols * DV * DV * 10,
            bytes_accessed=14 * MIB,
            transcendentals=nb * cols * cols * HV,
        ),
        name="attend",
    )(info, *ins)


def project_kernel(moves, position, nw, info, *refs):
    merged = refs[0]
    w_refs = refs[1 : 1 + nw]
    w_cache, llm_gain, out = refs[1 + nw : 4 + nw]
    held, slots, cache, acc, scaled, held_sem, slot_sem, cache_sem = refs[4 + nw :]
    units = scaled.shape[1]
    half = units // 2
    rows = held.shape[1]
    depth = slots.shape[0]
    width = min(256, half)
    chunks = [(h, i) for h in range(2) for i in range(MERGE)]

    def bring(n):
        return moves(info, w_refs, *chunks[n], slots.at[n % depth], slot_sem.at[n % depth])

    def bring_merged(i):
        c = position(info, i)
        return pltpu.make_async_copy(merged.at[c], held.at[c], held_sem.at[i])

    load_cache = pltpu.make_async_copy(w_cache, cache, cache_sem)
    for n in range(depth):
        bring_merged(n).start()
        for copy in bring(n):
            copy.start()
    for n in range(depth, MERGE):
        bring_merged(n).start()
    load_cache.start()
    total = jnp.zeros((rows, 1), F32)
    for n, (h, i) in enumerate(chunks):
        c = position(info, i)
        if h == 0:
            bring_merged(i).wait()
        for copy in bring(n):
            copy.wait()
        slot = n % depth

        def tile(j, carry):
            spot = pl.ds(pl.multiple_of(j * width, width), width)
            d = jnp.dot(held[c], slots[slot, :, spot], preferred_element_type=F32)
            if i == 0:
                acc[:, spot] = d
            else:
                acc[:, spot] += d
            return carry

        lax.fori_loop(0, half // width, tile, 0)
        if n + depth < len(chunks):
            for copy in bring(n + depth):
                copy.start()
        if i == MERGE - 1:
            hidden = acc[...].astype(BF).astype(F32)
            total = total + jnp.sum(hidden * hidden, axis=1, keepdims=True)
            part = slice(h * half, (h + 1) * half)
            scaled[:, part] = (hidden * llm_gain[:, part]).astype(BF)
    load_cache.wait()
    kvw = cache.shape[1]

    def kv_tile(j, carry):
        spot = pl.ds(pl.multiple_of(j * 256, 256), 256)
        out[:, spot] = jnp.dot(scaled[...], cache[:, spot], preferred_element_type=F32).astype(BF)
        return carry

    lax.fori_loop(0, kvw // 256, kv_tile, 0)
    out[:, kvw:] = jnp.broadcast_to(total, (rows, 128)).astype(BF)


def project(info, merged, weights, moves, position, w_cache, llm_gain):
    units, kvw = w_cache.shape
    rows = merged.shape[1] * merged.shape[2]
    anywhere = pl.BlockSpec(memory_space=pl.ANY)
    return pl.pallas_call(
        functools.partial(project_kernel, moves, position, len(weights)),
        out_shape=jax.ShapeDtypeStruct((rows, kvw + 128), BF),
        grid_spec=pltpu.PrefetchScalarGridSpec(
            num_scalar_prefetch=1,
            grid=(1,),
            in_specs=[anywhere] * (len(weights) + 2)
            + [pl.BlockSpec((1, units), lambda i, s: (0, 0))],
            out_specs=pl.BlockSpec((rows, kvw + 128), lambda i, s: (0, 0)),
            scratch_shapes=[
                pltpu.VMEM((MERGE, rows, DV), BF),
                pltpu.VMEM((3, DV, units // 2), BF),
                pltpu.VMEM((units, kvw), BF),
                pltpu.VMEM((rows, units // 2), F32),
                pltpu.VMEM((rows, units), BF),
                pltpu.SemaphoreType.DMA((MERGE,)),
                pltpu.SemaphoreType.DMA((3, 4)),
                pltpu.SemaphoreType.DMA,
            ],
        ),
        compiler_params=pltpu.CompilerParams(
            vmem_limit_bytes=48 * MIB, dimension_semantics=("arbitrary",)
        ),
        cost_estimate=pl.CostEstimate(
            flops=2 * rows * units * (MERGE * DV + kvw),
            bytes_accessed=36 * MIB,
            transcendentals=0,
        ),
        name="project",
    )(info, merged.reshape(MERGE, rows, DV), *weights, w_cache, llm_gain)


def shards(
    patches, route, order, tiles, w_qkv, w_proj, vit_gain, merge_gain, w_merge, llm_gain, w_cache
):
    seq_count = lax.axis_size("seq")
    tp = lax.axis_size("tp")
    s = lax.axis_index("seq").astype(jnp.int32)
    t = lax.axis_index("tp").astype(jnp.int32)
    win_dev = order.shape[1]
    feats = patches.shape[1]
    per_peer = win_dev // seq_count
    tokens = WIN // MERGE
    blocks = win_dev // GROUP
    picks = order[0]
    tile_index = picks // TILE_WIN
    counts = jnp.take(tiles, tile_index // TILE_SLOTS)
    live = (tile_index % TILE_SLOTS < counts).astype(jnp.int32)
    arrange = jnp.argsort(route[:, 0], stable=True)
    live_send = jnp.take(live, arrange).reshape(seq_count, per_peer)
    live_here = lax.all_to_all(live_send, "seq", split_axis=0, concat_axis=0, tiled=True)
    window = jnp.take(picks, arrange).reshape(seq_count, per_peer)

    def xor(x, d):
        return lax.ppermute(x, "seq", [(i, i ^ d) for i in range(seq_count)])

    def tie(x, after):
        return lax.optimization_barrier((x, after))[0]

    def tp_xor(x, d):
        return lax.ppermute(x, "tp", [(i, i ^ d) for i in range(tp)])

    def spread(x):
        held = {0: x}
        d = tp // 2
        while d:
            held.update({k ^ d: tp_xor(v, d) for k, v in list(held.items())})
            d //= 2
        return [held[d] for d in range(tp)]

    paired = seq_count == 8 and per_peer == GROUP

    source = (
        window[:, None, :, None] * WIN
        + jnp.arange(tokens)[None, None, None, :] * MERGE
        + jnp.arange(MERGE)[None, :, None, None]
    ).reshape(-1)
    pick = (jnp.arange(patches.shape[0])[:, None] == source[None, :]).astype(BF)
    sent = lax.dot_general(
        patches, pick, (((0,), (0,)), ((), ())), preferred_element_type=F32
    ).astype(BF)
    step = per_peer * WIN
    wq_t = w_qkv.T

    full = lax.all_to_all(
        sent.reshape(feats, seq_count, step).transpose(1, 0, 2),
        "seq",
        split_axis=0,
        concat_axis=0,
        tiled=True,
    )
    full = full.reshape(blocks, GROUP // per_peer, feats, MERGE, per_peer, tokens)
    full = full.transpose(0, 2, 3, 1, 4, 5).reshape(blocks, feats, GROUP * WIN)
    mid = blocks // 2

    if paired:
        share = (wq_t.shape[0] + w_proj.shape[0]) // seq_count
        q_parts = wq_t.shape[0] // share
        mine = jnp.where(
            s < q_parts,
            lax.dynamic_slice_in_dim(wq_t, jnp.minimum(s, q_parts - 1) * share, share),
            lax.dynamic_slice_in_dim(w_proj, jnp.maximum(s - q_parts, 0) * share, share),
        )
        others = jnp.concatenate(spread(mine)[1:])

        def sides(x):
            return list(lax.optimization_barrier((xor(x, 2), xor(x, 4))))

        def corners(by_x, by_y):
            half = by_x.shape[0] // 2
            return [xor(by_x[:half], 4), xor(by_y[half:], 2)]

        def cores(pieces):
            return [xor(v, 1) for v in pieces]

        vit_pieces = [others] + sides(others)
        vit_pieces += list(lax.optimization_barrier(tuple(corners(*vit_pieces[1:]))))
        merge_pieces = [w_merge] + sides(tie(w_merge, vit_pieces[3]))
        vit_weights = [wq_t, w_proj] + vit_pieces + cores(vit_pieces)
        q_rows, p_rows = wq_t.shape[0], w_proj.shape[0]

        def spans(rows):
            whole = [(0, 0, rows), (2, 0, rows), (4, 0, rows), (6, 0, rows // 2), (6, rows // 2, rows)]
            return [(d ^ e, lo, hi) for e in range(2) for d, lo, hi in whole]

        vit_parts = []
        for n, (d, lo, hi) in enumerate(spans(others.shape[0])):
            for j in range(1, tp):
                first, last = max(lo, (j - 1) * share), min(hi, j * share)
                if first < last:
                    vit_parts.append((n, d, j, first - lo, first - (j - 1) * share, last - first))
        vit_count = 2 + len(vit_parts)

        def vit_moves(info, refs, w, sem):
            t, s = info[0], info[1]
            copies = [
                pltpu.make_async_copy(
                    refs[0], w.at[pl.ds(pl.multiple_of(t * q_rows, 16), q_rows)], sem.at[0]
                ),
                pltpu.make_async_copy(
                    refs[1], w.at[pl.ds(pl.multiple_of(3 * DV + t * p_rows, 16), p_rows)], sem.at[1]
                ),
            ]
            for n, d, j, source, offset, count in vit_parts:
                part = s ^ d
                q = t ^ j
                row = offset + jnp.where(
                    part < q_parts,
                    q * q_rows + part * share,
                    3 * DV + q * p_rows + (part - q_parts) * share,
                )
                copies.append(
                    pltpu.make_async_copy(
                        refs[2 + n].at[source : source + count],
                        w.at[pl.ds(pl.multiple_of(row, 16), count)],
                        sem.at[len(copies)],
                    )
                )
            return copies

        def merge_moves(info, refs, h, i, slot, sem):
            s = info[1]
            wide = slot.shape[1]
            rows = slot.shape[0] // 2
            copies = []
            for n, (d, lo, hi) in enumerate(spans(rows)):
                if d // 2 == i:
                    at = pl.multiple_of(((s ^ d) & 1) * rows + lo, 16)
                    copies.append(
                        pltpu.make_async_copy(
                            refs[n].at[:, h * wide : (h + 1) * wide],
                            slot.at[pl.ds(at, hi - lo)],
                            sem.at[len(copies)],
                        )
                    )
            return copies

        def position(info, i):
            return (info[1] // 2) ^ i

    else:
        vit_weights = [
            lax.all_gather(wq_t, "tp", axis=0, tiled=True),
            lax.all_gather(w_proj, "tp", axis=0, tiled=True),
        ]
        merge_weights = [lax.all_gather(w_merge, "seq", axis=0, tiled=True)]
        vit_count = 2

        def vit_moves(info, refs, w, sem):
            return [
                pltpu.make_async_copy(refs[0], w.at[0 : 3 * DV], sem.at[0]),
                pltpu.make_async_copy(refs[1], w.at[3 * DV : 4 * DV], sem.at[1]),
            ]

        def merge_moves(info, refs, h, i, slot, sem):
            wide = slot.shape[1]
            part = refs[0].at[i * DV : (i + 1) * DV, h * wide : (h + 1) * wide]
            return [pltpu.make_async_copy(part, slot, sem.at[0])]

        def position(info, i):
            return i

    def encode(first, pieces, buf):
        info = jnp.concatenate([jnp.stack([t, s]), first + jnp.arange(mid, dtype=jnp.int32)])
        return attend(
            tp, info, pieces, vit_weights, vit_moves, vit_count,
            vit_gain[:, None], merge_gain[None, :], blocks, buf,
        )

    if paired:
        near = list(lax.optimization_barrier((tp_xor(full[:mid], 2), tp_xor(full[:mid], 1))))
        later = tie(full[mid:], near[0])
        far = [tp_xor(later, 2), tp_xor(later, 1)]
        merged = encode(0, [full[:mid], near[1], near[0], tp_xor(near[0], 1)], None)
        merged, far, by = lax.optimization_barrier((merged, far, merge_pieces[1:]))
        merge_pieces = [w_merge] + by + corners(*by)
        merge_weights = merge_pieces + cores(merge_pieces)
        merged = encode(mid, [full[mid:], far[1], far[0], tp_xor(far[0], 1)], merged)
    else:
        merged = None
        for first in (0, mid):
            merged = encode(first, spread(full[first : first + mid]), merged)
    partial_value = project(
        jnp.stack([t, s]), merged, merge_weights, merge_moves, position, w_cache, llm_gain[None, :]
    )
    summed = lax.psum_scatter(partial_value, "tp", scatter_dimension=0, tiled=True).astype(F32)
    kvw = w_cache.shape[1]
    cache, total_squares = summed[:, :kvw], summed[:, kvw : kvw + 1]
    share = cache.shape[0]
    live_tokens = jnp.repeat(live_here.reshape(-1), tokens)
    mine = lax.dynamic_slice_in_dim(live_tokens, t * share, share).astype(F32)
    return (cache * lax.rsqrt(total_squares / D + 1e-6) * mine[:, None]).astype(BF)


def solution(mesh):
    return jax.shard_map(
        shards,
        mesh=mesh,
        in_specs=(
            P("seq", "tp"),
            P("seq", None),
            P("seq", None),
            P("seq"),
            P(None, "tp"),
            P("tp", None),
            P(),
            P(),
            P("seq", "tp"),
            P("tp"),
            P("tp", None),
        ),
        out_specs=P(("seq", "tp"), None),
        check_vma=False,
    )
```

```python
import functools

import jax
import jax.numpy as jnp
from jax import lax
from jax.experimental import pallas as pl
from jax.experimental.pallas import tpu as pltpu
from jax.sharding import PartitionSpec as P

DV = 1280
HV = 16
HS = DV // HV
D = 8192
WIN = 64
MERGE = 4
TILE_WIN = 4
TILE_SLOTS = 4
GROUP = 4
F32 = jnp.float32
BF = jnp.bfloat16
MIB = 1024 * 1024


def attend_kernel(tp, moves, nw, aliased, info, *refs):
    pieces = refs[:tp]
    at = tp
    w_refs = refs[at : at + nw]
    vit_gain, merge_gain = refs[at + nw : at + nw + 2]
    at += nw + 2 + int(aliased)
    out = refs[at]
    w, xs, nrm, packed, mixed, vit, sem = refs[at + 1 :]
    t = info[0]
    heads = HV // tp
    rows = packed.shape[1]
    feats = pieces[0].shape[1]
    first_proj = 3 * DV
    cols = xs.shape[1]
    step = pl.program_id(0)

    @pl.when(step == 0)
    def _():
        for part in moves(info, w_refs, w, sem):
            for copy in part:
                copy.start()

    for d, piece in enumerate(pieces):
        xs[pl.ds(pl.multiple_of((t ^ d) * feats, feats), feats), :] = piece[0]

    xf = xs[...].astype(F32)
    scale = lax.rsqrt(jnp.mean(xf * xf, axis=0, keepdims=True) + 1e-6)
    nrm[...] = (xf * scale * vit_gain[...]).astype(BF)

    pair = 2 * WIN
    first = lax.broadcasted_iota(jnp.int32, (WIN, pair), 1) < WIN
    fold = (HS**-0.5) * 1.4426950408889634

    none = jnp.zeros((pair, pair), BF)

    def arrived(d):
        @pl.when(step == 0)
        def _():
            for copy in moves(info, w_refs, w, sem)[d]:
                copy.wait()

    def pack(d, slot):
        mine = w[pl.ds(pl.multiple_of((t ^ d) * rows, rows), rows), :]
        packed[slot] = jnp.dot(mine, nrm[...], preferred_element_type=F32).astype(BF)

    def heads_of(d, more):
        slot = lax.rem(d, 2)
        now = packed.at[slot]
        scores = []
        for h in range(heads):
            q, k = (now[(3 * h + n) * HS : (3 * h + n + 1) * HS, :] for n in range(2))
            s = lax.dot_general(k, q, (((0,), (0,)), ((), ())), preferred_element_type=F32)
            for n in range(cols // pair):
                at = n * pair
                s0, s1 = s[at : at + WIN, at : at + pair], s[at + WIN : at + pair, at : at + pair]
                scores.append(jnp.where(first, s0, s1) * fold)
        if more:
            pack(d + 1, 1 - slot)
        probs = []
        for s in scores:
            p = jnp.exp2(s - jnp.max(s, axis=0, keepdims=True))
            p = p * (1.0 / jnp.sum(p, axis=0, keepdims=True))
            probs.append(
                jnp.concatenate([jnp.where(first, p, 0.0), jnp.where(first, 0.0, p)]).astype(BF)
            )
        for h in range(heads):
            v = now[(3 * h + 2) * HS : (3 * h + 3) * HS, :]
            p = jnp.concatenate(
                [
                    jnp.concatenate([probs[2 * h], none], axis=1),
                    jnp.concatenate([none, probs[2 * h + 1]], axis=1),
                ]
            )
            m = jnp.dot(v, p, preferred_element_type=F32)
            at = pl.multiple_of((t ^ d) * heads * HS, heads * HS) + h * HS
            mixed[pl.ds(at, HS), :] = m.astype(BF)

    def one(d, carry):
        for later in range(1, tp):
            pl.when(d + 1 == later)(functools.partial(arrived, later))
        heads_of(d, True)
        return carry

    arrived(0)
    pack(0, 0)
    lax.fori_loop(0, tp - 1, one, 0)
    heads_of(jnp.int32(tp - 1), False)

    width = 256
    sums = jnp.zeros((cols, 1), F32)
    for n in range(DV // width):
        part = slice(n * width, (n + 1) * width)
        proj = lax.dot_general(
            mixed[...],
            w[first_proj : first_proj + DV, part],
            (((0,), (0,)), ((), ())),
            preferred_element_type=F32,
        )
        y = (xs[part, :].T.astype(F32) + proj).astype(BF)
        vit[:, part] = y
        yf = y.astype(F32)
        sums = sums + jnp.sum(yf * yf, axis=1, keepdims=True)
    scale = lax.rsqrt(sums * (1.0 / DV) + 1e-6)
    merged = (vit[...].astype(F32) * scale * merge_gain[...]).astype(BF)
    per = WIN // MERGE
    for w_at in range(cols // WIN):
        for c in range(MERGE):
            at = w_at * WIN + c * per
            out[c, 0, w_at * per : (w_at + 1) * per] = merged[at : at + per, :]


def attend(tp, info, pieces, weights, moves, count, vit_gain, merge_gain, blocks, buf):
    nb, feats, cols = pieces[0].shape
    per = cols // MERGE
    x_spec = pl.BlockSpec((1, feats, cols), lambda i, s: (i, 0, 0))
    anywhere = pl.BlockSpec(memory_space=pl.ANY)
    ins = [*pieces, *weights, vit_gain, merge_gain]
    specs = [x_spec] * tp + [anywhere] * len(weights)
    specs += [pl.BlockSpec((DV, 1), lambda i, s: (0, 0)), pl.BlockSpec((1, DV), lambda i, s: (0, 0))]
    alias = {}
    if buf is not None:
        ins.append(buf)
        specs.append(anywhere)
        alias = {len(ins): 0}
    return pl.pallas_call(
        functools.partial(attend_kernel, tp, moves, len(weights), buf is not None),
        out_shape=jax.ShapeDtypeStruct((MERGE, blocks, per, DV), BF),
        grid_spec=pltpu.PrefetchScalarGridSpec(
            num_scalar_prefetch=1,
            grid=(nb,),
            in_specs=specs,
            out_specs=pl.BlockSpec((MERGE, 1, per, DV), lambda i, s: (0, s[2 + i], 0, 0)),
            scratch_shapes=[
                pltpu.VMEM((4 * DV, DV), BF),
                pltpu.VMEM((DV, cols), BF),
                pltpu.VMEM((DV, cols), BF),
                pltpu.VMEM((2, 3 * DV // tp, cols), BF),
                pltpu.VMEM((DV, cols), BF),
                pltpu.VMEM((cols, DV), BF),
                pltpu.SemaphoreType.DMA((count,)),
            ],
        ),
        input_output_aliases=alias,
        compiler_params=pltpu.CompilerParams(
            vmem_limit_bytes=48 * MIB, dimension_semantics=("arbitrary",)
        ),
        cost_estimate=pl.CostEstimate(
            flops=nb * cols * DV * DV * 10,
            bytes_accessed=14 * MIB,
            transcendentals=nb * cols * cols * HV,
        ),
        name="attend",
    )(info, *ins)


def project_kernel(moves, position, nw, info, *refs):
    merged = refs[0]
    w_refs = refs[1 : 1 + nw]
    w_cache, llm_gain, out = refs[1 + nw : 4 + nw]
    held, slots, cache, acc, scaled, held_sem, slot_sem, cache_sem = refs[4 + nw :]
    units = scaled.shape[1]
    half = units // 2
    rows = held.shape[1]
    depth = slots.shape[0]
    width = min(256, half)
    chunks = [(h, i) for h in range(2) for i in range(MERGE)]

    def bring(n):
        return moves(info, w_refs, *chunks[n], slots.at[n % depth], slot_sem.at[n % depth])

    def bring_merged(i):
        c = position(info, i)
        return pltpu.make_async_copy(merged.at[c], held.at[c], held_sem.at[i])

    load_cache = pltpu.make_async_copy(w_cache, cache, cache_sem)
    for n in range(depth):
        bring_merged(n).start()
        for copy in bring(n):
            copy.start()
    for n in range(depth, MERGE):
        bring_merged(n).start()
    load_cache.start()
    total = jnp.zeros((rows, 1), F32)
    for n, (h, i) in enumerate(chunks):
        c = position(info, i)
        if h == 0:
            bring_merged(i).wait()
        for copy in bring(n):
            copy.wait()
        slot = n % depth

        def tile(j, carry):
            spot = pl.ds(pl.multiple_of(j * width, width), width)
            d = jnp.dot(held[c], slots[slot, :, spot], preferred_element_type=F32)
            if i == 0:
                acc[:, spot] = d
            else:
                acc[:, spot] += d
            return carry

        lax.fori_loop(0, half // width, tile, 0)
        if n + depth < len(chunks):
            for copy in bring(n + depth):
                copy.start()
        if i == MERGE - 1:
            hidden = acc[...].astype(BF).astype(F32)
            total = total + jnp.sum(hidden * hidden, axis=1, keepdims=True)
            part = slice(h * half, (h + 1) * half)
            scaled[:, part] = (hidden * llm_gain[:, part]).astype(BF)
    load_cache.wait()
    kvw = cache.shape[1]

    def kv_tile(j, carry):
        spot = pl.ds(pl.multiple_of(j * 256, 256), 256)
        out[:, spot] = jnp.dot(scaled[...], cache[:, spot], preferred_element_type=F32).astype(BF)
        return carry

    lax.fori_loop(0, kvw // 256, kv_tile, 0)
    out[:, kvw:] = jnp.broadcast_to(total, (rows, 128)).astype(BF)


def project(info, merged, weights, moves, position, w_cache, llm_gain):
    units, kvw = w_cache.shape
    rows = merged.shape[1] * merged.shape[2]
    anywhere = pl.BlockSpec(memory_space=pl.ANY)
    return pl.pallas_call(
        functools.partial(project_kernel, moves, position, len(weights)),
        out_shape=jax.ShapeDtypeStruct((rows, kvw + 128), BF),
        grid_spec=pltpu.PrefetchScalarGridSpec(
            num_scalar_prefetch=1,
            grid=(1,),
            in_specs=[anywhere] * (len(weights) + 2)
            + [pl.BlockSpec((1, units), lambda i, s: (0, 0))],
            out_specs=pl.BlockSpec((rows, kvw + 128), lambda i, s: (0, 0)),
            scratch_shapes=[
                pltpu.VMEM((MERGE, rows, DV), BF),
                pltpu.VMEM((3, DV, units // 2), BF),
                pltpu.VMEM((units, kvw), BF),
                pltpu.VMEM((rows, units // 2), F32),
                pltpu.VMEM((rows, units), BF),
                pltpu.SemaphoreType.DMA((MERGE,)),
                pltpu.SemaphoreType.DMA((3, 4)),
                pltpu.SemaphoreType.DMA,
            ],
        ),
        compiler_params=pltpu.CompilerParams(
            vmem_limit_bytes=48 * MIB, dimension_semantics=("arbitrary",)
        ),
        cost_estimate=pl.CostEstimate(
            flops=2 * rows * units * (MERGE * DV + kvw),
            bytes_accessed=36 * MIB,
            transcendentals=0,
        ),
        name="project",
    )(info, merged.reshape(MERGE, rows, DV), *weights, w_cache, llm_gain)


def shards(
    patches, route, order, tiles, w_qkv, w_proj, vit_gain, merge_gain, w_merge, llm_gain, w_cache
):
    seq_count = lax.axis_size("seq")
    tp = lax.axis_size("tp")
    s = lax.axis_index("seq").astype(jnp.int32)
    t = lax.axis_index("tp").astype(jnp.int32)
    win_dev = order.shape[1]
    feats = patches.shape[1]
    per_peer = win_dev // seq_count
    tokens = WIN // MERGE
    blocks = win_dev // GROUP
    picks = order[0]
    tile_index = picks // TILE_WIN
    counts = jnp.take(tiles, tile_index // TILE_SLOTS)
    live = (tile_index % TILE_SLOTS < counts).astype(jnp.int32)
    arrange = jnp.argsort(route[:, 0], stable=True)
    live_send = jnp.take(live, arrange).reshape(seq_count, per_peer)
    live_here = lax.all_to_all(live_send, "seq", split_axis=0, concat_axis=0, tiled=True)
    window = jnp.take(picks, arrange).reshape(seq_count, per_peer)

    def xor(x, d):
        return lax.ppermute(x, "seq", [(i, i ^ d) for i in range(seq_count)])

    def tie(x, after):
        return lax.optimization_barrier((x, after))[0]

    def tp_xor(x, d):
        return lax.ppermute(x, "tp", [(i, i ^ d) for i in range(tp)])

    def spread(x):
        held = {0: x}
        d = tp // 2
        while d:
            held.update({k ^ d: tp_xor(v, d) for k, v in list(held.items())})
            d //= 2
        return [held[d] for d in range(tp)]

    paired = seq_count == 8 and per_peer == GROUP

    source = (
        window[:, :, None, None] * WIN
        + jnp.arange(tokens)[None, None, None, :] * MERGE
        + jnp.arange(MERGE)[None, None, :, None]
    ).reshape(-1)
    pick = (jnp.arange(patches.shape[0])[:, None] == source[None, :]).astype(BF)
    sent = lax.dot_general(
        patches, pick, (((0,), (0,)), ((), ())), preferred_element_type=F32
    ).astype(BF)
    step = per_peer * WIN
    wq_t = w_qkv.T

    full = lax.all_to_all(
        sent.reshape(feats, seq_count, step).transpose(1, 0, 2),
        "seq",
        split_axis=0,
        concat_axis=0,
        tiled=True,
    )
    full = full.reshape(blocks, GROUP // per_peer, feats, step)
    full = full.transpose(0, 2, 1, 3).reshape(blocks, feats, GROUP * WIN)
    mid = blocks // 2

    if paired:
        share = (wq_t.shape[0] + w_proj.shape[0]) // seq_count
        q_parts = wq_t.shape[0] // share
        mine = jnp.where(
            s < q_parts,
            lax.dynamic_slice_in_dim(wq_t, jnp.minimum(s, q_parts - 1) * share, share),
            lax.dynamic_slice_in_dim(w_proj, jnp.maximum(s - q_parts, 0) * share, share),
        )
        early = lax.optimization_barrier((tp_xor(mine, 1), tp_xor(mine, 2)))
        others = [jnp.concatenate(early), tp_xor(early[1], 1)]
        held_planes = [(1, 2), (3,)]

        def sides(x):
            return list(lax.optimization_barrier((xor(x, 2), xor(x, 4))))

        def corners(by_x, by_y):
            half = by_x.shape[0] // 2
            return [xor(by_x[:half], 4), xor(by_y[half:], 2)]

        def cores(pieces):
            return [xor(v, 1) for v in pieces]

        first_by = sides(others[0])
        last_by = sides(tie(others[1], first_by))
        first_set = [others[0]] + first_by + corners(*first_by)
        last_set = [others[1]] + last_by + corners(*last_by)
        vit_weights = [wq_t, w_proj] + first_set + cores(first_set) + last_set + cores(last_set)
        merge_by = sides(tie(w_merge, last_by))
        q_rows, p_rows = wq_t.shape[0], w_proj.shape[0]

        def spans(rows):
            whole = [(0, 0, rows), (2, 0, rows), (4, 0, rows), (6, 0, rows // 2), (6, rows // 2, rows)]
            return [(d ^ e, lo, hi) for e in range(2) for d, lo, hi in whole]

        vit_parts = []
        for planes in held_planes:
            base = 2 + 10 * held_planes.index(planes)
            for n, (d, lo, hi) in enumerate(spans(share * len(planes))):
                for k, j in enumerate(planes):
                    top, end = max(lo, k * share), min(hi, (k + 1) * share)
                    if top < end:
                        vit_parts.append((base + n, d, j, top - lo, top - k * share, end - top))
        vit_count = 2 + len(vit_parts)

        def vit_moves(info, refs, w, sem):
            t, s = info[0], info[1]
            copies = [[] for _ in range(tp)]
            copies[0] = [
                pltpu.make_async_copy(
                    refs[0], w.at[pl.ds(pl.multiple_of(t * q_rows, 16), q_rows)], sem.at[0]
                ),
                pltpu.make_async_copy(
                    refs[1], w.at[pl.ds(pl.multiple_of(3 * DV + t * p_rows, 16), p_rows)], sem.at[1]
                ),
            ]
            for at, (n, d, j, source, offset, count) in enumerate(vit_parts):
                part = s ^ d
                q = t ^ j
                row = offset + jnp.where(
                    part < q_parts,
                    q * q_rows + part * share,
                    3 * DV + q * p_rows + (part - q_parts) * share,
                )
                copies[j].append(
                    pltpu.make_async_copy(
                        refs[n].at[source : source + count],
                        w.at[pl.ds(pl.multiple_of(row, 16), count)],
                        sem.at[2 + at],
                    )
                )
            return copies

        def merge_moves(info, refs, h, i, slot, sem):
            s = info[1]
            wide = slot.shape[1]
            rows = slot.shape[0] // 2
            copies = []
            for n, (d, lo, hi) in enumerate(spans(rows)):
                if d // 2 == i:
                    at = pl.multiple_of(((s ^ d) & 1) * rows + lo, 16)
                    copies.append(
                        pltpu.make_async_copy(
                            refs[n].at[:, h * wide : (h + 1) * wide],
                            slot.at[pl.ds(at, hi - lo)],
                            sem.at[len(copies)],
                        )
                    )
            return copies

        def position(info, i):
            return (info[1] // 2) ^ i

    else:
        vit_weights = [
            lax.all_gather(wq_t, "tp", axis=0, tiled=True),
            lax.all_gather(w_proj, "tp", axis=0, tiled=True),
        ]
        merge_weights = [lax.all_gather(w_merge, "seq", axis=0, tiled=True)]
        vit_count = 2 * tp
        q_rows, p_rows = wq_t.shape[0], w_proj.shape[0]

        def vit_moves(info, refs, w, sem):
            copies = []
            for d in range(tp):
                g = info[0] ^ d
                q_part = pl.ds(pl.multiple_of(g * q_rows, 16), q_rows)
                p_part = pl.ds(pl.multiple_of(g * p_rows, 16), p_rows)
                p_spot = pl.ds(pl.multiple_of(3 * DV + g * p_rows, 16), p_rows)
                copies.append(
                    [
                        pltpu.make_async_copy(refs[0].at[q_part], w.at[q_part], sem.at[2 * d]),
                        pltpu.make_async_copy(refs[1].at[p_part], w.at[p_spot], sem.at[2 * d + 1]),
                    ]
                )
            return copies

        def merge_moves(info, refs, h, i, slot, sem):
            wide = slot.shape[1]
            part = refs[0].at[i * DV : (i + 1) * DV, h * wide : (h + 1) * wide]
            return [pltpu.make_async_copy(part, slot, sem.at[0])]

        def position(info, i):
            return i

    def encode(first, pieces, buf):
        count = pieces[0].shape[0]
        info = jnp.concatenate([jnp.stack([t, s]), first + jnp.arange(count, dtype=jnp.int32)])
        return attend(
            tp, info, pieces, vit_weights, vit_moves, vit_count,
            vit_gain[:, None], merge_gain[None, :], blocks, buf,
        )

    merged = None
    if paired:
        cuts = [0, 2, 5, 8]
        near, done = [], []
        for lo, hi in zip(cuts[:-1], cuts[1:]):
            own = full[lo:hi] if not near else tie(full[lo:hi], near[-1])
            near.append(lax.optimization_barrier((tp_xor(own, 1), tp_xor(own, 2))))
        for n, lo in enumerate(cuts[:-1]):
            by1, by2 = near[n]
            if n >= 2:
                merged, by2 = lax.optimization_barrier((merged, by2))
            far = tp_xor(by2, 1)
            if n == len(cuts) - 2:
                merged, far, merge_by = lax.optimization_barrier((merged, far, merge_by))
            if n == 1:
                merged, live_here = lax.optimization_barrier((merged, live_here))
            merged = encode(lo, [full[lo : cuts[n + 1]], by1, by2, far], merged)
        merge_corners = corners(*merge_by)
        merged, merge_corners = lax.optimization_barrier((merged, merge_corners))
        merge_pieces = [w_merge] + list(merge_by) + list(merge_corners)
        merge_weights = merge_pieces + cores(merge_pieces)
    else:
        for first in (0, mid):
            merged = encode(first, spread(full[first : first + mid]), merged)
    partial_value = project(
        jnp.stack([t, s]), merged, merge_weights, merge_moves, position, w_cache, llm_gain[None, :]
    )
    summed = lax.psum_scatter(partial_value, "tp", scatter_dimension=0, tiled=True).astype(F32)
    kvw = w_cache.shape[1]
    cache, total_squares = summed[:, :kvw], summed[:, kvw : kvw + 1]
    share = cache.shape[0]
    live_tokens = jnp.repeat(live_here.reshape(-1), tokens)
    mine = lax.dynamic_slice_in_dim(live_tokens, t * share, share).astype(F32)
    return (cache * lax.rsqrt(total_squares / D + 1e-6) * mine[:, None]).astype(BF)


def solution(mesh):
    return jax.shard_map(
        shards,
        mesh=mesh,
        in_specs=(
            P("seq", "tp"),
            P("seq", None),
            P("seq", None),
            P("seq"),
            P(None, "tp"),
            P("tp", None),
            P(),
            P(),
            P("seq", "tp"),
            P("tp"),
            P("tp", None),
        ),
        out_specs=P(("seq", "tp"), None),
        check_vma=False,
    )
```

```python
import functools

import jax
import jax.numpy as jnp
from jax import lax
from jax.experimental import pallas as pl
from jax.experimental.pallas import tpu as pltpu
from jax.sharding import PartitionSpec as P

DV = 1280
HV = 16
HS = DV // HV
D = 8192
WIN = 64
MERGE = 4
TILE_WIN = 4
TILE_SLOTS = 4
GROUP = 4
F32 = jnp.float32
BF = jnp.bfloat16
MIB = 1024 * 1024


def attend_kernel(tp, moves, nw, aliased, info, *refs):
    pieces = refs[:tp]
    at = tp
    w_refs = refs[at : at + nw]
    vit_gain, merge_gain = refs[at + nw : at + nw + 2]
    at += nw + 2 + int(aliased)
    out = refs[at]
    w, xs, nrm, packed, mixed, vit, sem = refs[at + 1 :]
    t = info[0]
    heads = HV // tp
    rows = packed.shape[1]
    feats = pieces[0].shape[1]
    first_proj = 3 * DV
    cols = xs.shape[1]
    step = pl.program_id(0)

    @pl.when(step == 0)
    def _():
        for part in moves(info, w_refs, w, sem):
            for copy in part:
                copy.start()

    for d, piece in enumerate(pieces):
        xs[pl.ds(pl.multiple_of((t ^ d) * feats, feats), feats), :] = piece[0]

    xf = xs[...].astype(F32)
    scale = lax.rsqrt(jnp.mean(xf * xf, axis=0, keepdims=True) + 1e-6)
    nrm[...] = (xf * scale * vit_gain[...]).astype(BF)

    pair = 2 * WIN
    first = lax.broadcasted_iota(jnp.int32, (WIN, pair), 1) < WIN
    fold = (HS**-0.5) * 1.4426950408889634

    none = jnp.zeros((pair, pair), BF)

    def arrived(d):
        @pl.when(step == 0)
        def _():
            for copy in moves(info, w_refs, w, sem)[d]:
                copy.wait()

    def pack(d, slot):
        mine = w[pl.ds(pl.multiple_of((t ^ d) * rows, rows), rows), :]
        packed[slot] = jnp.dot(mine, nrm[...], preferred_element_type=F32).astype(BF)

    def heads_of(d, more):
        slot = lax.rem(d, 2)
        now = packed.at[slot]
        scores = []
        for h in range(heads):
            q, k = (now[(3 * h + n) * HS : (3 * h + n + 1) * HS, :] for n in range(2))
            s = lax.dot_general(k, q, (((0,), (0,)), ((), ())), preferred_element_type=F32)
            for n in range(cols // pair):
                at = n * pair
                s0, s1 = s[at : at + WIN, at : at + pair], s[at + WIN : at + pair, at : at + pair]
                scores.append(jnp.where(first, s0, s1) * fold)
        if more:
            pack(d + 1, 1 - slot)
        probs = []
        for s in scores:
            p = jnp.exp2(s - jnp.max(s, axis=0, keepdims=True))
            p = p * (1.0 / jnp.sum(p, axis=0, keepdims=True))
            probs.append(
                jnp.concatenate([jnp.where(first, p, 0.0), jnp.where(first, 0.0, p)]).astype(BF)
            )
        for h in range(heads):
            v = now[(3 * h + 2) * HS : (3 * h + 3) * HS, :]
            p = jnp.concatenate(
                [
                    jnp.concatenate([probs[2 * h], none], axis=1),
                    jnp.concatenate([none, probs[2 * h + 1]], axis=1),
                ]
            )
            m = jnp.dot(v, p, preferred_element_type=F32)
            at = pl.multiple_of((t ^ d) * heads * HS, heads * HS) + h * HS
            mixed[pl.ds(at, HS), :] = m.astype(BF)

    def one(d, carry):
        for later in range(1, tp):
            pl.when(d + 1 == later)(functools.partial(arrived, later))
        heads_of(d, True)
        return carry

    arrived(0)
    pack(0, 0)
    lax.fori_loop(0, tp - 1, one, 0)
    heads_of(jnp.int32(tp - 1), False)

    width = 256
    sums = jnp.zeros((cols, 1), F32)
    for n in range(DV // width):
        part = slice(n * width, (n + 1) * width)
        proj = lax.dot_general(
            mixed[...],
            w[first_proj : first_proj + DV, part],
            (((0,), (0,)), ((), ())),
            preferred_element_type=F32,
        )
        y = (xs[part, :].T.astype(F32) + proj).astype(BF)
        vit[:, part] = y
        yf = y.astype(F32)
        sums = sums + jnp.sum(yf * yf, axis=1, keepdims=True)
    scale = lax.rsqrt(sums * (1.0 / DV) + 1e-6)
    merged = (vit[...].astype(F32) * scale * merge_gain[...]).astype(BF)
    per = WIN // MERGE
    for w_at in range(cols // WIN):
        for c in range(MERGE):
            at = w_at * WIN + c * per
            out[c, 0, w_at * per : (w_at + 1) * per] = merged[at : at + per, :]


def attend(tp, info, pieces, weights, moves, count, vit_gain, merge_gain, blocks, buf):
    nb, feats, cols = pieces[0].shape
    per = cols // MERGE
    x_spec = pl.BlockSpec((1, feats, cols), lambda i, s: (i, 0, 0))
    anywhere = pl.BlockSpec(memory_space=pl.ANY)
    ins = [*pieces, *weights, vit_gain, merge_gain]
    specs = [x_spec] * tp + [anywhere] * len(weights)
    specs += [pl.BlockSpec((DV, 1), lambda i, s: (0, 0)), pl.BlockSpec((1, DV), lambda i, s: (0, 0))]
    alias = {}
    if buf is not None:
        ins.append(buf)
        specs.append(anywhere)
        alias = {len(ins): 0}
    return pl.pallas_call(
        functools.partial(attend_kernel, tp, moves, len(weights), buf is not None),
        out_shape=jax.ShapeDtypeStruct((MERGE, blocks, per, DV), BF),
        grid_spec=pltpu.PrefetchScalarGridSpec(
            num_scalar_prefetch=1,
            grid=(nb,),
            in_specs=specs,
            out_specs=pl.BlockSpec((MERGE, 1, per, DV), lambda i, s: (0, s[2 + i], 0, 0)),
            scratch_shapes=[
                pltpu.VMEM((4 * DV, DV), BF),
                pltpu.VMEM((DV, cols), BF),
                pltpu.VMEM((DV, cols), BF),
                pltpu.VMEM((2, 3 * DV // tp, cols), BF),
                pltpu.VMEM((DV, cols), BF),
                pltpu.VMEM((cols, DV), BF),
                pltpu.SemaphoreType.DMA((count,)),
            ],
        ),
        input_output_aliases=alias,
        compiler_params=pltpu.CompilerParams(
            vmem_limit_bytes=48 * MIB, dimension_semantics=("arbitrary",)
        ),
        cost_estimate=pl.CostEstimate(
            flops=nb * cols * DV * DV * 10,
            bytes_accessed=14 * MIB,
            transcendentals=nb * cols * cols * HV,
        ),
        name="attend",
    )(info, *ins)


def project_kernel(moves, position, nw, info, *refs):
    merged = refs[0]
    w_refs = refs[1 : 1 + nw]
    w_cache, llm_gain, out = refs[1 + nw : 4 + nw]
    held, slots, cache, acc, scaled, held_sem, slot_sem, cache_sem = refs[4 + nw :]
    units = scaled.shape[1]
    half = units // 2
    rows = held.shape[1]
    depth = slots.shape[0]
    width = min(256, half)
    chunks = [(h, i) for h in range(2) for i in range(MERGE)]

    def bring(n):
        return moves(info, w_refs, *chunks[n], slots.at[n % depth], slot_sem.at[n % depth])

    def bring_merged(i):
        c = position(info, i)
        return pltpu.make_async_copy(merged.at[c], held.at[c], held_sem.at[i])

    load_cache = pltpu.make_async_copy(w_cache, cache, cache_sem)
    for n in range(depth):
        bring_merged(n).start()
        for copy in bring(n):
            copy.start()
    for n in range(depth, MERGE):
        bring_merged(n).start()
    load_cache.start()
    total = jnp.zeros((rows, 1), F32)
    for n, (h, i) in enumerate(chunks):
        c = position(info, i)
        if h == 0:
            bring_merged(i).wait()
        for copy in bring(n):
            copy.wait()
        slot = n % depth

        def tile(j, carry):
            spot = pl.ds(pl.multiple_of(j * width, width), width)
            d = jnp.dot(held[c], slots[slot, :, spot], preferred_element_type=F32)
            if i == 0:
                acc[:, spot] = d
            else:
                acc[:, spot] += d
            return carry

        lax.fori_loop(0, half // width, tile, 0)
        if n + depth < len(chunks):
            for copy in bring(n + depth):
                copy.start()
        if i == MERGE - 1:
            hidden = acc[...].astype(BF).astype(F32)
            total = total + jnp.sum(hidden * hidden, axis=1, keepdims=True)
            part = slice(h * half, (h + 1) * half)
            scaled[:, part] = (hidden * llm_gain[:, part]).astype(BF)
    load_cache.wait()
    kvw = cache.shape[1]

    def kv_tile(j, carry):
        spot = pl.ds(pl.multiple_of(j * 256, 256), 256)
        out[:, spot] = jnp.dot(scaled[...], cache[:, spot], preferred_element_type=F32).astype(BF)
        return carry

    lax.fori_loop(0, kvw // 256, kv_tile, 0)
    out[:, kvw:] = jnp.broadcast_to(total, (rows, 128)).astype(BF)


def project(info, merged, weights, moves, position, w_cache, llm_gain):
    units, kvw = w_cache.shape
    rows = merged.shape[1] * merged.shape[2]
    anywhere = pl.BlockSpec(memory_space=pl.ANY)
    return pl.pallas_call(
        functools.partial(project_kernel, moves, position, len(weights)),
        out_shape=jax.ShapeDtypeStruct((rows, kvw + 128), BF),
        grid_spec=pltpu.PrefetchScalarGridSpec(
            num_scalar_prefetch=1,
            grid=(1,),
            in_specs=[anywhere] * (len(weights) + 2)
            + [pl.BlockSpec((1, units), lambda i, s: (0, 0))],
            out_specs=pl.BlockSpec((rows, kvw + 128), lambda i, s: (0, 0)),
            scratch_shapes=[
                pltpu.VMEM((MERGE, rows, DV), BF),
                pltpu.VMEM((3, DV, units // 2), BF),
                pltpu.VMEM((units, kvw), BF),
                pltpu.VMEM((rows, units // 2), F32),
                pltpu.VMEM((rows, units), BF),
                pltpu.SemaphoreType.DMA((MERGE,)),
                pltpu.SemaphoreType.DMA((3, 2)),
                pltpu.SemaphoreType.DMA,
            ],
        ),
        compiler_params=pltpu.CompilerParams(
            vmem_limit_bytes=48 * MIB, dimension_semantics=("arbitrary",)
        ),
        cost_estimate=pl.CostEstimate(
            flops=2 * rows * units * (MERGE * DV + kvw),
            bytes_accessed=36 * MIB,
            transcendentals=0,
        ),
        name="project",
    )(info, merged.reshape(MERGE, rows, DV), *weights, w_cache, llm_gain)


def shards(
    patches, route, order, tiles, w_qkv, w_proj, vit_gain, merge_gain, w_merge, llm_gain, w_cache
):
    seq_count = lax.axis_size("seq")
    tp = lax.axis_size("tp")
    s = lax.axis_index("seq").astype(jnp.int32)
    t = lax.axis_index("tp").astype(jnp.int32)
    win_dev = order.shape[1]
    feats = patches.shape[1]
    per_peer = win_dev // seq_count
    tokens = WIN // MERGE
    blocks = win_dev // GROUP
    picks = order[0]
    tile_index = picks // TILE_WIN
    counts = jnp.take(tiles, tile_index // TILE_SLOTS)
    live = (tile_index % TILE_SLOTS < counts).astype(jnp.int32)
    arrange = jnp.argsort(route[:, 0], stable=True)
    live_send = jnp.take(live, arrange).reshape(seq_count, per_peer)
    live_here = lax.all_to_all(live_send, "seq", split_axis=0, concat_axis=0, tiled=True)
    window = jnp.take(picks, arrange).reshape(seq_count, per_peer)

    def xor(x, d):
        return lax.ppermute(x, "seq", [(i, i ^ d) for i in range(seq_count)])

    def tie(x, after):
        return lax.optimization_barrier((x, after))[0]

    def tp_xor(x, d):
        return lax.ppermute(x, "tp", [(i, i ^ d) for i in range(tp)])

    def spread(x):
        held = {0: x}
        d = tp // 2
        while d:
            held.update({k ^ d: tp_xor(v, d) for k, v in list(held.items())})
            d //= 2
        return [held[d] for d in range(tp)]

    paired = seq_count == 8 and per_peer == GROUP

    source = (
        window[:, :, None, None] * WIN
        + jnp.arange(tokens)[None, None, None, :] * MERGE
        + jnp.arange(MERGE)[None, None, :, None]
    ).reshape(-1)
    pick = (jnp.arange(patches.shape[0])[:, None] == source[None, :]).astype(BF)
    sent = lax.dot_general(
        patches, pick, (((0,), (0,)), ((), ())), preferred_element_type=F32
    ).astype(BF)
    step = per_peer * WIN
    wq_t = w_qkv.T

    full = lax.all_to_all(
        sent.reshape(feats, seq_count, step).transpose(1, 0, 2),
        "seq",
        split_axis=0,
        concat_axis=0,
        tiled=True,
    )
    full = full.reshape(blocks, GROUP // per_peer, feats, step)
    full = full.transpose(0, 2, 1, 3).reshape(blocks, feats, GROUP * WIN)
    mid = blocks // 2

    if paired:
        share = (wq_t.shape[0] + w_proj.shape[0]) // seq_count
        q_parts = wq_t.shape[0] // share
        mine = jnp.where(
            s < q_parts,
            lax.dynamic_slice_in_dim(wq_t, jnp.minimum(s, q_parts - 1) * share, share),
            lax.dynamic_slice_in_dim(w_proj, jnp.maximum(s - q_parts, 0) * share, share),
        )
        def halves(x):
            mid = x.shape[1] // 2
            return x[:, :mid], x[:, mid:]

        def across(left, right):
            return xor(left, 2), xor(right, 4)

        def joined(left, right, others):
            return jnp.concatenate([left, others[0]]), jnp.concatenate([right, others[1]])

        def along(left, right):
            return xor(left, 4), xor(right, 2)

        def with_cores(pieces):
            return list(pieces) + [xor(v, 1) for v in pieces]

        above = {(0, 0): (0, 2), (1, 0): (0, 4), (0, 1): (4, 6), (1, 1): (2, 6)}
        places = [
            (4 * e + 2 * k + h, h, row, d ^ e)
            for e in range(2)
            for (h, k), peers in above.items()
            for row, d in enumerate(peers)
        ]

        by1, by2 = lax.optimization_barrier((tp_xor(mine, 1), tp_xor(mine, 2)))
        merge_halves = halves(w_merge)
        merge_across = across(*merge_halves)
        vit_halves = halves(jnp.concatenate([by1, by2, tp_xor(by2, 1)]))
        vit_joined = joined(*vit_halves, across(*vit_halves))
        merge_joined = joined(*merge_halves, merge_across)
        vit_joined, merge_joined = lax.optimization_barrier((vit_joined, merge_joined))
        vit_along = along(*vit_joined)
        vit_weights = [wq_t, w_proj] + with_cores(vit_joined + vit_along)
        q_rows, p_rows = wq_t.shape[0], w_proj.shape[0]

        vit_count = 2 + len(places) * (tp - 1)

        def vit_moves(info, refs, w, sem):
            t, s = info[0], info[1]
            copies = [[] for _ in range(tp)]
            copies[0] = [
                pltpu.make_async_copy(
                    refs[0], w.at[pl.ds(pl.multiple_of(t * q_rows, 16), q_rows)], sem.at[0]
                ),
                pltpu.make_async_copy(
                    refs[1], w.at[pl.ds(pl.multiple_of(3 * DV + t * p_rows, 16), p_rows)], sem.at[1]
                ),
            ]
            for at, (n, h, above, d) in enumerate(places):
                for j in range(1, tp):
                    part = s ^ d
                    q = t ^ j
                    row = jnp.where(
                        part < q_parts,
                        q * q_rows + part * share,
                        3 * DV + q * p_rows + (part - q_parts) * share,
                    )
                    first = (above * (tp - 1) + j - 1) * share
                    copies[j].append(
                        pltpu.make_async_copy(
                            refs[2 + n].at[first : first + share],
                            w.at[
                                pl.ds(pl.multiple_of(row, 16), share),
                                h * (DV // 2) : (h + 1) * (DV // 2),
                            ],
                            sem.at[2 + at * (tp - 1) + j - 1],
                        )
                    )
            return copies

        def merge_moves(info, refs, h, i, slot, sem):
            s = info[1]
            rows = slot.shape[0] // 2
            copies = []
            for n, half, above, d in places:
                if half == h and d // 2 == i:
                    spot = pl.ds(pl.multiple_of(((s ^ d) & 1) * rows, 16), rows)
                    part = refs[n].at[above * rows : (above + 1) * rows]
                    copies.append(pltpu.make_async_copy(part, slot.at[spot], sem.at[len(copies)]))
            return copies

        def position(info, i):
            return (info[1] // 2) ^ i

    else:
        vit_weights = [
            lax.all_gather(wq_t, "tp", axis=0, tiled=True),
            lax.all_gather(w_proj, "tp", axis=0, tiled=True),
        ]
        merge_weights = [lax.all_gather(w_merge, "seq", axis=0, tiled=True)]
        vit_count = 2 * tp
        q_rows, p_rows = wq_t.shape[0], w_proj.shape[0]

        def vit_moves(info, refs, w, sem):
            copies = []
            for d in range(tp):
                g = info[0] ^ d
                q_part = pl.ds(pl.multiple_of(g * q_rows, 16), q_rows)
                p_part = pl.ds(pl.multiple_of(g * p_rows, 16), p_rows)
                p_spot = pl.ds(pl.multiple_of(3 * DV + g * p_rows, 16), p_rows)
                copies.append(
                    [
                        pltpu.make_async_copy(refs[0].at[q_part], w.at[q_part], sem.at[2 * d]),
                        pltpu.make_async_copy(refs[1].at[p_part], w.at[p_spot], sem.at[2 * d + 1]),
                    ]
                )
            return copies

        def merge_moves(info, refs, h, i, slot, sem):
            wide = slot.shape[1]
            part = refs[0].at[i * DV : (i + 1) * DV, h * wide : (h + 1) * wide]
            return [pltpu.make_async_copy(part, slot, sem.at[0])]

        def position(info, i):
            return i

    def encode(first, pieces, buf):
        count = pieces[0].shape[0]
        info = jnp.concatenate([jnp.stack([t, s]), first + jnp.arange(count, dtype=jnp.int32)])
        return attend(
            tp, info, pieces, vit_weights, vit_moves, vit_count,
            vit_gain[:, None], merge_gain[None, :], blocks, buf,
        )

    merged = None
    if paired:
        cuts = [0, 5 * blocks // 8, blocks]
        merge_joined = tie(merge_joined, vit_along)
        merge_along = along(*merge_joined)
        far = None
        for n, lo in enumerate(cuts[:-1]):
            own = full[lo : cuts[n + 1]]
            near = own if far is None else tie(own, (far, vit_weights[2:]))
            by1, by2 = lax.optimization_barrier((tp_xor(near, 1), tp_xor(near, 2)))
            if n:
                merged, by2, live_here = lax.optimization_barrier((merged, by2, live_here))
            far = tp_xor(by2, 1)
            merged = encode(lo, [own, by1, by2, far], merged)
        merged, merge_along = lax.optimization_barrier((merged, merge_along))
        merge_weights = with_cores(merge_joined + merge_along)
    else:
        for first in (0, mid):
            merged = encode(first, spread(full[first : first + mid]), merged)
    partial_value = project(
        jnp.stack([t, s]), merged, merge_weights, merge_moves, position, w_cache, llm_gain[None, :]
    )
    summed = lax.psum_scatter(partial_value, "tp", scatter_dimension=0, tiled=True).astype(F32)
    kvw = w_cache.shape[1]
    cache, total_squares = summed[:, :kvw], summed[:, kvw : kvw + 1]
    share = cache.shape[0]
    live_tokens = jnp.repeat(live_here.reshape(-1), tokens)
    mine = lax.dynamic_slice_in_dim(live_tokens, t * share, share).astype(F32)
    return (cache * lax.rsqrt(total_squares / D + 1e-6) * mine[:, None]).astype(BF)


def solution(mesh):
    return jax.shard_map(
        shards,
        mesh=mesh,
        in_specs=(
            P("seq", "tp"),
            P("seq", None),
            P("seq", None),
            P("seq"),
            P(None, "tp"),
            P("tp", None),
            P(),
            P(),
            P("seq", "tp"),
            P("tp"),
            P("tp", None),
        ),
        out_specs=P(("seq", "tp"), None),
        check_vma=False,
    )
```

```python
import functools

import jax
import jax.numpy as jnp
from jax import lax
from jax.experimental import pallas as pl
from jax.experimental.pallas import tpu as pltpu
from jax.sharding import PartitionSpec as P

DV = 1280
HV = 16
HS = DV // HV
D = 8192
WIN = 64
MERGE = 4
TILE_WIN = 4
TILE_SLOTS = 4
GROUP = 4
F32 = jnp.float32
BF = jnp.bfloat16
MIB = 1024 * 1024


def attend_kernel(tp, moves, nw, aliased, info, *refs):
    pieces = refs[:tp]
    at = tp
    w_refs = refs[at : at + nw]
    vit_gain, merge_gain = refs[at + nw : at + nw + 2]
    at += nw + 2 + int(aliased)
    out = refs[at]
    w, xs, nrm, packed, mixed, vit, sem = refs[at + 1 :]
    t = info[0]
    heads = HV // tp
    rows = packed.shape[1]
    feats = pieces[0].shape[1]
    first_proj = 3 * DV
    cols = xs.shape[1]
    step = pl.program_id(0)

    @pl.when(step == 0)
    def _():
        for part in moves(info, w_refs, w, sem):
            for copy in part:
                copy.start()

    for d, piece in enumerate(pieces):
        xs[pl.ds(pl.multiple_of((t ^ d) * feats, feats), feats), :] = piece[0]

    xf = xs[...].astype(F32)
    scale = lax.rsqrt(jnp.mean(xf * xf, axis=0, keepdims=True) + 1e-6)
    nrm[...] = (xf * scale * vit_gain[...]).astype(BF)

    pair = 2 * WIN
    first = lax.broadcasted_iota(jnp.int32, (WIN, pair), 1) < WIN
    fold = (HS**-0.5) * 1.4426950408889634

    none = jnp.zeros((pair, pair), BF)

    def arrived(d):
        @pl.when(step == 0)
        def _():
            for copy in moves(info, w_refs, w, sem)[d]:
                copy.wait()

    def pack(d, slot):
        mine = w[pl.ds(pl.multiple_of((t ^ d) * rows, rows), rows), :]
        packed[slot] = jnp.dot(mine, nrm[...], preferred_element_type=F32).astype(BF)

    def heads_of(d, more):
        slot = lax.rem(d, 2)
        now = packed.at[slot]
        scores = []
        for h in range(heads):
            q, k = (now[(3 * h + n) * HS : (3 * h + n + 1) * HS, :] for n in range(2))
            s = lax.dot_general(k, q, (((0,), (0,)), ((), ())), preferred_element_type=F32)
            for n in range(cols // pair):
                at = n * pair
                s0, s1 = s[at : at + WIN, at : at + pair], s[at + WIN : at + pair, at : at + pair]
                scores.append(jnp.where(first, s0, s1) * fold)
        if more:
            pack(d + 1, 1 - slot)
        probs = []
        for s in scores:
            p = jnp.exp2(s - jnp.max(s, axis=0, keepdims=True))
            p = p * (1.0 / jnp.sum(p, axis=0, keepdims=True))
            probs.append(
                jnp.concatenate([jnp.where(first, p, 0.0), jnp.where(first, 0.0, p)]).astype(BF)
            )
        for h in range(heads):
            v = now[(3 * h + 2) * HS : (3 * h + 3) * HS, :]
            p = jnp.concatenate(
                [
                    jnp.concatenate([probs[2 * h], none], axis=1),
                    jnp.concatenate([none, probs[2 * h + 1]], axis=1),
                ]
            )
            m = jnp.dot(v, p, preferred_element_type=F32)
            at = pl.multiple_of((t ^ d) * heads * HS, heads * HS) + h * HS
            mixed[pl.ds(at, HS), :] = m.astype(BF)

    def one(d, carry):
        for later in range(1, tp):
            pl.when(d + 1 == later)(functools.partial(arrived, later))
        heads_of(d, True)
        return carry

    arrived(0)
    pack(0, 0)
    lax.fori_loop(0, tp - 1, one, 0)
    heads_of(jnp.int32(tp - 1), False)

    width = 256
    sums = jnp.zeros((cols, 1), F32)
    for n in range(DV // width):
        part = slice(n * width, (n + 1) * width)
        proj = lax.dot_general(
            mixed[...],
            w[first_proj : first_proj + DV, part],
            (((0,), (0,)), ((), ())),
            preferred_element_type=F32,
        )
        y = (xs[part, :].T.astype(F32) + proj).astype(BF)
        vit[:, part] = y
        yf = y.astype(F32)
        sums = sums + jnp.sum(yf * yf, axis=1, keepdims=True)
    scale = lax.rsqrt(sums * (1.0 / DV) + 1e-6)
    merged = (vit[...].astype(F32) * scale * merge_gain[...]).astype(BF)
    per = WIN // MERGE
    for w_at in range(cols // WIN):
        for c in range(MERGE):
            at = w_at * WIN + c * per
            out[c, 0, w_at * per : (w_at + 1) * per] = merged[at : at + per, :]


def attend(tp, info, pieces, weights, moves, count, vit_gain, merge_gain, blocks, buf):
    nb, feats, cols = pieces[0].shape
    per = cols // MERGE
    x_spec = pl.BlockSpec((1, feats, cols), lambda i, s: (i, 0, 0))
    anywhere = pl.BlockSpec(memory_space=pl.ANY)
    ins = [*pieces, *weights, vit_gain, merge_gain]
    specs = [x_spec] * tp + [anywhere] * len(weights)
    specs += [pl.BlockSpec((DV, 1), lambda i, s: (0, 0)), pl.BlockSpec((1, DV), lambda i, s: (0, 0))]
    alias = {}
    if buf is not None:
        ins.append(buf)
        specs.append(anywhere)
        alias = {len(ins): 0}
    return pl.pallas_call(
        functools.partial(attend_kernel, tp, moves, len(weights), buf is not None),
        out_shape=jax.ShapeDtypeStruct((MERGE, blocks, per, DV), BF),
        grid_spec=pltpu.PrefetchScalarGridSpec(
            num_scalar_prefetch=1,
            grid=(nb,),
            in_specs=specs,
            out_specs=pl.BlockSpec((MERGE, 1, per, DV), lambda i, s: (0, s[2 + i], 0, 0)),
            scratch_shapes=[
                pltpu.VMEM((4 * DV, DV), BF),
                pltpu.VMEM((DV, cols), BF),
                pltpu.VMEM((DV, cols), BF),
                pltpu.VMEM((2, 3 * DV // tp, cols), BF),
                pltpu.VMEM((DV, cols), BF),
                pltpu.VMEM((cols, DV), BF),
                pltpu.SemaphoreType.DMA((count,)),
            ],
        ),
        input_output_aliases=alias,
        compiler_params=pltpu.CompilerParams(
            vmem_limit_bytes=48 * MIB, dimension_semantics=("arbitrary",)
        ),
        cost_estimate=pl.CostEstimate(
            flops=nb * cols * DV * DV * 10,
            bytes_accessed=14 * MIB,
            transcendentals=nb * cols * cols * HV,
        ),
        name="attend",
    )(info, *ins)


def project_kernel(moves, position, nw, info, *refs):
    merged = refs[0]
    w_refs = refs[1 : 1 + nw]
    w_cache, llm_gain, out = refs[1 + nw : 4 + nw]
    held, slots, cache, acc, scaled, held_sem, slot_sem, cache_sem = refs[4 + nw :]
    units = scaled.shape[1]
    half = units // 2
    rows = held.shape[1]
    depth = slots.shape[0]
    width = min(256, half)
    chunks = [(h, i) for h in range(2) for i in range(MERGE)]

    def bring(n):
        return moves(info, w_refs, *chunks[n], slots.at[n % depth], slot_sem.at[n % depth])

    def bring_merged(i):
        c = position(info, i)
        return pltpu.make_async_copy(merged.at[c], held.at[c], held_sem.at[i])

    load_cache = pltpu.make_async_copy(w_cache, cache, cache_sem)
    for n in range(depth):
        bring_merged(n).start()
        for copy in bring(n):
            copy.start()
    for n in range(depth, MERGE):
        bring_merged(n).start()
    load_cache.start()
    total = jnp.zeros((rows, 1), F32)
    for n, (h, i) in enumerate(chunks):
        c = position(info, i)
        if h == 0:
            bring_merged(i).wait()
        for copy in bring(n):
            copy.wait()
        slot = n % depth

        def tile(j, carry):
            spot = pl.ds(pl.multiple_of(j * width, width), width)
            d = jnp.dot(held[c], slots[slot, :, spot], preferred_element_type=F32)
            if i == 0:
                acc[:, spot] = d
            else:
                acc[:, spot] += d
            return carry

        lax.fori_loop(0, half // width, tile, 0)
        if n + depth < len(chunks):
            for copy in bring(n + depth):
                copy.start()
        if i == MERGE - 1:
            hidden = acc[...].astype(BF).astype(F32)
            total = total + jnp.sum(hidden * hidden, axis=1, keepdims=True)
            part = slice(h * half, (h + 1) * half)
            scaled[:, part] = (hidden * llm_gain[:, part]).astype(BF)
    load_cache.wait()
    kvw = cache.shape[1]

    def kv_tile(j, carry):
        spot = pl.ds(pl.multiple_of(j * 256, 256), 256)
        out[:, spot] = jnp.dot(scaled[...], cache[:, spot], preferred_element_type=F32).astype(BF)
        return carry

    lax.fori_loop(0, kvw // 256, kv_tile, 0)
    out[:, kvw:] = jnp.broadcast_to(total, (rows, 128)).astype(BF)


def project(info, merged, weights, moves, position, w_cache, llm_gain):
    units, kvw = w_cache.shape
    rows = merged.shape[1] * merged.shape[2]
    anywhere = pl.BlockSpec(memory_space=pl.ANY)
    return pl.pallas_call(
        functools.partial(project_kernel, moves, position, len(weights)),
        out_shape=jax.ShapeDtypeStruct((rows, kvw + 128), BF),
        grid_spec=pltpu.PrefetchScalarGridSpec(
            num_scalar_prefetch=1,
            grid=(1,),
            in_specs=[anywhere] * (len(weights) + 2)
            + [pl.BlockSpec((1, units), lambda i, s: (0, 0))],
            out_specs=pl.BlockSpec((rows, kvw + 128), lambda i, s: (0, 0)),
            scratch_shapes=[
                pltpu.VMEM((MERGE, rows, DV), BF),
                pltpu.VMEM((3, DV, units // 2), BF),
                pltpu.VMEM((units, kvw), BF),
                pltpu.VMEM((rows, units // 2), F32),
                pltpu.VMEM((rows, units), BF),
                pltpu.SemaphoreType.DMA((MERGE,)),
                pltpu.SemaphoreType.DMA((3, 4)),
                pltpu.SemaphoreType.DMA,
            ],
        ),
        compiler_params=pltpu.CompilerParams(
            vmem_limit_bytes=48 * MIB, dimension_semantics=("arbitrary",)
        ),
        cost_estimate=pl.CostEstimate(
            flops=2 * rows * units * (MERGE * DV + kvw),
            bytes_accessed=36 * MIB,
            transcendentals=0,
        ),
        name="project",
    )(info, merged.reshape(MERGE, rows, DV), *weights, w_cache, llm_gain)


def shards(
    patches, route, order, tiles, w_qkv, w_proj, vit_gain, merge_gain, w_merge, llm_gain, w_cache
):
    seq_count = lax.axis_size("seq")
    tp = lax.axis_size("tp")
    s = lax.axis_index("seq").astype(jnp.int32)
    t = lax.axis_index("tp").astype(jnp.int32)
    win_dev = order.shape[1]
    feats = patches.shape[1]
    per_peer = win_dev // seq_count
    tokens = WIN // MERGE
    blocks = win_dev // GROUP
    picks = order[0]
    tile_index = picks // TILE_WIN
    counts = jnp.take(tiles, tile_index // TILE_SLOTS)
    live = (tile_index % TILE_SLOTS < counts).astype(jnp.int32)
    arrange = jnp.argsort(route[:, 0], stable=True)
    live_send = jnp.take(live, arrange).reshape(seq_count, per_peer)
    live_here = lax.all_to_all(live_send, "seq", split_axis=0, concat_axis=0, tiled=True)
    window = jnp.take(picks, arrange).reshape(seq_count, per_peer)

    def xor(x, d):
        return lax.ppermute(x, "seq", [(i, i ^ d) for i in range(seq_count)])

    def tie(x, after):
        return lax.optimization_barrier((x, after))[0]

    def tp_xor(x, d):
        return lax.ppermute(x, "tp", [(i, i ^ d) for i in range(tp)])

    def spread(x):
        held = {0: x}
        d = tp // 2
        while d:
            held.update({k ^ d: tp_xor(v, d) for k, v in list(held.items())})
            d //= 2
        return [held[d] for d in range(tp)]

    paired = seq_count == 8 and per_peer == GROUP

    source = (
        window[:, :, None, None] * WIN
        + jnp.arange(tokens)[None, None, None, :] * MERGE
        + jnp.arange(MERGE)[None, None, :, None]
    ).reshape(-1)
    pick = (jnp.arange(patches.shape[0])[:, None] == source[None, :]).astype(BF)
    sent = lax.dot_general(
        patches, pick, (((0,), (0,)), ((), ())), preferred_element_type=F32
    ).astype(BF)
    step = per_peer * WIN
    wq_t = w_qkv.T

    full = lax.all_to_all(
        sent.reshape(feats, seq_count, step).transpose(1, 0, 2),
        "seq",
        split_axis=0,
        concat_axis=0,
        tiled=True,
    )
    full = full.reshape(blocks, GROUP // per_peer, feats, step)
    full = full.transpose(0, 2, 1, 3).reshape(blocks, feats, GROUP * WIN)
    mid = blocks // 2

    if paired:
        share = (wq_t.shape[0] + w_proj.shape[0]) // seq_count
        q_parts = wq_t.shape[0] // share
        mine = jnp.where(
            s < q_parts,
            lax.dynamic_slice_in_dim(wq_t, jnp.minimum(s, q_parts - 1) * share, share),
            lax.dynamic_slice_in_dim(w_proj, jnp.maximum(s - q_parts, 0) * share, share),
        )
        def sides(x):
            return lax.optimization_barrier((xor(x, 2), xor(x, 4)))

        def corners(by_x, by_y):
            half = by_x.shape[0] // 2
            return xor(by_x[:half], 4), xor(by_y[half:], 2)

        def with_cores(pieces):
            return list(pieces) + [xor(v, 1) for v in pieces]

        def parts(rows):
            half = rows // 2
            own = [(0, 0, rows), (2, 0, rows), (4, 0, rows), (6, 0, half), (6, half, rows)]
            return own + [(d ^ 1, lo, hi) for d, lo, hi in own]

        by1, by2 = lax.optimization_barrier((tp_xor(mine, 1), tp_xor(mine, 2)))
        others = jnp.concatenate([by1, by2, tp_xor(by2, 1)])
        vit_sides = sides(others)
        vit_corners = lax.optimization_barrier(corners(*vit_sides))
        vit_weights = [wq_t, w_proj] + with_cores([others, *vit_sides, *vit_corners])
        merge_sides = sides(tie(w_merge, vit_corners))
        q_rows, p_rows = wq_t.shape[0], w_proj.shape[0]
        vit_parts = []
        for n, (d, lo, hi) in enumerate(parts(others.shape[0])):
            for j in range(1, tp):
                top, end = max(lo, (j - 1) * share), min(hi, j * share)
                if top < end:
                    vit_parts.append((2 + n, d, j, top - lo, top - (j - 1) * share, end - top))
        vit_count = 2 + len(vit_parts)

        def vit_moves(info, refs, w, sem):
            t, s = info[0], info[1]
            copies = [[] for _ in range(tp)]
            copies[0] = [
                pltpu.make_async_copy(
                    refs[0], w.at[pl.ds(pl.multiple_of(t * q_rows, 16), q_rows)], sem.at[0]
                ),
                pltpu.make_async_copy(
                    refs[1], w.at[pl.ds(pl.multiple_of(3 * DV + t * p_rows, 16), p_rows)], sem.at[1]
                ),
            ]
            for at, (n, d, j, source, offset, count) in enumerate(vit_parts):
                part = s ^ d
                q = t ^ j
                row = offset + jnp.where(
                    part < q_parts,
                    q * q_rows + part * share,
                    3 * DV + q * p_rows + (part - q_parts) * share,
                )
                copies[j].append(
                    pltpu.make_async_copy(
                        refs[n].at[source : source + count],
                        w.at[pl.ds(pl.multiple_of(row, 16), count)],
                        sem.at[2 + at],
                    )
                )
            return copies

        def merge_moves(info, refs, h, i, slot, sem):
            s = info[1]
            wide = slot.shape[1]
            rows = slot.shape[0] // 2
            copies = []
            for n, (d, lo, hi) in enumerate(parts(rows)):
                if d // 2 == i:
                    spot = pl.ds(pl.multiple_of(((s ^ d) & 1) * rows + lo, 16), hi - lo)
                    part = refs[n].at[:, h * wide : (h + 1) * wide]
                    copies.append(pltpu.make_async_copy(part, slot.at[spot], sem.at[len(copies)]))
            return copies

        def position(info, i):
            return (info[1] // 2) ^ i

    else:
        vit_weights = [
            lax.all_gather(wq_t, "tp", axis=0, tiled=True),
            lax.all_gather(w_proj, "tp", axis=0, tiled=True),
        ]
        merge_weights = [lax.all_gather(w_merge, "seq", axis=0, tiled=True)]
        vit_count = 2 * tp
        q_rows, p_rows = wq_t.shape[0], w_proj.shape[0]

        def vit_moves(info, refs, w, sem):
            copies = []
            for d in range(tp):
                g = info[0] ^ d
                q_part = pl.ds(pl.multiple_of(g * q_rows, 16), q_rows)
                p_part = pl.ds(pl.multiple_of(g * p_rows, 16), p_rows)
                p_spot = pl.ds(pl.multiple_of(3 * DV + g * p_rows, 16), p_rows)
                copies.append(
                    [
                        pltpu.make_async_copy(refs[0].at[q_part], w.at[q_part], sem.at[2 * d]),
                        pltpu.make_async_copy(refs[1].at[p_part], w.at[p_spot], sem.at[2 * d + 1]),
                    ]
                )
            return copies

        def merge_moves(info, refs, h, i, slot, sem):
            wide = slot.shape[1]
            part = refs[0].at[i * DV : (i + 1) * DV, h * wide : (h + 1) * wide]
            return [pltpu.make_async_copy(part, slot, sem.at[0])]

        def position(info, i):
            return i

    def encode(first, pieces, buf):
        count = pieces[0].shape[0]
        info = jnp.concatenate([jnp.stack([t, s]), first + jnp.arange(count, dtype=jnp.int32)])
        return attend(
            tp, info, pieces, vit_weights, vit_moves, vit_count,
            vit_gain[:, None], merge_gain[None, :], blocks, buf,
        )

    merged = None
    if paired:
        cuts = [0, mid, blocks]
        far = None
        for n, lo in enumerate(cuts[:-1]):
            own = full[lo : cuts[n + 1]]
            near = own if far is None else tie(own, (far, vit_weights[2:]))
            by1, by2 = lax.optimization_barrier((tp_xor(near, 1), tp_xor(near, 2)))
            if n:
                merged, by2, live_here = lax.optimization_barrier((merged, by2, live_here))
            far = tp_xor(by2, 1)
            if n:
                far, merge_sides = lax.optimization_barrier((far, merge_sides))
            merged = encode(lo, [own, by1, by2, far], merged)
        merge_corners = corners(*merge_sides)
        merged, merge_corners = lax.optimization_barrier((merged, merge_corners))
        merge_weights = with_cores([w_merge, *merge_sides, *merge_corners])
    else:
        for first in (0, mid):
            merged = encode(first, spread(full[first : first + mid]), merged)
    partial_value = project(
        jnp.stack([t, s]), merged, merge_weights, merge_moves, position, w_cache, llm_gain[None, :]
    )
    summed = lax.psum_scatter(partial_value, "tp", scatter_dimension=0, tiled=True).astype(F32)
    kvw = w_cache.shape[1]
    cache, total_squares = summed[:, :kvw], summed[:, kvw : kvw + 1]
    share = cache.shape[0]
    live_tokens = jnp.repeat(live_here.reshape(-1), tokens)
    mine = lax.dynamic_slice_in_dim(live_tokens, t * share, share).astype(F32)
    return (cache * lax.rsqrt(total_squares / D + 1e-6) * mine[:, None]).astype(BF)


def solution(mesh):
    return jax.shard_map(
        shards,
        mesh=mesh,
        in_specs=(
            P("seq", "tp"),
            P("seq", None),
            P("seq", None),
            P("seq"),
            P(None, "tp"),
            P("tp", None),
            P(),
            P(),
            P("seq", "tp"),
            P("tp"),
            P("tp", None),
        ),
        out_specs=P(("seq", "tp"), None),
        check_vma=False,
    )
```

```python
import functools

import jax
import jax.numpy as jnp
from jax import lax
from jax.experimental import pallas as pl
from jax.experimental.pallas import tpu as pltpu
from jax.sharding import PartitionSpec as P

DV = 1280
HV = 16
HS = DV // HV
D = 8192
WIN = 64
MERGE = 4
TILE_WIN = 4
TILE_SLOTS = 4
GROUP = 4
F32 = jnp.float32
BF = jnp.bfloat16
MIB = 1024 * 1024


def attend_kernel(tp, moves, nw, aliased, info, *refs):
    pieces = refs[:tp]
    at = tp
    w_refs = refs[at : at + nw]
    vit_gain, merge_gain = refs[at + nw : at + nw + 2]
    at += nw + 2 + int(aliased)
    out = refs[at]
    w, xs, nrm, packed, mixed, vit, sem = refs[at + 1 :]
    t = info[0]
    heads = HV // tp
    rows = packed.shape[1]
    feats = pieces[0].shape[1]
    first_proj = 3 * DV
    cols = xs.shape[1]
    step = pl.program_id(0)

    @pl.when(step == 0)
    def _():
        for part in moves(info, w_refs, w, sem):
            for copy in part:
                copy.start()

    for d, piece in enumerate(pieces):
        xs[pl.ds(pl.multiple_of((t ^ d) * feats, feats), feats), :] = piece[0]

    xf = xs[...].astype(F32)
    scale = lax.rsqrt(jnp.mean(xf * xf, axis=0, keepdims=True) + 1e-6)
    nrm[...] = (xf * scale * vit_gain[...]).astype(BF)

    pair = 2 * WIN
    first = lax.broadcasted_iota(jnp.int32, (WIN, pair), 1) < WIN
    fold = (HS**-0.5) * 1.4426950408889634

    none = jnp.zeros((pair, pair), BF)

    def arrived(d):
        @pl.when(step == 0)
        def _():
            for copy in moves(info, w_refs, w, sem)[d]:
                copy.wait()

    def pack(d, slot):
        mine = w[pl.ds(pl.multiple_of((t ^ d) * rows, rows), rows), :]
        packed[slot] = jnp.dot(mine, nrm[...], preferred_element_type=F32).astype(BF)

    def heads_of(d, more):
        slot = lax.rem(d, 2)
        now = packed.at[slot]
        scores = []
        for h in range(heads):
            q, k = (now[(3 * h + n) * HS : (3 * h + n + 1) * HS, :] for n in range(2))
            s = lax.dot_general(k, q, (((0,), (0,)), ((), ())), preferred_element_type=F32)
            for n in range(cols // pair):
                at = n * pair
                s0, s1 = s[at : at + WIN, at : at + pair], s[at + WIN : at + pair, at : at + pair]
                scores.append(jnp.where(first, s0, s1) * fold)
        if more:
            pack(d + 1, 1 - slot)
        probs = []
        for s in scores:
            p = jnp.exp2(s - jnp.max(s, axis=0, keepdims=True))
            p = p * (1.0 / jnp.sum(p, axis=0, keepdims=True))
            probs.append(
                jnp.concatenate([jnp.where(first, p, 0.0), jnp.where(first, 0.0, p)]).astype(BF)
            )
        for h in range(heads):
            v = now[(3 * h + 2) * HS : (3 * h + 3) * HS, :]
            p = jnp.concatenate(
                [
                    jnp.concatenate([probs[2 * h], none], axis=1),
                    jnp.concatenate([none, probs[2 * h + 1]], axis=1),
                ]
            )
            m = jnp.dot(v, p, preferred_element_type=F32)
            at = pl.multiple_of((t ^ d) * heads * HS, heads * HS) + h * HS
            mixed[pl.ds(at, HS), :] = m.astype(BF)

    def one(d, carry):
        for later in range(1, tp):
            pl.when(d + 1 == later)(functools.partial(arrived, later))
        heads_of(d, True)
        return carry

    arrived(0)
    pack(0, 0)
    lax.fori_loop(0, tp - 1, one, 0)
    heads_of(jnp.int32(tp - 1), False)

    width = 256
    sums = jnp.zeros((cols, 1), F32)
    for n in range(DV // width):
        part = slice(n * width, (n + 1) * width)
        proj = lax.dot_general(
            mixed[...],
            w[first_proj : first_proj + DV, part],
            (((0,), (0,)), ((), ())),
            preferred_element_type=F32,
        )
        y = (xs[part, :].T.astype(F32) + proj).astype(BF)
        vit[:, part] = y
        yf = y.astype(F32)
        sums = sums + jnp.sum(yf * yf, axis=1, keepdims=True)
    scale = lax.rsqrt(sums * (1.0 / DV) + 1e-6)
    merged = (vit[...].astype(F32) * scale * merge_gain[...]).astype(BF)
    per = WIN // MERGE
    for w_at in range(cols // WIN):
        for c in range(MERGE):
            at = w_at * WIN + c * per
            out[c, 0, w_at * per : (w_at + 1) * per] = merged[at : at + per, :]


def attend(tp, info, pieces, weights, moves, count, vit_gain, merge_gain, blocks, buf):
    nb, feats, cols = pieces[0].shape
    per = cols // MERGE
    x_spec = pl.BlockSpec((1, feats, cols), lambda i, s: (i, 0, 0))
    anywhere = pl.BlockSpec(memory_space=pl.ANY)
    ins = [*pieces, *weights, vit_gain, merge_gain]
    specs = [x_spec] * tp + [anywhere] * len(weights)
    specs += [pl.BlockSpec((DV, 1), lambda i, s: (0, 0)), pl.BlockSpec((1, DV), lambda i, s: (0, 0))]
    alias = {}
    if buf is not None:
        ins.append(buf)
        specs.append(anywhere)
        alias = {len(ins): 0}
    return pl.pallas_call(
        functools.partial(attend_kernel, tp, moves, len(weights), buf is not None),
        out_shape=jax.ShapeDtypeStruct((MERGE, blocks, per, DV), BF),
        grid_spec=pltpu.PrefetchScalarGridSpec(
            num_scalar_prefetch=1,
            grid=(nb,),
            in_specs=specs,
            out_specs=pl.BlockSpec((MERGE, 1, per, DV), lambda i, s: (0, s[2 + i], 0, 0)),
            scratch_shapes=[
                pltpu.VMEM((4 * DV, DV), BF),
                pltpu.VMEM((DV, cols), BF),
                pltpu.VMEM((DV, cols), BF),
                pltpu.VMEM((2, 3 * DV // tp, cols), BF),
                pltpu.VMEM((DV, cols), BF),
                pltpu.VMEM((cols, DV), BF),
                pltpu.SemaphoreType.DMA((count,)),
            ],
        ),
        input_output_aliases=alias,
        compiler_params=pltpu.CompilerParams(
            vmem_limit_bytes=48 * MIB, dimension_semantics=("arbitrary",)
        ),
        cost_estimate=pl.CostEstimate(
            flops=nb * cols * DV * DV * 10,
            bytes_accessed=14 * MIB,
            transcendentals=nb * cols * cols * HV,
        ),
        name="attend",
    )(info, *ins)


def project_kernel(moves, position, nw, info, *refs):
    merged = refs[0]
    w_refs = refs[1 : 1 + nw]
    w_cache, llm_gain, out = refs[1 + nw : 4 + nw]
    held, slots, cache, acc, scaled, held_sem, slot_sem, cache_sem = refs[4 + nw :]
    units = scaled.shape[1]
    half = units // 2
    rows = held.shape[1]
    depth = slots.shape[0]
    width = min(1024, half)
    chunks = [(h, i) for h in range(2) for i in range(MERGE)]

    def bring(n):
        return moves(info, w_refs, *chunks[n], slots.at[n % depth], slot_sem.at[n % depth])

    def bring_merged(i):
        c = position(info, i)
        return pltpu.make_async_copy(merged.at[c], held.at[c], held_sem.at[i])

    load_cache = pltpu.make_async_copy(w_cache, cache, cache_sem)
    for n in range(depth):
        bring_merged(n).start()
        for copy in bring(n):
            copy.start()
    for n in range(depth, MERGE):
        bring_merged(n).start()
    load_cache.start()
    total = jnp.zeros((rows, 1), F32)
    for n, (h, i) in enumerate(chunks):
        c = position(info, i)
        if h == 0:
            bring_merged(i).wait()
        for copy in bring(n):
            copy.wait()
        slot = n % depth

        def tile(j, carry):
            spot = pl.ds(pl.multiple_of(j * width, width), width)
            d = jnp.dot(held[c], slots[slot, :, spot], preferred_element_type=F32)
            if i == 0:
                acc[:, spot] = d
            else:
                acc[:, spot] += d
            return carry

        lax.fori_loop(0, half // width, tile, 0)
        if n + depth < len(chunks):
            for copy in bring(n + depth):
                copy.start()
        if i == MERGE - 1:
            hidden = acc[...].astype(BF).astype(F32)
            total = total + jnp.sum(hidden * hidden, axis=1, keepdims=True)
            part = slice(h * half, (h + 1) * half)
            scaled[:, part] = (hidden * llm_gain[:, part]).astype(BF)
    load_cache.wait()
    kvw = cache.shape[1]

    def kv_tile(j, carry):
        spot = pl.ds(pl.multiple_of(j * 256, 256), 256)
        out[:, spot] = jnp.dot(scaled[...], cache[:, spot], preferred_element_type=F32).astype(BF)
        return carry

    lax.fori_loop(0, kvw // 256, kv_tile, 0)
    out[:, kvw:] = jnp.broadcast_to(total, (rows, 128)).astype(BF)


def project(info, merged, weights, moves, position, w_cache, llm_gain):
    units, kvw = w_cache.shape
    rows = merged.shape[1] * merged.shape[2]
    anywhere = pl.BlockSpec(memory_space=pl.ANY)
    return pl.pallas_call(
        functools.partial(project_kernel, moves, position, len(weights)),
        out_shape=jax.ShapeDtypeStruct((rows, kvw + 128), BF),
        grid_spec=pltpu.PrefetchScalarGridSpec(
            num_scalar_prefetch=1,
            grid=(1,),
            in_specs=[anywhere] * (len(weights) + 2)
            + [pl.BlockSpec((1, units), lambda i, s: (0, 0))],
            out_specs=pl.BlockSpec((rows, kvw + 128), lambda i, s: (0, 0)),
            scratch_shapes=[
                pltpu.VMEM((MERGE, rows, DV), BF),
                pltpu.VMEM((3, DV, units // 2), BF),
                pltpu.VMEM((units, kvw), BF),
                pltpu.VMEM((rows, units // 2), F32),
                pltpu.VMEM((rows, units), BF),
                pltpu.SemaphoreType.DMA((MERGE,)),
                pltpu.SemaphoreType.DMA((3, 4)),
                pltpu.SemaphoreType.DMA,
            ],
        ),
        compiler_params=pltpu.CompilerParams(
            vmem_limit_bytes=48 * MIB, dimension_semantics=("arbitrary",)
        ),
        cost_estimate=pl.CostEstimate(
            flops=2 * rows * units * (MERGE * DV + kvw),
            bytes_accessed=36 * MIB,
            transcendentals=0,
        ),
        name="project",
    )(info, merged.reshape(MERGE, rows, DV), *weights, w_cache, llm_gain)


def shards(
    patches, route, order, tiles, w_qkv, w_proj, vit_gain, merge_gain, w_merge, llm_gain, w_cache
):
    seq_count = lax.axis_size("seq")
    tp = lax.axis_size("tp")
    s = lax.axis_index("seq").astype(jnp.int32)
    t = lax.axis_index("tp").astype(jnp.int32)
    win_dev = order.shape[1]
    feats = patches.shape[1]
    per_peer = win_dev // seq_count
    tokens = WIN // MERGE
    blocks = win_dev // GROUP
    picks = order[0]
    tile_index = picks // TILE_WIN
    counts = jnp.take(tiles, tile_index // TILE_SLOTS)
    live = (tile_index % TILE_SLOTS < counts).astype(jnp.int32)
    arrange = jnp.argsort(route[:, 0], stable=True)
    live_send = jnp.take(live, arrange).reshape(seq_count, per_peer)
    window = jnp.take(picks, arrange).reshape(seq_count, per_peer)

    def xor(x, d):
        return lax.ppermute(x, "seq", [(i, i ^ d) for i in range(seq_count)])

    def tie(x, after):
        return lax.optimization_barrier((x, after))[0]

    def tp_xor(x, d):
        return lax.ppermute(x, "tp", [(i, i ^ d) for i in range(tp)])

    def spread(x):
        held = {0: x}
        d = tp // 2
        while d:
            held.update({k ^ d: tp_xor(v, d) for k, v in list(held.items())})
            d //= 2
        return [held[d] for d in range(tp)]

    paired = seq_count == 8 and per_peer == GROUP

    source = (
        window[:, :, None, None] * WIN
        + jnp.arange(tokens)[None, None, None, :] * MERGE
        + jnp.arange(MERGE)[None, None, :, None]
    ).reshape(-1)
    pick = (jnp.arange(patches.shape[0])[:, None] == source[None, :]).astype(BF)
    sent = lax.dot_general(
        patches, pick, (((0,), (0,)), ((), ())), preferred_element_type=F32
    ).astype(BF)
    alive = jnp.repeat(live_send.reshape(-1), WIN).astype(BF)
    sent = jnp.concatenate([sent, jnp.broadcast_to(alive, (16, alive.shape[0]))])
    step = per_peer * WIN
    wq_t = w_qkv.T

    full = lax.all_to_all(
        sent.reshape(feats + 16, seq_count, step).transpose(1, 0, 2),
        "seq",
        split_axis=0,
        concat_axis=0,
        tiled=True,
    )
    live_here = full[:, feats, ::WIN]
    full = full[:, :feats].reshape(blocks, GROUP // per_peer, feats, step)
    full = full.transpose(0, 2, 1, 3).reshape(blocks, feats, GROUP * WIN)
    mid = blocks // 2

    if paired:
        share = (wq_t.shape[0] + w_proj.shape[0]) // seq_count
        q_parts = wq_t.shape[0] // share
        mine = jnp.where(
            s < q_parts,
            lax.dynamic_slice_in_dim(wq_t, jnp.minimum(s, q_parts - 1) * share, share),
            lax.dynamic_slice_in_dim(w_proj, jnp.maximum(s - q_parts, 0) * share, share),
        )
        def sides(x):
            return lax.optimization_barrier((xor(x, 2), xor(x, 4)))

        def corners(by_x, by_y):
            half = by_x.shape[0] // 2
            return xor(by_x[:half], 4), xor(by_y[half:], 2)

        def with_cores(pieces):
            return list(pieces) + [xor(v, 1) for v in pieces]

        def parts(rows):
            half = rows // 2
            own = [(0, 0, rows), (2, 0, rows), (4, 0, rows), (6, 0, half), (6, half, rows)]
            return own + [(d ^ 1, lo, hi) for d, lo, hi in own]

        def sides_of_tp(x):
            return lax.optimization_barrier((tp_xor(x, 1), tp_xor(x, 2)))

        by1, by2 = sides_of_tp(mine)
        others = jnp.concatenate([by1, by2, tp_xor(by2, 1)])
        vit_sides = sides(tie(others, full))
        near = sides_of_tp(full[:mid])
        vit_sides, near = lax.optimization_barrier((vit_sides, near))
        far = tp_xor(near[1], 1)
        far, vit_corners = lax.optimization_barrier((far, corners(*vit_sides)))
        vit_weights = [wq_t, w_proj] + with_cores([jnp.concatenate([others, *vit_sides, *vit_corners])])
        merge_sides = sides(tie(w_merge, vit_sides))
        q_rows, p_rows = wq_t.shape[0], w_proj.shape[0]
        vit_parts = []
        for n, (d, lo, hi) in enumerate(parts(others.shape[0])):
            base = sum(last - first for _, first, last in parts(others.shape[0])[n // 5 * 5 : n])
            for j in range(1, tp):
                top, end = max(lo, (j - 1) * share), min(hi, j * share)
                if top < end:
                    vit_parts.append(
                        (2 + n // 5, d, j, base + top - lo, top - (j - 1) * share, end - top)
                    )
        vit_count = 2 + len(vit_parts)

        def vit_moves(info, refs, w, sem):
            t, s = info[0], info[1]
            copies = [[] for _ in range(tp)]
            copies[0] = [
                pltpu.make_async_copy(
                    refs[0], w.at[pl.ds(pl.multiple_of(t * q_rows, 16), q_rows)], sem.at[0]
                ),
                pltpu.make_async_copy(
                    refs[1], w.at[pl.ds(pl.multiple_of(3 * DV + t * p_rows, 16), p_rows)], sem.at[1]
                ),
            ]
            for at, (n, d, j, source, offset, count) in enumerate(vit_parts):
                part = s ^ d
                q = t ^ j
                row = offset + jnp.where(
                    part < q_parts,
                    q * q_rows + part * share,
                    3 * DV + q * p_rows + (part - q_parts) * share,
                )
                copies[j].append(
                    pltpu.make_async_copy(
                        refs[n].at[source : source + count],
                        w.at[pl.ds(pl.multiple_of(row, 16), count)],
                        sem.at[2 + at],
                    )
                )
            return copies

        def merge_moves(info, refs, h, i, slot, sem):
            s = info[1]
            wide = slot.shape[1]
            rows = slot.shape[0] // 2
            copies = []
            for n, (d, lo, hi) in enumerate(parts(rows)):
                if d // 2 == i:
                    spot = pl.ds(pl.multiple_of(((s ^ d) & 1) * rows + lo, 16), hi - lo)
                    part = refs[n].at[:, h * wide : (h + 1) * wide]
                    copies.append(pltpu.make_async_copy(part, slot.at[spot], sem.at[len(copies)]))
            return copies

        def position(info, i):
            return (info[1] // 2) ^ i

    else:
        vit_weights = [
            lax.all_gather(wq_t, "tp", axis=0, tiled=True),
            lax.all_gather(w_proj, "tp", axis=0, tiled=True),
        ]
        merge_weights = [lax.all_gather(w_merge, "seq", axis=0, tiled=True)]
        vit_count = 2 * tp
        q_rows, p_rows = wq_t.shape[0], w_proj.shape[0]

        def vit_moves(info, refs, w, sem):
            copies = []
            for d in range(tp):
                g = info[0] ^ d
                q_part = pl.ds(pl.multiple_of(g * q_rows, 16), q_rows)
                p_part = pl.ds(pl.multiple_of(g * p_rows, 16), p_rows)
                p_spot = pl.ds(pl.multiple_of(3 * DV + g * p_rows, 16), p_rows)
                copies.append(
                    [
                        pltpu.make_async_copy(refs[0].at[q_part], w.at[q_part], sem.at[2 * d]),
                        pltpu.make_async_copy(refs[1].at[p_part], w.at[p_spot], sem.at[2 * d + 1]),
                    ]
                )
            return copies

        def merge_moves(info, refs, h, i, slot, sem):
            wide = slot.shape[1]
            part = refs[0].at[i * DV : (i + 1) * DV, h * wide : (h + 1) * wide]
            return [pltpu.make_async_copy(part, slot, sem.at[0])]

        def position(info, i):
            return i

    def encode(first, pieces, buf):
        count = pieces[0].shape[0]
        info = jnp.concatenate([jnp.stack([t, s]), first + jnp.arange(count, dtype=jnp.int32)])
        return attend(
            tp, info, pieces, vit_weights, vit_moves, vit_count,
            vit_gain[:, None], merge_gain[None, :], blocks, buf,
        )

    merged = None
    if paired:
        by1, by2 = near
        own = tie(full[mid:], (far, vit_weights[2:]))
        merged = encode(0, [full[:mid], by1, by2, far], None)
        by1, by2 = sides_of_tp(own)
        merged, by2 = lax.optimization_barrier((merged, by2))
        far, merge_sides = lax.optimization_barrier((tp_xor(by2, 1), merge_sides))
        merged = encode(mid, [full[mid:], by1, by2, far], merged)
        merge_corners = corners(*merge_sides)
        merged, merge_corners = lax.optimization_barrier((merged, merge_corners))
        merge_weights = with_cores([w_merge, *merge_sides, *merge_corners])
    else:
        for first in (0, mid):
            merged = encode(first, spread(full[first : first + mid]), merged)
    partial_value = project(
        jnp.stack([t, s]), merged, merge_weights, merge_moves, position, w_cache, llm_gain[None, :]
    )
    summed = lax.psum_scatter(partial_value, "tp", scatter_dimension=0, tiled=True).astype(F32)
    kvw = w_cache.shape[1]
    cache, total_squares = summed[:, :kvw], summed[:, kvw : kvw + 1]
    share = cache.shape[0]
    live_tokens = jnp.repeat(live_here.reshape(-1), tokens)
    mine = lax.dynamic_slice_in_dim(live_tokens, t * share, share).astype(F32)
    return (cache * lax.rsqrt(total_squares / D + 1e-6) * mine[:, None]).astype(BF)


def solution(mesh):
    return jax.shard_map(
        shards,
        mesh=mesh,
        in_specs=(
            P("seq", "tp"),
            P("seq", None),
            P("seq", None),
            P("seq"),
            P(None, "tp"),
            P("tp", None),
            P(),
            P(),
            P("seq", "tp"),
            P("tp"),
            P("tp", None),
        ),
        out_specs=P(("seq", "tp"), None),
        check_vma=False,
    )
```

```python
import functools

import jax
import jax.numpy as jnp
from jax import lax
from jax.experimental import pallas as pl
from jax.experimental.pallas import tpu as pltpu
from jax.sharding import PartitionSpec as P

DV = 1280
HV = 16
HS = DV // HV
D = 8192
WIN = 64
MERGE = 4
TILE_WIN = 4
TILE_SLOTS = 4
GROUP = 4
F32 = jnp.float32
BF = jnp.bfloat16
MIB = 1024 * 1024


def attend_kernel(tp, moves, nw, aliased, info, *refs):
    pieces = refs[:tp]
    at = tp
    w_refs = refs[at : at + nw]
    vit_gain, merge_gain = refs[at + nw : at + nw + 2]
    at += nw + 2 + int(aliased)
    out = refs[at]
    w, xs, nrm, packed, mixed, vit, sem = refs[at + 1 :]
    t = info[0]
    heads = HV // tp
    rows = packed.shape[1]
    feats = pieces[0].shape[1]
    first_proj = 3 * DV
    cols = xs.shape[1]
    step = pl.program_id(0)

    @pl.when(step == 0)
    def _():
        for part in moves(info, w_refs, w, sem):
            for copy in part:
                copy.start()

    for d, piece in enumerate(pieces):
        xs[pl.ds(pl.multiple_of((t ^ d) * feats, feats), feats), :] = piece[0]

    xf = xs[...].astype(F32)
    scale = lax.rsqrt(jnp.mean(xf * xf, axis=0, keepdims=True) + 1e-6)
    nrm[...] = (xf * scale * vit_gain[...]).astype(BF)

    pair = 2 * WIN
    first = lax.broadcasted_iota(jnp.int32, (WIN, pair), 1) < WIN
    fold = (HS**-0.5) * 1.4426950408889634

    none = jnp.zeros((pair, pair), BF)

    def arrived(d):
        @pl.when(step == 0)
        def _():
            for copy in moves(info, w_refs, w, sem)[d]:
                copy.wait()

    def pack(d, slot):
        mine = w[pl.ds(pl.multiple_of((t ^ d) * rows, rows), rows), :]
        packed[slot] = jnp.dot(mine, nrm[...], preferred_element_type=F32).astype(BF)

    def heads_of(d, more):
        slot = lax.rem(d, 2)
        now = packed.at[slot]
        scores = []
        for h in range(heads):
            q, k = (now[(3 * h + n) * HS : (3 * h + n + 1) * HS, :] for n in range(2))
            s = lax.dot_general(k, q, (((0,), (0,)), ((), ())), preferred_element_type=F32)
            for n in range(cols // pair):
                at = n * pair
                s0, s1 = s[at : at + WIN, at : at + pair], s[at + WIN : at + pair, at : at + pair]
                scores.append(jnp.where(first, s0, s1) * fold)
        if more:
            pack(d + 1, 1 - slot)
        probs = []
        for s in scores:
            p = jnp.exp2(s - jnp.max(s, axis=0, keepdims=True))
            p = p * (1.0 / jnp.sum(p, axis=0, keepdims=True))
            probs.append(
                jnp.concatenate([jnp.where(first, p, 0.0), jnp.where(first, 0.0, p)]).astype(BF)
            )
        for h in range(heads):
            v = now[(3 * h + 2) * HS : (3 * h + 3) * HS, :]
            p = jnp.concatenate(
                [
                    jnp.concatenate([probs[2 * h], none], axis=1),
                    jnp.concatenate([none, probs[2 * h + 1]], axis=1),
                ]
            )
            m = jnp.dot(v, p, preferred_element_type=F32)
            at = pl.multiple_of((t ^ d) * heads * HS, heads * HS) + h * HS
            mixed[pl.ds(at, HS), :] = m.astype(BF)

    def one(d, carry):
        for later in range(1, tp):
            pl.when(d + 1 == later)(functools.partial(arrived, later))
        heads_of(d, True)
        return carry

    arrived(0)
    pack(0, 0)
    lax.fori_loop(0, tp - 1, one, 0)
    heads_of(jnp.int32(tp - 1), False)

    width = 256
    sums = jnp.zeros((cols, 1), F32)
    for n in range(DV // width):
        part = slice(n * width, (n + 1) * width)
        proj = lax.dot_general(
            mixed[...],
            w[first_proj : first_proj + DV, part],
            (((0,), (0,)), ((), ())),
            preferred_element_type=F32,
        )
        y = (xs[part, :].T.astype(F32) + proj).astype(BF)
        vit[:, part] = y
        yf = y.astype(F32)
        sums = sums + jnp.sum(yf * yf, axis=1, keepdims=True)
    scale = lax.rsqrt(sums * (1.0 / DV) + 1e-6)
    merged = (vit[...].astype(F32) * scale * merge_gain[...]).astype(BF)
    per = WIN // MERGE
    for w_at in range(cols // WIN):
        for c in range(MERGE):
            at = w_at * WIN + c * per
            out[c, 0, w_at * per : (w_at + 1) * per] = merged[at : at + per, :]


def attend(tp, info, pieces, weights, moves, count, vit_gain, merge_gain, blocks, buf, skip, nb):
    _, feats, cols = pieces[0].shape
    per = cols // MERGE
    x_spec = pl.BlockSpec((1, feats, cols), lambda i, s: (skip + i, 0, 0))
    anywhere = pl.BlockSpec(memory_space=pl.ANY)
    ins = [*pieces, *weights, vit_gain, merge_gain]
    specs = [x_spec] * tp + [anywhere] * len(weights)
    specs += [pl.BlockSpec((DV, 1), lambda i, s: (0, 0)), pl.BlockSpec((1, DV), lambda i, s: (0, 0))]
    alias = {}
    if buf is not None:
        ins.append(buf)
        specs.append(anywhere)
        alias = {len(ins): 0}
    return pl.pallas_call(
        functools.partial(attend_kernel, tp, moves, len(weights), buf is not None),
        out_shape=jax.ShapeDtypeStruct((MERGE, blocks, per, DV), BF),
        grid_spec=pltpu.PrefetchScalarGridSpec(
            num_scalar_prefetch=1,
            grid=(nb,),
            in_specs=specs,
            out_specs=pl.BlockSpec((MERGE, 1, per, DV), lambda i, s: (0, s[2 + i], 0, 0)),
            scratch_shapes=[
                pltpu.VMEM((4 * DV, DV), BF),
                pltpu.VMEM((DV, cols), BF),
                pltpu.VMEM((DV, cols), BF),
                pltpu.VMEM((2, 3 * DV // tp, cols), BF),
                pltpu.VMEM((DV, cols), BF),
                pltpu.VMEM((cols, DV), BF),
                pltpu.SemaphoreType.DMA((count,)),
            ],
        ),
        input_output_aliases=alias,
        compiler_params=pltpu.CompilerParams(
            vmem_limit_bytes=48 * MIB, dimension_semantics=("arbitrary",)
        ),
        cost_estimate=pl.CostEstimate(
            flops=nb * cols * DV * DV * 10,
            bytes_accessed=14 * MIB,
            transcendentals=nb * cols * cols * HV,
        ),
        name="attend",
    )(info, *ins)


def project_kernel(moves, position, nw, info, *refs):
    merged = refs[0]
    w_refs = refs[1 : 1 + nw]
    w_cache, llm_gain, out = refs[1 + nw : 4 + nw]
    held, slots, cache, acc, scaled, held_sem, slot_sem, cache_sem = refs[4 + nw :]
    units = scaled.shape[1]
    half = units // 2
    rows = held.shape[1]
    depth = slots.shape[0]
    width = min(1024, half)
    chunks = [(h, i) for h in range(2) for i in range(MERGE)]

    def bring(n):
        return moves(info, w_refs, *chunks[n], slots.at[n % depth], slot_sem.at[n % depth])

    def bring_merged(i):
        c = position(info, i)
        return pltpu.make_async_copy(merged.at[c], held.at[c], held_sem.at[i])

    load_cache = pltpu.make_async_copy(w_cache, cache, cache_sem)
    for n in range(depth):
        bring_merged(n).start()
        for copy in bring(n):
            copy.start()
    for n in range(depth, MERGE):
        bring_merged(n).start()
    load_cache.start()
    total = jnp.zeros((rows, 1), F32)
    for n, (h, i) in enumerate(chunks):
        c = position(info, i)
        if h == 0:
            bring_merged(i).wait()
        for copy in bring(n):
            copy.wait()
        slot = n % depth

        def tile(j, carry):
            spot = pl.ds(pl.multiple_of(j * width, width), width)
            d = jnp.dot(held[c], slots[slot, :, spot], preferred_element_type=F32)
            if i == 0:
                acc[:, spot] = d
            else:
                acc[:, spot] += d
            return carry

        lax.fori_loop(0, half // width, tile, 0)
        if n + depth < len(chunks):
            for copy in bring(n + depth):
                copy.start()
        if i == MERGE - 1:
            hidden = acc[...].astype(BF).astype(F32)
            total = total + jnp.sum(hidden * hidden, axis=1, keepdims=True)
            part = slice(h * half, (h + 1) * half)
            scaled[:, part] = (hidden * llm_gain[:, part]).astype(BF)
    load_cache.wait()
    kvw = cache.shape[1]

    def kv_tile(j, carry):
        spot = pl.ds(pl.multiple_of(j * 256, 256), 256)
        out[:, spot] = jnp.dot(scaled[...], cache[:, spot], preferred_element_type=F32).astype(BF)
        return carry

    lax.fori_loop(0, kvw // 256, kv_tile, 0)
    out[:, kvw:] = jnp.broadcast_to(total, (rows, 128)).astype(BF)


def project(info, merged, weights, moves, position, w_cache, llm_gain):
    units, kvw = w_cache.shape
    rows = merged.shape[1] * merged.shape[2]
    anywhere = pl.BlockSpec(memory_space=pl.ANY)
    return pl.pallas_call(
        functools.partial(project_kernel, moves, position, len(weights)),
        out_shape=jax.ShapeDtypeStruct((rows, kvw + 128), BF),
        grid_spec=pltpu.PrefetchScalarGridSpec(
            num_scalar_prefetch=1,
            grid=(1,),
            in_specs=[anywhere] * (len(weights) + 2)
            + [pl.BlockSpec((1, units), lambda i, s: (0, 0))],
            out_specs=pl.BlockSpec((rows, kvw + 128), lambda i, s: (0, 0)),
            scratch_shapes=[
                pltpu.VMEM((MERGE, rows, DV), BF),
                pltpu.VMEM((3, DV, units // 2), BF),
                pltpu.VMEM((units, kvw), BF),
                pltpu.VMEM((rows, units // 2), F32),
                pltpu.VMEM((rows, units), BF),
                pltpu.SemaphoreType.DMA((MERGE,)),
                pltpu.SemaphoreType.DMA((3, 4)),
                pltpu.SemaphoreType.DMA,
            ],
        ),
        compiler_params=pltpu.CompilerParams(
            vmem_limit_bytes=48 * MIB, dimension_semantics=("arbitrary",)
        ),
        cost_estimate=pl.CostEstimate(
            flops=2 * rows * units * (MERGE * DV + kvw),
            bytes_accessed=36 * MIB,
            transcendentals=0,
        ),
        name="project",
    )(info, merged.reshape(MERGE, rows, DV), *weights, w_cache, llm_gain)


def shards(
    patches, route, order, tiles, w_qkv, w_proj, vit_gain, merge_gain, w_merge, llm_gain, w_cache
):
    seq_count = lax.axis_size("seq")
    tp = lax.axis_size("tp")
    s = lax.axis_index("seq").astype(jnp.int32)
    t = lax.axis_index("tp").astype(jnp.int32)
    win_dev = order.shape[1]
    feats = patches.shape[1]
    per_peer = win_dev // seq_count
    tokens = WIN // MERGE
    blocks = win_dev // GROUP
    picks = order[0]
    tile_index = picks // TILE_WIN
    counts = jnp.take(tiles, tile_index // TILE_SLOTS)
    live = (tile_index % TILE_SLOTS < counts).astype(jnp.int32)
    arrange = jnp.argsort(route[:, 0], stable=True)
    live_send = jnp.take(live, arrange).reshape(seq_count, per_peer)
    window = jnp.take(picks, arrange).reshape(seq_count, per_peer)

    def xor(x, d):
        return lax.ppermute(x, "seq", [(i, i ^ d) for i in range(seq_count)])

    def tie(x, after):
        return lax.optimization_barrier((x, after))[0]

    def tp_xor(x, d):
        return lax.ppermute(x, "tp", [(i, i ^ d) for i in range(tp)])

    def spread(x):
        held = {0: x}
        d = tp // 2
        while d:
            held.update({k ^ d: tp_xor(v, d) for k, v in list(held.items())})
            d //= 2
        return [held[d] for d in range(tp)]

    paired = seq_count == 8 and per_peer == GROUP

    source = (
        window[:, :, None, None] * WIN
        + jnp.arange(tokens)[None, None, None, :] * MERGE
        + jnp.arange(MERGE)[None, None, :, None]
    ).reshape(-1)
    pick = (jnp.arange(patches.shape[0])[:, None] == source[None, :]).astype(BF)
    sent = lax.dot_general(
        patches, pick, (((0,), (0,)), ((), ())), preferred_element_type=F32
    ).astype(BF)
    alive = jnp.repeat(live_send.reshape(-1), WIN).astype(BF)
    sent = jnp.concatenate([sent, jnp.broadcast_to(alive, (16, alive.shape[0]))])
    step = per_peer * WIN
    wq_t = w_qkv.T

    full = lax.all_to_all(
        sent.reshape(feats + 16, seq_count, step).transpose(1, 0, 2),
        "seq",
        split_axis=0,
        concat_axis=0,
        tiled=True,
    )
    live_here = full[:, feats, ::WIN]
    full = full[:, :feats].reshape(blocks, GROUP // per_peer, feats, step)
    full = full.transpose(0, 2, 1, 3).reshape(blocks, feats, GROUP * WIN)
    mid = blocks // 2

    if paired:
        share = w_proj.shape[0]
        q_parts = wq_t.shape[0] // share

        def left_part(s):
            return s & 3

        def right_part(s):
            return (s & 1) + (s // 4) * 2

        def shard_part(n):
            first = jnp.minimum(n, q_parts - 1) * share
            return jnp.where(n < q_parts, lax.dynamic_slice_in_dim(wq_t, first, share), w_proj)

        def sides_of_tp(x):
            return lax.optimization_barrier((tp_xor(x, 1), tp_xor(x, 2)))

        wide = DV // 2
        mine = jnp.concatenate(
            [shard_part(left_part(s))[:, :wide], shard_part(right_part(s))[:, wide:]], axis=1
        )
        by1, by2 = sides_of_tp(mine)
        by3 = tp_xor(by2, 1)
        near = sides_of_tp(tie(full[:mid], by3))

        cut = w_merge.shape[0] // 2
        upper, lower = w_merge[:cut], w_merge[cut:]
        first_upper, first_lower = tie((upper, lower), full)
        first_upper, first_lower = xor(first_upper, 2), xor(first_lower, 4)

        left = jnp.concatenate([b[:, :wide] for b in (by1, by2, by3)])
        right = jnp.concatenate([b[:, wide:] for b in (by1, by2, by3)])
        (left, right), (first_upper, first_lower) = lax.optimization_barrier(
            ((left, right), (first_upper, first_lower))
        )
        by_x, by_y, near = lax.optimization_barrier((xor(left, 2), xor(right, 4), near))
        far = tp_xor(near[1], 1)
        upper = jnp.concatenate([upper, first_upper])
        lower = jnp.concatenate([lower, first_lower])
        upper, lower = tie((upper, lower), (by_x, by_y))
        merge_along = xor(upper, 4), xor(lower, 2)
        stack = jnp.concatenate([left, by_x, right, by_y])
        vit_weights = [wq_t, w_proj, stack, xor(stack, 1)]
        q_rows, p_rows = wq_t.shape[0], w_proj.shape[0]
        vit_count = 2 + 8 * (tp - 1)
        halves = [[(0, 0), (2, 0)], [(0, 1), (4, 1)], [(4, 0), (6, 0)], [(2, 1), (6, 1)]]
        merge_parts = [
            (4 * e + n, d ^ e, half, at)
            for e in range(2)
            for n, pieces in enumerate(halves)
            for at, (d, half) in enumerate(pieces)
        ]

        def vit_moves(info, refs, w, sem):
            t, s = info[0], info[1]
            copies = [[] for _ in range(tp)]
            copies[0] = [
                pltpu.make_async_copy(
                    refs[0], w.at[pl.ds(pl.multiple_of(t * q_rows, 16), q_rows)], sem.at[0]
                ),
                pltpu.make_async_copy(
                    refs[1], w.at[pl.ds(pl.multiple_of(3 * DV + t * p_rows, 16), p_rows)], sem.at[1]
                ),
            ]
            for e in range(2):
                parts = [left_part(s ^ e), left_part(s ^ e ^ 2), right_part(s ^ e), right_part(s ^ e ^ 4)]
                for b, part in enumerate(parts):
                    for j in range(1, tp):
                        q = t ^ j
                        row = jnp.where(
                            part < q_parts, q * q_rows + part * share, 3 * DV + q * p_rows
                        )
                        first = (b * (tp - 1) + j - 1) * share
                        copies[j].append(
                            pltpu.make_async_copy(
                                refs[2 + e].at[first : first + share],
                                w.at[
                                    pl.ds(pl.multiple_of(row, 16), share),
                                    b // 2 * wide : (b // 2 + 1) * wide,
                                ],
                                sem.at[2 + (e * 4 + b) * (tp - 1) + j - 1],
                            )
                        )
            return copies

        def merge_moves(info, refs, h, i, slot, sem):
            s = info[1]
            wide = slot.shape[1]
            rows = slot.shape[0] // 2
            copies = []
            for n, d, half, at in merge_parts:
                if d // 2 == i:
                    spot = pl.ds(pl.multiple_of(((s ^ d) & 1) * rows + half * cut, 16), cut)
                    part = refs[n].at[at * cut : (at + 1) * cut, h * wide : (h + 1) * wide]
                    copies.append(pltpu.make_async_copy(part, slot.at[spot], sem.at[len(copies)]))
            return copies

        def position(info, i):
            return (info[1] // 2) ^ i

    else:
        vit_weights = [
            lax.all_gather(wq_t, "tp", axis=0, tiled=True),
            lax.all_gather(w_proj, "tp", axis=0, tiled=True),
        ]
        merge_weights = [lax.all_gather(w_merge, "seq", axis=0, tiled=True)]
        vit_count = 2 * tp
        q_rows, p_rows = wq_t.shape[0], w_proj.shape[0]

        def vit_moves(info, refs, w, sem):
            copies = []
            for d in range(tp):
                g = info[0] ^ d
                q_part = pl.ds(pl.multiple_of(g * q_rows, 16), q_rows)
                p_part = pl.ds(pl.multiple_of(g * p_rows, 16), p_rows)
                p_spot = pl.ds(pl.multiple_of(3 * DV + g * p_rows, 16), p_rows)
                copies.append(
                    [
                        pltpu.make_async_copy(refs[0].at[q_part], w.at[q_part], sem.at[2 * d]),
                        pltpu.make_async_copy(refs[1].at[p_part], w.at[p_spot], sem.at[2 * d + 1]),
                    ]
                )
            return copies

        def merge_moves(info, refs, h, i, slot, sem):
            wide = slot.shape[1]
            part = refs[0].at[i * DV : (i + 1) * DV, h * wide : (h + 1) * wide]
            return [pltpu.make_async_copy(part, slot, sem.at[0])]

        def position(info, i):
            return i

    def encode(first, pieces, buf, skip=0, count=None):
        count = pieces[0].shape[0] if count is None else count
        info = jnp.concatenate([jnp.stack([t, s]), first + jnp.arange(count, dtype=jnp.int32)])
        return attend(
            tp, info, pieces, vit_weights, vit_moves, vit_count,
            vit_gain[:, None], merge_gain[None, :], blocks, buf, skip, count,
        )

    merged = None
    if paired:
        by1, by2 = near
        own = tie(full[mid:], (far, vit_weights[2:]))
        merged = encode(0, [full[:mid], by1, by2, far], None)
        by1, by2 = sides_of_tp(own)
        merged, by2 = lax.optimization_barrier((merged, by2))
        pieces = [full[mid:], by1, by2, tp_xor(by2, 1)]
        part = mid // 2
        merged = encode(mid, pieces, merged, 0, part)
        merged, merge_along = lax.optimization_barrier((merged, merge_along))
        merge_weights = [upper, lower, *merge_along]
        merge_weights += [xor(v, 1) for v in merge_weights]
        merged = encode(mid + part, pieces, merged, part, mid - part)
    else:
        for first in (0, mid):
            merged = encode(first, spread(full[first : first + mid]), merged)
    partial_value = project(
        jnp.stack([t, s]), merged, merge_weights, merge_moves, position, w_cache, llm_gain[None, :]
    )
    summed = lax.psum_scatter(partial_value, "tp", scatter_dimension=0, tiled=True).astype(F32)
    kvw = w_cache.shape[1]
    cache, total_squares = summed[:, :kvw], summed[:, kvw : kvw + 1]
    share = cache.shape[0]
    live_tokens = jnp.repeat(live_here.reshape(-1), tokens)
    mine = lax.dynamic_slice_in_dim(live_tokens, t * share, share).astype(F32)
    return (cache * lax.rsqrt(total_squares / D + 1e-6) * mine[:, None]).astype(BF)


def solution(mesh):
    return jax.shard_map(
        shards,
        mesh=mesh,
        in_specs=(
            P("seq", "tp"),
            P("seq", None),
            P("seq", None),
            P("seq"),
            P(None, "tp"),
            P("tp", None),
            P(),
            P(),
            P("seq", "tp"),
            P("tp"),
            P("tp", None),
        ),
        out_specs=P(("seq", "tp"), None),
        check_vma=False,
    )
```

```python
import functools

import jax
import jax.numpy as jnp
from jax import lax
from jax.experimental import pallas as pl
from jax.experimental.pallas import tpu as pltpu
from jax.sharding import PartitionSpec as P

DV = 1280
HV = 16
HS = DV // HV
D = 8192
WIN = 64
MERGE = 4
TILE_WIN = 4
TILE_SLOTS = 4
GROUP = 4
F32 = jnp.float32
BF = jnp.bfloat16
MIB = 1024 * 1024


def attend_kernel(tp, moves, nw, aliased, info, *refs):
    pieces = refs[:tp]
    at = tp
    w_refs = refs[at : at + nw]
    vit_gain, merge_gain = refs[at + nw : at + nw + 2]
    at += nw + 2 + int(aliased)
    out = refs[at]
    w, xs, nrm, packed, mixed, vit, sem = refs[at + 1 :]
    t = info[0]
    heads = HV // tp
    rows = packed.shape[1]
    feats = pieces[0].shape[1]
    first_proj = 3 * DV
    cols = xs.shape[1]
    step = pl.program_id(0)

    @pl.when(step == 0)
    def _():
        for part in moves(info, w_refs, w, sem):
            for copy in part:
                copy.start()

    for d, piece in enumerate(pieces):
        xs[pl.ds(pl.multiple_of((t ^ d) * feats, feats), feats), :] = piece[0]

    xf = xs[...].astype(F32)
    scale = lax.rsqrt(jnp.mean(xf * xf, axis=0, keepdims=True) + 1e-6)
    nrm[...] = (xf * scale * vit_gain[...]).astype(BF)

    pair = 2 * WIN
    first = lax.broadcasted_iota(jnp.int32, (WIN, pair), 1) < WIN
    fold = (HS**-0.5) * 1.4426950408889634

    none = jnp.zeros((pair, pair), BF)

    def arrived(d):
        @pl.when(step == 0)
        def _():
            for copy in moves(info, w_refs, w, sem)[d]:
                copy.wait()

    def pack(d, slot):
        mine = w[pl.ds(pl.multiple_of((t ^ d) * rows, rows), rows), :]
        packed[slot] = jnp.dot(mine, nrm[...], preferred_element_type=F32).astype(BF)

    def heads_of(d, more):
        slot = lax.rem(d, 2)
        now = packed.at[slot]
        scores = []
        for h in range(heads):
            q, k = (now[(3 * h + n) * HS : (3 * h + n + 1) * HS, :] for n in range(2))
            s = lax.dot_general(k, q, (((0,), (0,)), ((), ())), preferred_element_type=F32)
            for n in range(cols // pair):
                at = n * pair
                s0, s1 = s[at : at + WIN, at : at + pair], s[at + WIN : at + pair, at : at + pair]
                scores.append(jnp.where(first, s0, s1) * fold)
        if more:
            pack(d + 1, 1 - slot)
        probs = []
        for s in scores:
            p = jnp.exp2(s - jnp.max(s, axis=0, keepdims=True))
            p = p * (1.0 / jnp.sum(p, axis=0, keepdims=True))
            probs.append(
                jnp.concatenate([jnp.where(first, p, 0.0), jnp.where(first, 0.0, p)]).astype(BF)
            )
        for h in range(heads):
            v = now[(3 * h + 2) * HS : (3 * h + 3) * HS, :]
            p = jnp.concatenate(
                [
                    jnp.concatenate([probs[2 * h], none], axis=1),
                    jnp.concatenate([none, probs[2 * h + 1]], axis=1),
                ]
            )
            m = jnp.dot(v, p, preferred_element_type=F32)
            at = pl.multiple_of((t ^ d) * heads * HS, heads * HS) + h * HS
            mixed[pl.ds(at, HS), :] = m.astype(BF)

    def one(d, carry):
        for later in range(1, tp):
            pl.when(d + 1 == later)(functools.partial(arrived, later))
        heads_of(d, True)
        return carry

    arrived(0)
    pack(0, 0)
    lax.fori_loop(0, tp - 1, one, 0)
    heads_of(jnp.int32(tp - 1), False)

    width = 256
    sums = jnp.zeros((cols, 1), F32)
    for n in range(DV // width):
        part = slice(n * width, (n + 1) * width)
        proj = lax.dot_general(
            mixed[...],
            w[first_proj : first_proj + DV, part],
            (((0,), (0,)), ((), ())),
            preferred_element_type=F32,
        )
        y = (xs[part, :].T.astype(F32) + proj).astype(BF)
        vit[:, part] = y
        yf = y.astype(F32)
        sums = sums + jnp.sum(yf * yf, axis=1, keepdims=True)
    scale = lax.rsqrt(sums * (1.0 / DV) + 1e-6)
    merged = (vit[...].astype(F32) * scale * merge_gain[...]).astype(BF)
    per = WIN // MERGE
    for w_at in range(cols // WIN):
        for c in range(MERGE):
            at = w_at * WIN + c * per
            out[c, 0, w_at * per : (w_at + 1) * per] = merged[at : at + per, :]


def attend(tp, info, pieces, weights, moves, count, vit_gain, merge_gain, blocks, buf):
    nb, feats, cols = pieces[0].shape
    per = cols // MERGE
    x_spec = pl.BlockSpec((1, feats, cols), lambda i, s: (i, 0, 0))
    anywhere = pl.BlockSpec(memory_space=pl.ANY)
    ins = [*pieces, *weights, vit_gain, merge_gain]
    specs = [x_spec] * tp + [anywhere] * len(weights)
    specs += [pl.BlockSpec((DV, 1), lambda i, s: (0, 0)), pl.BlockSpec((1, DV), lambda i, s: (0, 0))]
    alias = {}
    if buf is not None:
        ins.append(buf)
        specs.append(anywhere)
        alias = {len(ins): 0}
    return pl.pallas_call(
        functools.partial(attend_kernel, tp, moves, len(weights), buf is not None),
        out_shape=jax.ShapeDtypeStruct((MERGE, blocks, per, DV), BF),
        grid_spec=pltpu.PrefetchScalarGridSpec(
            num_scalar_prefetch=1,
            grid=(nb,),
            in_specs=specs,
            out_specs=pl.BlockSpec((MERGE, 1, per, DV), lambda i, s: (0, s[2 + i], 0, 0)),
            scratch_shapes=[
                pltpu.VMEM((4 * DV, DV), BF),
                pltpu.VMEM((DV, cols), BF),
                pltpu.VMEM((DV, cols), BF),
                pltpu.VMEM((2, 3 * DV // tp, cols), BF),
                pltpu.VMEM((DV, cols), BF),
                pltpu.VMEM((cols, DV), BF),
                pltpu.SemaphoreType.DMA((count,)),
            ],
        ),
        input_output_aliases=alias,
        compiler_params=pltpu.CompilerParams(
            vmem_limit_bytes=48 * MIB, dimension_semantics=("arbitrary",)
        ),
        cost_estimate=pl.CostEstimate(
            flops=nb * cols * DV * DV * 10,
            bytes_accessed=14 * MIB,
            transcendentals=nb * cols * cols * HV,
        ),
        name="attend",
    )(info, *ins)


def project_kernel(moves, position, nw, info, *refs):
    merged = refs[0]
    w_refs = refs[1 : 1 + nw]
    w_cache, llm_gain, out = refs[1 + nw : 4 + nw]
    held, slots, cache, acc, scaled, held_sem, slot_sem, cache_sem = refs[4 + nw :]
    units = scaled.shape[1]
    half = units // 2
    rows = held.shape[1]
    depth = slots.shape[0]
    width = min(1024, half)
    chunks = [(h, i) for h in range(2) for i in range(MERGE)]

    def bring(n):
        return moves(info, w_refs, *chunks[n], slots.at[n % depth], slot_sem.at[n % depth])

    def bring_merged(i):
        c = position(info, i)
        return pltpu.make_async_copy(merged.at[c], held.at[c], held_sem.at[i])

    load_cache = pltpu.make_async_copy(w_cache, cache, cache_sem)
    for n in range(depth):
        bring_merged(n).start()
        for copy in bring(n):
            copy.start()
    for n in range(depth, MERGE):
        bring_merged(n).start()
    load_cache.start()
    total = jnp.zeros((rows, 1), F32)
    for n, (h, i) in enumerate(chunks):
        c = position(info, i)
        if h == 0:
            bring_merged(i).wait()
        for copy in bring(n):
            copy.wait()
        slot = n % depth

        def tile(j, carry):
            spot = pl.ds(pl.multiple_of(j * width, width), width)
            d = jnp.dot(held[c], slots[slot, :, spot], preferred_element_type=F32)
            if i == 0:
                acc[:, spot] = d
            else:
                acc[:, spot] += d
            return carry

        lax.fori_loop(0, half // width, tile, 0)
        if n + depth < len(chunks):
            for copy in bring(n + depth):
                copy.start()
        if i == MERGE - 1:
            hidden = acc[...].astype(BF).astype(F32)
            total = total + jnp.sum(hidden * hidden, axis=1, keepdims=True)
            part = slice(h * half, (h + 1) * half)
            scaled[:, part] = (hidden * llm_gain[:, part]).astype(BF)
    load_cache.wait()
    kvw = cache.shape[1]

    def kv_tile(j, carry):
        spot = pl.ds(pl.multiple_of(j * 256, 256), 256)
        out[:, spot] = jnp.dot(scaled[...], cache[:, spot], preferred_element_type=F32).astype(BF)
        return carry

    lax.fori_loop(0, kvw // 256, kv_tile, 0)
    out[:, kvw:] = jnp.broadcast_to(total, (rows, 128)).astype(BF)


def project(info, merged, weights, moves, position, w_cache, llm_gain):
    units, kvw = w_cache.shape
    rows = merged.shape[1] * merged.shape[2]
    anywhere = pl.BlockSpec(memory_space=pl.ANY)
    return pl.pallas_call(
        functools.partial(project_kernel, moves, position, len(weights)),
        out_shape=jax.ShapeDtypeStruct((rows, kvw + 128), BF),
        grid_spec=pltpu.PrefetchScalarGridSpec(
            num_scalar_prefetch=1,
            grid=(1,),
            in_specs=[anywhere] * (len(weights) + 2)
            + [pl.BlockSpec((1, units), lambda i, s: (0, 0))],
            out_specs=pl.BlockSpec((rows, kvw + 128), lambda i, s: (0, 0)),
            scratch_shapes=[
                pltpu.VMEM((MERGE, rows, DV), BF),
                pltpu.VMEM((3, DV, units // 2), BF),
                pltpu.VMEM((units, kvw), BF),
                pltpu.VMEM((rows, units // 2), F32),
                pltpu.VMEM((rows, units), BF),
                pltpu.SemaphoreType.DMA((MERGE,)),
                pltpu.SemaphoreType.DMA((3, 4)),
                pltpu.SemaphoreType.DMA,
            ],
        ),
        compiler_params=pltpu.CompilerParams(
            vmem_limit_bytes=48 * MIB, dimension_semantics=("arbitrary",)
        ),
        cost_estimate=pl.CostEstimate(
            flops=2 * rows * units * (MERGE * DV + kvw),
            bytes_accessed=36 * MIB,
            transcendentals=0,
        ),
        name="project",
    )(info, merged.reshape(MERGE, rows, DV), *weights, w_cache, llm_gain)


def shards(
    patches, route, order, tiles, w_qkv, w_proj, vit_gain, merge_gain, w_merge, llm_gain, w_cache
):
    seq_count = lax.axis_size("seq")
    tp = lax.axis_size("tp")
    s = lax.axis_index("seq").astype(jnp.int32)
    t = lax.axis_index("tp").astype(jnp.int32)
    win_dev = order.shape[1]
    feats = patches.shape[1]
    per_peer = win_dev // seq_count
    tokens = WIN // MERGE
    blocks = win_dev // GROUP
    picks = order[0]
    tile_index = picks // TILE_WIN
    counts = jnp.take(tiles, tile_index // TILE_SLOTS)
    live = (tile_index % TILE_SLOTS < counts).astype(jnp.int32)
    arrange = jnp.argsort(route[:, 0], stable=True)
    live_send = jnp.take(live, arrange).reshape(seq_count, per_peer)
    window = jnp.take(picks, arrange).reshape(seq_count, per_peer)

    def xor(x, d):
        return lax.ppermute(x, "seq", [(i, i ^ d) for i in range(seq_count)])

    def tie(x, after):
        return lax.optimization_barrier((x, after))[0]

    def tp_xor(x, d):
        return lax.ppermute(x, "tp", [(i, i ^ d) for i in range(tp)])

    def spread(x):
        held = {0: x}
        d = tp // 2
        while d:
            held.update({k ^ d: tp_xor(v, d) for k, v in list(held.items())})
            d //= 2
        return [held[d] for d in range(tp)]

    paired = seq_count == 8 and per_peer == GROUP

    source = (
        window[:, :, None, None] * WIN
        + jnp.arange(tokens)[None, None, None, :] * MERGE
        + jnp.arange(MERGE)[None, None, :, None]
    ).reshape(-1)
    pick = (jnp.arange(patches.shape[0])[:, None] == source[None, :]).astype(BF)
    sent = lax.dot_general(
        patches, pick, (((0,), (0,)), ((), ())), preferred_element_type=F32
    ).astype(BF)
    alive = jnp.repeat(live_send.reshape(-1), WIN).astype(BF)
    sent = jnp.concatenate([sent, jnp.broadcast_to(alive, (16, alive.shape[0]))])
    step = per_peer * WIN
    wq_t = w_qkv.T

    full = lax.all_to_all(
        sent.reshape(feats + 16, seq_count, step).transpose(1, 0, 2),
        "seq",
        split_axis=0,
        concat_axis=0,
        tiled=True,
    )
    live_here = full[:, feats, ::WIN]
    full = full[:, :feats].reshape(blocks, GROUP // per_peer, feats, step)
    full = full.transpose(0, 2, 1, 3).reshape(blocks, feats, GROUP * WIN)
    mid = blocks // 2

    if paired:
        share = (wq_t.shape[0] + w_proj.shape[0]) // seq_count
        q_parts = wq_t.shape[0] // share
        mine = jnp.where(
            s < q_parts,
            lax.dynamic_slice_in_dim(wq_t, jnp.minimum(s, q_parts - 1) * share, share),
            lax.dynamic_slice_in_dim(w_proj, jnp.maximum(s - q_parts, 0) * share, share),
        )
        def sides(x):
            return lax.optimization_barrier((xor(x, 2), xor(x, 4)))

        def corners(by_x, by_y):
            half = by_x.shape[0] // 2
            return xor(by_x[:half], 4), xor(by_y[half:], 2)

        def with_cores(pieces):
            return list(pieces) + [xor(v, 1) for v in pieces]

        def parts(rows):
            half = rows // 2
            own = [(0, 0, rows), (2, 0, rows), (4, 0, rows), (6, 0, half), (6, half, rows)]
            return own + [(d ^ 1, lo, hi) for d, lo, hi in own]

        def sides_of_tp(x):
            return lax.optimization_barrier((tp_xor(x, 1), tp_xor(x, 2)))

        by1, by2 = sides_of_tp(mine)
        others = jnp.concatenate([by1, by2, tp_xor(by2, 1)])
        vit_sides = sides(tie(others, full))
        near = sides_of_tp(full[:mid])
        vit_sides, near = lax.optimization_barrier((vit_sides, near))
        far = tp_xor(near[1], 1)
        straight = jnp.concatenate([others, *vit_sides])
        swapped = xor(straight, 1)
        far, vit_corners, swapped = lax.optimization_barrier((far, corners(*vit_sides), swapped))
        diagonal = jnp.concatenate(vit_corners)
        vit_weights = [wq_t, w_proj, straight, swapped, diagonal, xor(diagonal, 1)]
        merge_sides = sides(tie(w_merge, vit_sides))
        q_rows, p_rows = wq_t.shape[0], w_proj.shape[0]
        vit_parts = []
        for n, (d, lo, hi) in enumerate(parts(others.shape[0])):
            at, piece = 2 + n // 5 + 2 * (n % 5 // 3), n % 5 - n % 5 // 3 * 3
            for j in range(1, tp):
                top, end = max(lo, (j - 1) * share), min(hi, j * share)
                if top < end:
                    first = piece * (hi - lo) + top - lo
                    vit_parts.append((at, d, j, first, top - (j - 1) * share, end - top))
        vit_count = 2 + len(vit_parts)

        def vit_moves(info, refs, w, sem):
            t, s = info[0], info[1]
            copies = [[] for _ in range(tp)]
            copies[0] = [
                pltpu.make_async_copy(
                    refs[0], w.at[pl.ds(pl.multiple_of(t * q_rows, 16), q_rows)], sem.at[0]
                ),
                pltpu.make_async_copy(
                    refs[1], w.at[pl.ds(pl.multiple_of(3 * DV + t * p_rows, 16), p_rows)], sem.at[1]
                ),
            ]
            for at, (n, d, j, source, offset, count) in enumerate(vit_parts):
                part = s ^ d
                q = t ^ j
                row = offset + jnp.where(
                    part < q_parts,
                    q * q_rows + part * share,
                    3 * DV + q * p_rows + (part - q_parts) * share,
                )
                copies[j].append(
                    pltpu.make_async_copy(
                        refs[n].at[source : source + count],
                        w.at[pl.ds(pl.multiple_of(row, 16), count)],
                        sem.at[2 + at],
                    )
                )
            return copies

        def merge_moves(info, refs, h, i, slot, sem):
            s = info[1]
            wide = slot.shape[1]
            rows = slot.shape[0] // 2
            copies = []
            for n, (d, lo, hi) in enumerate(parts(rows)):
                if d // 2 == i:
                    spot = pl.ds(pl.multiple_of(((s ^ d) & 1) * rows + lo, 16), hi - lo)
                    part = refs[n].at[:, h * wide : (h + 1) * wide]
                    copies.append(pltpu.make_async_copy(part, slot.at[spot], sem.at[len(copies)]))
            return copies

        def position(info, i):
            return (info[1] // 2) ^ i

    else:
        vit_weights = [
            lax.all_gather(wq_t, "tp", axis=0, tiled=True),
            lax.all_gather(w_proj, "tp", axis=0, tiled=True),
        ]
        merge_weights = [lax.all_gather(w_merge, "seq", axis=0, tiled=True)]
        vit_count = 2 * tp
        q_rows, p_rows = wq_t.shape[0], w_proj.shape[0]

        def vit_moves(info, refs, w, sem):
            copies = []
            for d in range(tp):
                g = info[0] ^ d
                q_part = pl.ds(pl.multiple_of(g * q_rows, 16), q_rows)
                p_part = pl.ds(pl.multiple_of(g * p_rows, 16), p_rows)
                p_spot = pl.ds(pl.multiple_of(3 * DV + g * p_rows, 16), p_rows)
                copies.append(
                    [
                        pltpu.make_async_copy(refs[0].at[q_part], w.at[q_part], sem.at[2 * d]),
                        pltpu.make_async_copy(refs[1].at[p_part], w.at[p_spot], sem.at[2 * d + 1]),
                    ]
                )
            return copies

        def merge_moves(info, refs, h, i, slot, sem):
            wide = slot.shape[1]
            part = refs[0].at[i * DV : (i + 1) * DV, h * wide : (h + 1) * wide]
            return [pltpu.make_async_copy(part, slot, sem.at[0])]

        def position(info, i):
            return i

    def encode(first, pieces, buf):
        count = pieces[0].shape[0]
        info = jnp.concatenate([jnp.stack([t, s]), first + jnp.arange(count, dtype=jnp.int32)])
        return attend(
            tp, info, pieces, vit_weights, vit_moves, vit_count,
            vit_gain[:, None], merge_gain[None, :], blocks, buf,
        )

    merged = None
    if paired:
        by1, by2 = near
        own = tie(full[mid:], (far, vit_weights[2:]))
        merged = encode(0, [full[:mid], by1, by2, far], None)
        by1, by2 = sides_of_tp(own)
        merged, by2 = lax.optimization_barrier((merged, by2))
        far, merge_sides = lax.optimization_barrier((tp_xor(by2, 1), merge_sides))
        merged = encode(mid, [full[mid:], by1, by2, far], merged)
        merge_corners = corners(*merge_sides)
        merged, merge_corners = lax.optimization_barrier((merged, merge_corners))
        merge_weights = with_cores([w_merge, *merge_sides, *merge_corners])
    else:
        for first in (0, mid):
            merged = encode(first, spread(full[first : first + mid]), merged)
    partial_value = project(
        jnp.stack([t, s]), merged, merge_weights, merge_moves, position, w_cache, llm_gain[None, :]
    )
    summed = lax.psum_scatter(partial_value, "tp", scatter_dimension=0, tiled=True).astype(F32)
    kvw = w_cache.shape[1]
    cache, total_squares = summed[:, :kvw], summed[:, kvw : kvw + 1]
    share = cache.shape[0]
    live_tokens = jnp.repeat(live_here.reshape(-1), tokens)
    mine = lax.dynamic_slice_in_dim(live_tokens, t * share, share).astype(F32)
    return (cache * lax.rsqrt(total_squares / D + 1e-6) * mine[:, None]).astype(BF)


def solution(mesh):
    return jax.shard_map(
        shards,
        mesh=mesh,
        in_specs=(
            P("seq", "tp"),
            P("seq", None),
            P("seq", None),
            P("seq"),
            P(None, "tp"),
            P("tp", None),
            P(),
            P(),
            P("seq", "tp"),
            P("tp"),
            P("tp", None),
        ),
        out_specs=P(("seq", "tp"), None),
        check_vma=False,
    )
```

```python
import functools

import jax
import jax.numpy as jnp
from jax import lax
from jax.experimental import pallas as pl
from jax.experimental.pallas import tpu as pltpu
from jax.sharding import PartitionSpec as P

DV = 1280
HV = 16
HS = DV // HV
D = 8192
WIN = 64
MERGE = 4
TILE_WIN = 4
TILE_SLOTS = 4
GROUP = 4
F32 = jnp.float32
BF = jnp.bfloat16
MIB = 1024 * 1024


def attend_kernel(tp, moves, nw, aliased, info, *refs):
    pieces = refs[:tp]
    at = tp
    w_refs = refs[at : at + nw]
    vit_gain, merge_gain = refs[at + nw : at + nw + 2]
    at += nw + 2 + int(aliased)
    out = refs[at]
    w, xs, nrm, packed, mixed, vit, sem = refs[at + 1 :]
    t = info[0]
    heads = HV // tp
    rows = packed.shape[1]
    feats = pieces[0].shape[1]
    first_proj = 3 * DV
    cols = xs.shape[1]
    step = pl.program_id(0)

    @pl.when(step == 0)
    def _():
        for part in moves(info, w_refs, w, sem):
            for copy in part:
                copy.start()

    for d, piece in enumerate(pieces):
        xs[pl.ds(pl.multiple_of((t ^ d) * feats, feats), feats), :] = piece[0]

    xf = xs[...].astype(F32)
    scale = lax.rsqrt(jnp.mean(xf * xf, axis=0, keepdims=True) + 1e-6)
    nrm[...] = (xf * scale * vit_gain[...]).astype(BF)

    pair = 2 * WIN
    first = lax.broadcasted_iota(jnp.int32, (WIN, pair), 1) < WIN
    fold = (HS**-0.5) * 1.4426950408889634

    none = jnp.zeros((pair, pair), BF)

    def arrived(d):
        @pl.when(step == 0)
        def _():
            for copy in moves(info, w_refs, w, sem)[d]:
                copy.wait()

    def pack(d, slot):
        mine = w[pl.ds(pl.multiple_of((t ^ d) * rows, rows), rows), :]
        packed[slot] = jnp.dot(mine, nrm[...], preferred_element_type=F32).astype(BF)

    def heads_of(d, more):
        slot = lax.rem(d, 2)
        now = packed.at[slot]
        scores = []
        for h in range(heads):
            q, k = (now[(3 * h + n) * HS : (3 * h + n + 1) * HS, :] for n in range(2))
            s = lax.dot_general(k, q, (((0,), (0,)), ((), ())), preferred_element_type=F32)
            for n in range(cols // pair):
                at = n * pair
                s0, s1 = s[at : at + WIN, at : at + pair], s[at + WIN : at + pair, at : at + pair]
                scores.append(jnp.where(first, s0, s1) * fold)
        if more:
            pack(d + 1, 1 - slot)
        probs = []
        for s in scores:
            p = jnp.exp2(s - jnp.max(s, axis=0, keepdims=True))
            p = p * (1.0 / jnp.sum(p, axis=0, keepdims=True))
            probs.append(
                jnp.concatenate([jnp.where(first, p, 0.0), jnp.where(first, 0.0, p)]).astype(BF)
            )
        for h in range(heads):
            v = now[(3 * h + 2) * HS : (3 * h + 3) * HS, :]
            p = jnp.concatenate(
                [
                    jnp.concatenate([probs[2 * h], none], axis=1),
                    jnp.concatenate([none, probs[2 * h + 1]], axis=1),
                ]
            )
            m = jnp.dot(v, p, preferred_element_type=F32)
            at = pl.multiple_of((t ^ d) * heads * HS, heads * HS) + h * HS
            mixed[pl.ds(at, HS), :] = m.astype(BF)

    def one(d, carry):
        for later in range(1, tp):
            pl.when(d + 1 == later)(functools.partial(arrived, later))
        heads_of(d, True)
        return carry

    arrived(0)
    pack(0, 0)
    lax.fori_loop(0, tp - 1, one, 0)
    heads_of(jnp.int32(tp - 1), False)

    width = 256
    sums = jnp.zeros((cols, 1), F32)
    for n in range(DV // width):
        part = slice(n * width, (n + 1) * width)
        proj = lax.dot_general(
            mixed[...],
            w[first_proj : first_proj + DV, part],
            (((0,), (0,)), ((), ())),
            preferred_element_type=F32,
        )
        y = (xs[part, :].T.astype(F32) + proj).astype(BF)
        vit[:, part] = y
        yf = y.astype(F32)
        sums = sums + jnp.sum(yf * yf, axis=1, keepdims=True)
    scale = lax.rsqrt(sums * (1.0 / DV) + 1e-6)
    merged = (vit[...].astype(F32) * scale * merge_gain[...]).astype(BF)
    per = WIN // MERGE
    for w_at in range(cols // WIN):
        for c in range(MERGE):
            at = w_at * WIN + c * per
            out[c, 0, w_at * per : (w_at + 1) * per] = merged[at : at + per, :]


def attend(tp, info, pieces, weights, moves, count, vit_gain, merge_gain, blocks, buf):
    nb, feats, cols = pieces[0].shape
    per = cols // MERGE
    x_spec = pl.BlockSpec((1, feats, cols), lambda i, s: (i, 0, 0))
    anywhere = pl.BlockSpec(memory_space=pl.ANY)
    ins = [*pieces, *weights, vit_gain, merge_gain]
    specs = [x_spec] * tp + [anywhere] * len(weights)
    specs += [pl.BlockSpec((DV, 1), lambda i, s: (0, 0)), pl.BlockSpec((1, DV), lambda i, s: (0, 0))]
    alias = {}
    if buf is not None:
        ins.append(buf)
        specs.append(anywhere)
        alias = {len(ins): 0}
    return pl.pallas_call(
        functools.partial(attend_kernel, tp, moves, len(weights), buf is not None),
        out_shape=jax.ShapeDtypeStruct((MERGE, blocks, per, DV), BF),
        grid_spec=pltpu.PrefetchScalarGridSpec(
            num_scalar_prefetch=1,
            grid=(nb,),
            in_specs=specs,
            out_specs=pl.BlockSpec((MERGE, 1, per, DV), lambda i, s: (0, s[2 + i], 0, 0)),
            scratch_shapes=[
                pltpu.VMEM((4 * DV, DV), BF),
                pltpu.VMEM((DV, cols), BF),
                pltpu.VMEM((DV, cols), BF),
                pltpu.VMEM((2, 3 * DV // tp, cols), BF),
                pltpu.VMEM((DV, cols), BF),
                pltpu.VMEM((cols, DV), BF),
                pltpu.SemaphoreType.DMA((count,)),
            ],
        ),
        input_output_aliases=alias,
        compiler_params=pltpu.CompilerParams(
            vmem_limit_bytes=48 * MIB, dimension_semantics=("arbitrary",)
        ),
        cost_estimate=pl.CostEstimate(
            flops=nb * cols * DV * DV * 10,
            bytes_accessed=14 * MIB,
            transcendentals=nb * cols * cols * HV,
        ),
        name="attend",
    )(info, *ins)


def project_kernel(moves, position, nw, info, *refs):
    merged = refs[0]
    w_refs = refs[1 : 1 + nw]
    w_cache, llm_gain, out = refs[1 + nw : 4 + nw]
    held, slots, cache, acc, scaled, held_sem, slot_sem, cache_sem = refs[4 + nw :]
    units = scaled.shape[1]
    half = units // 2
    rows = held.shape[1]
    depth = slots.shape[0]
    width = min(1024, half)
    chunks = [(h, i) for h in range(2) for i in range(MERGE)]

    def bring(n):
        return moves(info, w_refs, *chunks[n], slots.at[n % depth], slot_sem.at[n % depth])

    def bring_merged(i):
        c = position(info, i)
        return pltpu.make_async_copy(merged.at[c], held.at[c], held_sem.at[i])

    load_cache = pltpu.make_async_copy(w_cache, cache, cache_sem)
    for n in range(depth):
        bring_merged(n).start()
        for copy in bring(n):
            copy.start()
    for n in range(depth, MERGE):
        bring_merged(n).start()
    load_cache.start()
    total = jnp.zeros((rows, 1), F32)
    for n, (h, i) in enumerate(chunks):
        c = position(info, i)
        if h == 0:
            bring_merged(i).wait()
        for copy in bring(n):
            copy.wait()
        slot = n % depth

        def tile(j, carry):
            spot = pl.ds(pl.multiple_of(j * width, width), width)
            d = jnp.dot(held[c], slots[slot, :, spot], preferred_element_type=F32)
            if i == 0:
                acc[:, spot] = d
            else:
                acc[:, spot] += d
            return carry

        lax.fori_loop(0, half // width, tile, 0)
        if n + depth < len(chunks):
            for copy in bring(n + depth):
                copy.start()
        if i == MERGE - 1:
            hidden = acc[...].astype(BF).astype(F32)
            total = total + jnp.sum(hidden * hidden, axis=1, keepdims=True)
            part = slice(h * half, (h + 1) * half)
            scaled[:, part] = (hidden * llm_gain[:, part]).astype(BF)
    load_cache.wait()
    kvw = cache.shape[1]

    def kv_tile(j, carry):
        spot = pl.ds(pl.multiple_of(j * 256, 256), 256)
        out[:, spot] = jnp.dot(scaled[...], cache[:, spot], preferred_element_type=F32).astype(BF)
        return carry

    lax.fori_loop(0, kvw // 256, kv_tile, 0)
    out[:, kvw:] = jnp.broadcast_to(total, (rows, 128)).astype(BF)


def project(info, merged, weights, moves, position, w_cache, llm_gain):
    units, kvw = w_cache.shape
    rows = merged.shape[1] * merged.shape[2]
    anywhere = pl.BlockSpec(memory_space=pl.ANY)
    return pl.pallas_call(
        functools.partial(project_kernel, moves, position, len(weights)),
        out_shape=jax.ShapeDtypeStruct((rows, kvw + 128), BF),
        grid_spec=pltpu.PrefetchScalarGridSpec(
            num_scalar_prefetch=1,
            grid=(1,),
            in_specs=[anywhere] * (len(weights) + 2)
            + [pl.BlockSpec((1, units), lambda i, s: (0, 0))],
            out_specs=pl.BlockSpec((rows, kvw + 128), lambda i, s: (0, 0)),
            scratch_shapes=[
                pltpu.VMEM((MERGE, rows, DV), BF),
                pltpu.VMEM((3, DV, units // 2), BF),
                pltpu.VMEM((units, kvw), BF),
                pltpu.VMEM((rows, units // 2), F32),
                pltpu.VMEM((rows, units), BF),
                pltpu.SemaphoreType.DMA((MERGE,)),
                pltpu.SemaphoreType.DMA((3, 4)),
                pltpu.SemaphoreType.DMA,
            ],
        ),
        compiler_params=pltpu.CompilerParams(
            vmem_limit_bytes=48 * MIB, dimension_semantics=("arbitrary",)
        ),
        cost_estimate=pl.CostEstimate(
            flops=2 * rows * units * (MERGE * DV + kvw),
            bytes_accessed=36 * MIB,
            transcendentals=0,
        ),
        name="project",
    )(info, merged.reshape(MERGE, rows, DV), *weights, w_cache, llm_gain)


def shards(
    patches, route, order, tiles, w_qkv, w_proj, vit_gain, merge_gain, w_merge, llm_gain, w_cache
):
    seq_count = lax.axis_size("seq")
    tp = lax.axis_size("tp")
    s = lax.axis_index("seq").astype(jnp.int32)
    t = lax.axis_index("tp").astype(jnp.int32)
    win_dev = order.shape[1]
    feats = patches.shape[1]
    per_peer = win_dev // seq_count
    tokens = WIN // MERGE
    blocks = win_dev // GROUP
    picks = order[0]
    tile_index = picks // TILE_WIN
    counts = jnp.take(tiles, tile_index // TILE_SLOTS)
    live = (tile_index % TILE_SLOTS < counts).astype(jnp.int32)
    arrange = jnp.argsort(route[:, 0], stable=True)
    live_send = jnp.take(live, arrange).reshape(seq_count, per_peer)
    window = jnp.take(picks, arrange).reshape(seq_count, per_peer)

    def xor(x, d):
        return lax.ppermute(x, "seq", [(i, i ^ d) for i in range(seq_count)])

    def tie(x, after):
        return lax.optimization_barrier((x, after))[0]

    def tp_xor(x, d):
        return lax.ppermute(x, "tp", [(i, i ^ d) for i in range(tp)])

    def spread(x):
        held = {0: x}
        d = tp // 2
        while d:
            held.update({k ^ d: tp_xor(v, d) for k, v in list(held.items())})
            d //= 2
        return [held[d] for d in range(tp)]

    paired = seq_count == 8 and per_peer == GROUP

    source = (
        window[:, :, None, None] * WIN
        + jnp.arange(tokens)[None, None, None, :] * MERGE
        + jnp.arange(MERGE)[None, None, :, None]
    ).reshape(-1)
    pick = (jnp.arange(patches.shape[0])[:, None] == source[None, :]).astype(BF)
    sent = lax.dot_general(
        patches, pick, (((0,), (0,)), ((), ())), preferred_element_type=F32
    ).astype(BF)
    alive = jnp.repeat(live_send.reshape(-1), WIN).astype(BF)
    sent = jnp.concatenate([sent, jnp.broadcast_to(alive, (16, alive.shape[0]))])
    step = per_peer * WIN
    wq_t = w_qkv.T

    full = lax.all_to_all(
        sent.reshape(feats + 16, seq_count, step).transpose(1, 0, 2),
        "seq",
        split_axis=0,
        concat_axis=0,
        tiled=True,
    )
    live_here = full[:, feats, ::WIN]
    full = full[:, :feats].reshape(blocks, GROUP // per_peer, feats, step)
    full = full.transpose(0, 2, 1, 3).reshape(blocks, feats, GROUP * WIN)
    mid = blocks // 2

    if paired:
        share = (wq_t.shape[0] + w_proj.shape[0]) // seq_count
        q_parts = wq_t.shape[0] // share
        mine = jnp.where(
            s < q_parts,
            lax.dynamic_slice_in_dim(wq_t, jnp.minimum(s, q_parts - 1) * share, share),
            lax.dynamic_slice_in_dim(w_proj, jnp.maximum(s - q_parts, 0) * share, share),
        )
        def sides(x):
            return lax.optimization_barrier((xor(x, 2), xor(x, 4)))

        def corners(by_x, by_y):
            half = by_x.shape[0] // 2
            return xor(by_x[:half], 4), xor(by_y[half:], 2)

        def with_cores(pieces):
            return list(pieces) + [xor(v, 1) for v in pieces]

        def parts(rows):
            half = rows // 2
            own = [(0, 0, rows), (2, 0, rows), (4, 0, rows), (6, 0, half), (6, half, rows)]
            return own + [(d ^ 1, lo, hi) for d, lo, hi in own]

        def sides_of_tp(x):
            return lax.optimization_barrier((tp_xor(x, 1), tp_xor(x, 2)))

        quarter = w_merge.shape[0] // 4
        early = xor(w_merge[:quarter], 2), xor(w_merge[:quarter], 4)
        (by1, by2), early = lax.optimization_barrier((sides_of_tp(mine), early))
        others = jnp.concatenate([by1, by2, tp_xor(by2, 1)])
        vit_sides = sides(tie(others, full))
        near = sides_of_tp(full[:mid])
        vit_sides, near = lax.optimization_barrier((vit_sides, near))
        far = tp_xor(near[1], 1)
        far, vit_corners = lax.optimization_barrier((far, corners(*vit_sides)))
        vit_weights = [wq_t, w_proj] + with_cores([jnp.concatenate([others, *vit_sides, *vit_corners])])
        merge_sides = sides(tie(w_merge[quarter:], vit_sides))
        q_rows, p_rows = wq_t.shape[0], w_proj.shape[0]
        vit_parts = []
        for n, (d, lo, hi) in enumerate(parts(others.shape[0])):
            base = sum(last - first for _, first, last in parts(others.shape[0])[n // 5 * 5 : n])
            for j in range(1, tp):
                top, end = max(lo, (j - 1) * share), min(hi, j * share)
                if top < end:
                    vit_parts.append(
                        (2 + n // 5, d, j, base + top - lo, top - (j - 1) * share, end - top)
                    )
        vit_count = 2 + len(vit_parts)

        def vit_moves(info, refs, w, sem):
            t, s = info[0], info[1]
            copies = [[] for _ in range(tp)]
            copies[0] = [
                pltpu.make_async_copy(
                    refs[0], w.at[pl.ds(pl.multiple_of(t * q_rows, 16), q_rows)], sem.at[0]
                ),
                pltpu.make_async_copy(
                    refs[1], w.at[pl.ds(pl.multiple_of(3 * DV + t * p_rows, 16), p_rows)], sem.at[1]
                ),
            ]
            for at, (n, d, j, source, offset, count) in enumerate(vit_parts):
                part = s ^ d
                q = t ^ j
                row = offset + jnp.where(
                    part < q_parts,
                    q * q_rows + part * share,
                    3 * DV + q * p_rows + (part - q_parts) * share,
                )
                copies[j].append(
                    pltpu.make_async_copy(
                        refs[n].at[source : source + count],
                        w.at[pl.ds(pl.multiple_of(row, 16), count)],
                        sem.at[2 + at],
                    )
                )
            return copies

        def merge_moves(info, refs, h, i, slot, sem):
            s = info[1]
            wide = slot.shape[1]
            rows = slot.shape[0] // 2
            copies = []
            for n, (d, lo, hi) in enumerate(parts(rows)):
                if d // 2 == i:
                    spot = pl.ds(pl.multiple_of(((s ^ d) & 1) * rows + lo, 16), hi - lo)
                    part = refs[n].at[:, h * wide : (h + 1) * wide]
                    copies.append(pltpu.make_async_copy(part, slot.at[spot], sem.at[len(copies)]))
            return copies

        def position(info, i):
            return (info[1] // 2) ^ i

    else:
        vit_weights = [
            lax.all_gather(wq_t, "tp", axis=0, tiled=True),
            lax.all_gather(w_proj, "tp", axis=0, tiled=True),
        ]
        merge_weights = [lax.all_gather(w_merge, "seq", axis=0, tiled=True)]
        vit_count = 2 * tp
        q_rows, p_rows = wq_t.shape[0], w_proj.shape[0]

        def vit_moves(info, refs, w, sem):
            copies = []
            for d in range(tp):
                g = info[0] ^ d
                q_part = pl.ds(pl.multiple_of(g * q_rows, 16), q_rows)
                p_part = pl.ds(pl.multiple_of(g * p_rows, 16), p_rows)
                p_spot = pl.ds(pl.multiple_of(3 * DV + g * p_rows, 16), p_rows)
                copies.append(
                    [
                        pltpu.make_async_copy(refs[0].at[q_part], w.at[q_part], sem.at[2 * d]),
                        pltpu.make_async_copy(refs[1].at[p_part], w.at[p_spot], sem.at[2 * d + 1]),
                    ]
                )
            return copies

        def merge_moves(info, refs, h, i, slot, sem):
            wide = slot.shape[1]
            part = refs[0].at[i * DV : (i + 1) * DV, h * wide : (h + 1) * wide]
            return [pltpu.make_async_copy(part, slot, sem.at[0])]

        def position(info, i):
            return i

    def encode(first, pieces, buf):
        count = pieces[0].shape[0]
        info = jnp.concatenate([jnp.stack([t, s]), first + jnp.arange(count, dtype=jnp.int32)])
        return attend(
            tp, info, pieces, vit_weights, vit_moves, vit_count,
            vit_gain[:, None], merge_gain[None, :], blocks, buf,
        )

    merged = None
    if paired:
        by1, by2 = near
        own = tie(full[mid:], (far, vit_weights[2:]))
        merged = encode(0, [full[:mid], by1, by2, far], None)
        by1, by2 = sides_of_tp(own)
        merged, by2 = lax.optimization_barrier((merged, by2))
        far, merge_sides = lax.optimization_barrier((tp_xor(by2, 1), merge_sides))
        merged = encode(mid, [full[mid:], by1, by2, far], merged)
        merge_sides = [jnp.concatenate(pair) for pair in zip(early, merge_sides)]
        merge_corners = corners(*merge_sides)
        merged, merge_corners = lax.optimization_barrier((merged, merge_corners))
        merge_weights = with_cores([w_merge, *merge_sides, *merge_corners])
    else:
        for first in (0, mid):
            merged = encode(first, spread(full[first : first + mid]), merged)
    partial_value = project(
        jnp.stack([t, s]), merged, merge_weights, merge_moves, position, w_cache, llm_gain[None, :]
    )
    summed = lax.psum_scatter(partial_value, "tp", scatter_dimension=0, tiled=True).astype(F32)
    kvw = w_cache.shape[1]
    cache, total_squares = summed[:, :kvw], summed[:, kvw : kvw + 1]
    share = cache.shape[0]
    live_tokens = jnp.repeat(live_here.reshape(-1), tokens)
    mine = lax.dynamic_slice_in_dim(live_tokens, t * share, share).astype(F32)
    return (cache * lax.rsqrt(total_squares / D + 1e-6) * mine[:, None]).astype(BF)


def solution(mesh):
    return jax.shard_map(
        shards,
        mesh=mesh,
        in_specs=(
            P("seq", "tp"),
            P("seq", None),
            P("seq", None),
            P("seq"),
            P(None, "tp"),
            P("tp", None),
            P(),
            P(),
            P("seq", "tp"),
            P("tp"),
            P("tp", None),
        ),
        out_specs=P(("seq", "tp"), None),
        check_vma=False,
    )
```

```python
import functools

import jax
import jax.numpy as jnp
from jax import lax
from jax.experimental import pallas as pl
from jax.experimental.pallas import tpu as pltpu
from jax.sharding import PartitionSpec as P

DV = 1280
HV = 16
HS = DV // HV
D = 8192
WIN = 64
MERGE = 4
TILE_WIN = 4
TILE_SLOTS = 4
GROUP = 4
F32 = jnp.float32
BF = jnp.bfloat16
MIB = 1024 * 1024


def attend_kernel(tp, moves, nw, aliased, info, *refs):
    pieces = refs[:tp]
    at = tp
    w_refs = refs[at : at + nw]
    vit_gain, merge_gain = refs[at + nw : at + nw + 2]
    at += nw + 2 + int(aliased)
    out = refs[at]
    w, xs, nrm, packed, mixed, vit, sem = refs[at + 1 :]
    t = info[0]
    heads = HV // tp
    rows = packed.shape[1]
    feats = pieces[0].shape[1]
    first_proj = 3 * DV
    cols = xs.shape[1]
    step = pl.program_id(0)

    @pl.when(step == 0)
    def _():
        for part in moves(info, w_refs, w, sem):
            for copy in part:
                copy.start()

    for d, piece in enumerate(pieces):
        xs[pl.ds(pl.multiple_of((t ^ d) * feats, feats), feats), :] = piece[0]

    xf = xs[...].astype(F32)
    scale = lax.rsqrt(jnp.mean(xf * xf, axis=0, keepdims=True) + 1e-6)
    nrm[...] = (xf * scale * vit_gain[...]).astype(BF)

    pair = 2 * WIN
    first = lax.broadcasted_iota(jnp.int32, (WIN, pair), 1) < WIN
    fold = (HS**-0.5) * 1.4426950408889634

    none = jnp.zeros((pair, pair), BF)

    def arrived(d):
        @pl.when(step == 0)
        def _():
            for copy in moves(info, w_refs, w, sem)[d]:
                copy.wait()

    def pack(d, slot):
        mine = w[pl.ds(pl.multiple_of((t ^ d) * rows, rows), rows), :]
        packed[slot] = jnp.dot(mine, nrm[...], preferred_element_type=F32).astype(BF)

    def heads_of(d, more):
        slot = lax.rem(d, 2)
        now = packed.at[slot]
        scores = []
        for h in range(heads):
            q, k = (now[(3 * h + n) * HS : (3 * h + n + 1) * HS, :] for n in range(2))
            s = lax.dot_general(k, q, (((0,), (0,)), ((), ())), preferred_element_type=F32)
            for n in range(cols // pair):
                at = n * pair
                s0, s1 = s[at : at + WIN, at : at + pair], s[at + WIN : at + pair, at : at + pair]
                scores.append(jnp.where(first, s0, s1) * fold)
        if more:
            pack(d + 1, 1 - slot)
        probs = []
        for s in scores:
            p = jnp.exp2(s - jnp.max(s, axis=0, keepdims=True))
            p = p * (1.0 / jnp.sum(p, axis=0, keepdims=True))
            probs.append(
                jnp.concatenate([jnp.where(first, p, 0.0), jnp.where(first, 0.0, p)]).astype(BF)
            )
        for h in range(heads):
            v = now[(3 * h + 2) * HS : (3 * h + 3) * HS, :]
            p = jnp.concatenate(
                [
                    jnp.concatenate([probs[2 * h], none], axis=1),
                    jnp.concatenate([none, probs[2 * h + 1]], axis=1),
                ]
            )
            m = jnp.dot(v, p, preferred_element_type=F32)
            at = pl.multiple_of((t ^ d) * heads * HS, heads * HS) + h * HS
            mixed[pl.ds(at, HS), :] = m.astype(BF)

    def one(d, carry):
        for later in range(1, tp):
            pl.when(d + 1 == later)(functools.partial(arrived, later))
        heads_of(d, True)
        return carry

    arrived(0)
    pack(0, 0)
    lax.fori_loop(0, tp - 1, one, 0)
    heads_of(jnp.int32(tp - 1), False)

    width = 256
    sums = jnp.zeros((cols, 1), F32)
    for n in range(DV // width):
        part = slice(n * width, (n + 1) * width)
        proj = lax.dot_general(
            mixed[...],
            w[first_proj : first_proj + DV, part],
            (((0,), (0,)), ((), ())),
            preferred_element_type=F32,
        )
        y = (xs[part, :].T.astype(F32) + proj).astype(BF)
        vit[:, part] = y
        yf = y.astype(F32)
        sums = sums + jnp.sum(yf * yf, axis=1, keepdims=True)
    scale = lax.rsqrt(sums * (1.0 / DV) + 1e-6)
    merged = (vit[...].astype(F32) * scale * merge_gain[...]).astype(BF)
    per = WIN // MERGE
    for w_at in range(cols // WIN):
        for c in range(MERGE):
            at = w_at * WIN + c * per
            out[c, 0, w_at * per : (w_at + 1) * per] = merged[at : at + per, :]


def attend(tp, info, pieces, weights, moves, count, vit_gain, merge_gain, blocks, buf):
    nb, feats, cols = pieces[0].shape
    per = cols // MERGE
    x_spec = pl.BlockSpec((1, feats, cols), lambda i, s: (i, 0, 0))
    anywhere = pl.BlockSpec(memory_space=pl.ANY)
    ins = [*pieces, *weights, vit_gain, merge_gain]
    specs = [x_spec] * tp + [anywhere] * len(weights)
    specs += [pl.BlockSpec((DV, 1), lambda i, s: (0, 0)), pl.BlockSpec((1, DV), lambda i, s: (0, 0))]
    alias = {}
    if buf is not None:
        ins.append(buf)
        specs.append(anywhere)
        alias = {len(ins): 0}
    return pl.pallas_call(
        functools.partial(attend_kernel, tp, moves, len(weights), buf is not None),
        out_shape=jax.ShapeDtypeStruct((MERGE, blocks, per, DV), BF),
        grid_spec=pltpu.PrefetchScalarGridSpec(
            num_scalar_prefetch=1,
            grid=(nb,),
            in_specs=specs,
            out_specs=pl.BlockSpec((MERGE, 1, per, DV), lambda i, s: (0, s[2 + i], 0, 0)),
            scratch_shapes=[
                pltpu.VMEM((4 * DV, DV), BF),
                pltpu.VMEM((DV, cols), BF),
                pltpu.VMEM((DV, cols), BF),
                pltpu.VMEM((2, 3 * DV // tp, cols), BF),
                pltpu.VMEM((DV, cols), BF),
                pltpu.VMEM((cols, DV), BF),
                pltpu.SemaphoreType.DMA((count,)),
            ],
        ),
        input_output_aliases=alias,
        compiler_params=pltpu.CompilerParams(
            vmem_limit_bytes=48 * MIB, dimension_semantics=("arbitrary",)
        ),
        cost_estimate=pl.CostEstimate(
            flops=nb * cols * DV * DV * 10,
            bytes_accessed=14 * MIB,
            transcendentals=nb * cols * cols * HV,
        ),
        name="attend",
    )(info, *ins)


def project_kernel(moves, position, nw, info, *refs):
    merged = refs[0]
    w_refs = refs[1 : 1 + nw]
    w_cache, llm_gain, out = refs[1 + nw : 4 + nw]
    held, slots, cache, acc, scaled, held_sem, slot_sem, cache_sem = refs[4 + nw :]
    units = scaled.shape[1]
    half = units // 2
    rows = held.shape[1]
    depth = slots.shape[0]
    width = min(1024, half)
    chunks = [(h, i) for h in range(2) for i in range(MERGE)]

    def bring(n):
        return moves(info, w_refs, *chunks[n], slots.at[n % depth], slot_sem.at[n % depth])

    def bring_merged(i):
        c = position(info, i)
        return pltpu.make_async_copy(merged.at[c], held.at[c], held_sem.at[i])

    load_cache = pltpu.make_async_copy(w_cache, cache, cache_sem)
    for n in range(depth):
        bring_merged(n).start()
        for copy in bring(n):
            copy.start()
    for n in range(depth, MERGE):
        bring_merged(n).start()
    load_cache.start()
    total = jnp.zeros((rows, 1), F32)
    for n, (h, i) in enumerate(chunks):
        c = position(info, i)
        if h == 0:
            bring_merged(i).wait()
        for copy in bring(n):
            copy.wait()
        slot = n % depth

        def tile(j, carry):
            spot = pl.ds(pl.multiple_of(j * width, width), width)
            d = jnp.dot(held[c], slots[slot, :, spot], preferred_element_type=F32)
            if i == 0:
                acc[:, spot] = d
            else:
                acc[:, spot] += d
            return carry

        lax.fori_loop(0, half // width, tile, 0)
        if n + depth < len(chunks):
            for copy in bring(n + depth):
                copy.start()
        if i == MERGE - 1:
            hidden = acc[...].astype(BF).astype(F32)
            total = total + jnp.sum(hidden * hidden, axis=1, keepdims=True)
            part = slice(h * half, (h + 1) * half)
            scaled[:, part] = (hidden * llm_gain[:, part]).astype(BF)
    load_cache.wait()
    kvw = cache.shape[1]

    def kv_tile(j, carry):
        spot = pl.ds(pl.multiple_of(j * 256, 256), 256)
        out[:, spot] = jnp.dot(scaled[...], cache[:, spot], preferred_element_type=F32).astype(BF)
        return carry

    lax.fori_loop(0, kvw // 256, kv_tile, 0)
    out[:, kvw:] = jnp.broadcast_to(total, (rows, 128)).astype(BF)


def project(info, merged, weights, moves, position, w_cache, llm_gain):
    units, kvw = w_cache.shape
    rows = merged.shape[1] * merged.shape[2]
    anywhere = pl.BlockSpec(memory_space=pl.ANY)
    return pl.pallas_call(
        functools.partial(project_kernel, moves, position, len(weights)),
        out_shape=jax.ShapeDtypeStruct((rows, kvw + 128), BF),
        grid_spec=pltpu.PrefetchScalarGridSpec(
            num_scalar_prefetch=1,
            grid=(1,),
            in_specs=[anywhere] * (len(weights) + 2)
            + [pl.BlockSpec((1, units), lambda i, s: (0, 0))],
            out_specs=pl.BlockSpec((rows, kvw + 128), lambda i, s: (0, 0)),
            scratch_shapes=[
                pltpu.VMEM((MERGE, rows, DV), BF),
                pltpu.VMEM((3, DV, units // 2), BF),
                pltpu.VMEM((units, kvw), BF),
                pltpu.VMEM((rows, units // 2), F32),
                pltpu.VMEM((rows, units), BF),
                pltpu.SemaphoreType.DMA((MERGE,)),
                pltpu.SemaphoreType.DMA((3, 4)),
                pltpu.SemaphoreType.DMA,
            ],
        ),
        compiler_params=pltpu.CompilerParams(
            vmem_limit_bytes=48 * MIB, dimension_semantics=("arbitrary",)
        ),
        cost_estimate=pl.CostEstimate(
            flops=2 * rows * units * (MERGE * DV + kvw),
            bytes_accessed=36 * MIB,
            transcendentals=0,
        ),
        name="project",
    )(info, merged.reshape(MERGE, rows, DV), *weights, w_cache, llm_gain)


def shards(
    patches, route, order, tiles, w_qkv, w_proj, vit_gain, merge_gain, w_merge, llm_gain, w_cache
):
    seq_count = lax.axis_size("seq")
    tp = lax.axis_size("tp")
    s = lax.axis_index("seq").astype(jnp.int32)
    t = lax.axis_index("tp").astype(jnp.int32)
    win_dev = order.shape[1]
    feats = patches.shape[1]
    per_peer = win_dev // seq_count
    tokens = WIN // MERGE
    blocks = win_dev // GROUP
    picks = order[0]
    tile_index = picks // TILE_WIN
    counts = jnp.take(tiles, tile_index // TILE_SLOTS)
    live = (tile_index % TILE_SLOTS < counts).astype(jnp.int32)
    arrange = jnp.argsort(route[:, 0], stable=True)
    live_send = jnp.take(live, arrange).reshape(seq_count, per_peer)
    window = jnp.take(picks, arrange).reshape(seq_count, per_peer)

    def xor(x, d):
        return lax.ppermute(x, "seq", [(i, i ^ d) for i in range(seq_count)])

    def tie(x, after):
        return lax.optimization_barrier((x, after))[0]

    def tp_xor(x, d):
        return lax.ppermute(x, "tp", [(i, i ^ d) for i in range(tp)])

    def spread(x):
        held = {0: x}
        d = tp // 2
        while d:
            held.update({k ^ d: tp_xor(v, d) for k, v in list(held.items())})
            d //= 2
        return [held[d] for d in range(tp)]

    paired = seq_count == 8 and per_peer == GROUP

    source = (
        window[:, :, None, None] * WIN
        + jnp.arange(tokens)[None, None, None, :] * MERGE
        + jnp.arange(MERGE)[None, None, :, None]
    ).reshape(-1)
    pick = (jnp.arange(patches.shape[0])[:, None] == source[None, :]).astype(BF)
    sent = lax.dot_general(
        patches, pick, (((0,), (0,)), ((), ())), preferred_element_type=F32
    ).astype(BF)
    alive = jnp.repeat(live_send.reshape(-1), WIN).astype(BF)
    sent = jnp.concatenate([sent, jnp.broadcast_to(alive, (16, alive.shape[0]))])
    step = per_peer * WIN
    wq_t = w_qkv.T

    full = lax.all_to_all(
        sent.reshape(feats + 16, seq_count, step).transpose(1, 0, 2),
        "seq",
        split_axis=0,
        concat_axis=0,
        tiled=True,
    )
    live_here = full[:, feats, ::WIN]
    full = full[:, :feats].reshape(blocks, GROUP // per_peer, feats, step)
    full = full.transpose(0, 2, 1, 3).reshape(blocks, feats, GROUP * WIN)
    mid = blocks // 2

    if paired:
        share = (wq_t.shape[0] + w_proj.shape[0]) // seq_count
        q_parts = wq_t.shape[0] // share
        mine = jnp.where(
            s < q_parts,
            lax.dynamic_slice_in_dim(wq_t, jnp.minimum(s, q_parts - 1) * share, share),
            lax.dynamic_slice_in_dim(w_proj, jnp.maximum(s - q_parts, 0) * share, share),
        )
        def sides(x):
            return lax.optimization_barrier((xor(x, 2), xor(x, 4)))

        def corners(by_x, by_y):
            half = by_x.shape[0] // 2
            return xor(by_x[:half], 4), xor(by_y[half:], 2)

        def with_cores(pieces):
            return list(pieces) + [xor(v, 1) for v in pieces]

        def parts(rows):
            half = rows // 2
            own = [(0, 0, rows), (2, 0, rows), (4, 0, rows), (6, 0, half), (6, half, rows)]
            return own + [(d ^ 1, lo, hi) for d, lo, hi in own]

        def sides_of_tp(x):
            return lax.optimization_barrier((tp_xor(x, 1), tp_xor(x, 2)))

        quarter = w_merge.shape[0] // 4
        early = xor(w_merge[:quarter], 2), xor(w_merge[:quarter], 4)
        (by1, by2), early = lax.optimization_barrier((sides_of_tp(mine), early))
        others = jnp.concatenate([by1, by2, tp_xor(by2, 1)])
        vit_sides = sides(tie(others, full))
        near = sides_of_tp(full[:mid])
        vit_sides, near, rest = lax.optimization_barrier((vit_sides, near, w_merge[quarter:]))
        far = tp_xor(near[1], 1)
        far, vit_corners = lax.optimization_barrier((far, corners(*vit_sides)))
        vit_weights = [wq_t, w_proj] + with_cores([jnp.concatenate([others, *vit_sides, *vit_corners])])
        merge_sides = sides(rest)
        q_rows, p_rows = wq_t.shape[0], w_proj.shape[0]
        vit_parts = []
        for n, (d, lo, hi) in enumerate(parts(others.shape[0])):
            base = sum(last - first for _, first, last in parts(others.shape[0])[n // 5 * 5 : n])
            for j in range(1, tp):
                top, end = max(lo, (j - 1) * share), min(hi, j * share)
                if top < end:
                    vit_parts.append(
                        (2 + n // 5, d, j, base + top - lo, top - (j - 1) * share, end - top)
                    )
        vit_count = 2 + len(vit_parts)

        def vit_moves(info, refs, w, sem):
            t, s = info[0], info[1]
            copies = [[] for _ in range(tp)]
            copies[0] = [
                pltpu.make_async_copy(
                    refs[0], w.at[pl.ds(pl.multiple_of(t * q_rows, 16), q_rows)], sem.at[0]
                ),
                pltpu.make_async_copy(
                    refs[1], w.at[pl.ds(pl.multiple_of(3 * DV + t * p_rows, 16), p_rows)], sem.at[1]
                ),
            ]
            for at, (n, d, j, source, offset, count) in enumerate(vit_parts):
                part = s ^ d
                q = t ^ j
                row = offset + jnp.where(
                    part < q_parts,
                    q * q_rows + part * share,
                    3 * DV + q * p_rows + (part - q_parts) * share,
                )
                copies[j].append(
                    pltpu.make_async_copy(
                        refs[n].at[source : source + count],
                        w.at[pl.ds(pl.multiple_of(row, 16), count)],
                        sem.at[2 + at],
                    )
                )
            return copies

        def merge_moves(info, refs, h, i, slot, sem):
            s = info[1]
            wide = slot.shape[1]
            rows = slot.shape[0] // 2
            copies = []
            for n, (d, lo, hi) in enumerate(parts(rows)):
                if d // 2 == i:
                    spot = pl.ds(pl.multiple_of(((s ^ d) & 1) * rows + lo, 16), hi - lo)
                    part = refs[n].at[:, h * wide : (h + 1) * wide]
                    copies.append(pltpu.make_async_copy(part, slot.at[spot], sem.at[len(copies)]))
            return copies

        def position(info, i):
            return (info[1] // 2) ^ i

    else:
        vit_weights = [
            lax.all_gather(wq_t, "tp", axis=0, tiled=True),
            lax.all_gather(w_proj, "tp", axis=0, tiled=True),
        ]
        merge_weights = [lax.all_gather(w_merge, "seq", axis=0, tiled=True)]
        vit_count = 2 * tp
        q_rows, p_rows = wq_t.shape[0], w_proj.shape[0]

        def vit_moves(info, refs, w, sem):
            copies = []
            for d in range(tp):
                g = info[0] ^ d
                q_part = pl.ds(pl.multiple_of(g * q_rows, 16), q_rows)
                p_part = pl.ds(pl.multiple_of(g * p_rows, 16), p_rows)
                p_spot = pl.ds(pl.multiple_of(3 * DV + g * p_rows, 16), p_rows)
                copies.append(
                    [
                        pltpu.make_async_copy(refs[0].at[q_part], w.at[q_part], sem.at[2 * d]),
                        pltpu.make_async_copy(refs[1].at[p_part], w.at[p_spot], sem.at[2 * d + 1]),
                    ]
                )
            return copies

        def merge_moves(info, refs, h, i, slot, sem):
            wide = slot.shape[1]
            part = refs[0].at[i * DV : (i + 1) * DV, h * wide : (h + 1) * wide]
            return [pltpu.make_async_copy(part, slot, sem.at[0])]

        def position(info, i):
            return i

    def encode(first, pieces, buf):
        count = pieces[0].shape[0]
        info = jnp.concatenate([jnp.stack([t, s]), first + jnp.arange(count, dtype=jnp.int32)])
        return attend(
            tp, info, pieces, vit_weights, vit_moves, vit_count,
            vit_gain[:, None], merge_gain[None, :], blocks, buf,
        )

    merged = None
    if paired:
        by1, by2 = near
        own = tie(full[mid:], (far, vit_weights[2:]))
        merged = encode(0, [full[:mid], by1, by2, far], None)
        by1, by2 = sides_of_tp(own)
        merged, by2 = lax.optimization_barrier((merged, by2))
        merge_sides = [jnp.concatenate(pair) for pair in zip(early, merge_sides)]
        merge_corners = corners(*merge_sides)
        far, merge_sides = lax.optimization_barrier((tp_xor(by2, 1), merge_sides))
        merged = encode(mid, [full[mid:], by1, by2, far], merged)
        merged, merge_corners = lax.optimization_barrier((merged, merge_corners))
        merge_weights = with_cores([w_merge, *merge_sides, *merge_corners])
    else:
        for first in (0, mid):
            merged = encode(first, spread(full[first : first + mid]), merged)
    partial_value = project(
        jnp.stack([t, s]), merged, merge_weights, merge_moves, position, w_cache, llm_gain[None, :]
    )
    summed = lax.psum_scatter(partial_value, "tp", scatter_dimension=0, tiled=True).astype(F32)
    kvw = w_cache.shape[1]
    cache, total_squares = summed[:, :kvw], summed[:, kvw : kvw + 1]
    share = cache.shape[0]
    live_tokens = jnp.repeat(live_here.reshape(-1), tokens)
    mine = lax.dynamic_slice_in_dim(live_tokens, t * share, share).astype(F32)
    return (cache * lax.rsqrt(total_squares / D + 1e-6) * mine[:, None]).astype(BF)


def solution(mesh):
    return jax.shard_map(
        shards,
        mesh=mesh,
        in_specs=(
            P("seq", "tp"),
            P("seq", None),
            P("seq", None),
            P("seq"),
            P(None, "tp"),
            P("tp", None),
            P(),
            P(),
            P("seq", "tp"),
            P("tp"),
            P("tp", None),
        ),
        out_specs=P(("seq", "tp"), None),
        check_vma=False,
    )
```

```python
import functools

import jax
import jax.numpy as jnp
from jax import lax
from jax.experimental import pallas as pl
from jax.experimental.pallas import tpu as pltpu
from jax.sharding import PartitionSpec as P

DV = 1280
HV = 16
HS = DV // HV
D = 8192
WIN = 64
MERGE = 4
TILE_WIN = 4
TILE_SLOTS = 4
GROUP = 4
F32 = jnp.float32
BF = jnp.bfloat16
MIB = 1024 * 1024


def attend_kernel(tp, moves, nw, aliased, info, *refs):
    pieces = refs[:tp]
    at = tp
    w_refs = refs[at : at + nw]
    vit_gain, merge_gain = refs[at + nw : at + nw + 2]
    at += nw + 2 + int(aliased)
    out = refs[at]
    w, xs, nrm, packed, mixed, vit, sem = refs[at + 1 :]
    t = info[0]
    heads = HV // tp
    rows = packed.shape[1]
    feats = pieces[0].shape[1]
    first_proj = 3 * DV
    cols = xs.shape[1]
    step = pl.program_id(0)

    @pl.when(step == 0)
    def _():
        for part in moves(info, w_refs, w, sem):
            for copy in part:
                copy.start()

    for d, piece in enumerate(pieces):
        xs[pl.ds(pl.multiple_of((t ^ d) * feats, feats), feats), :] = piece[0]

    xf = xs[...].astype(F32)
    scale = lax.rsqrt(jnp.mean(xf * xf, axis=0, keepdims=True) + 1e-6)
    nrm[...] = (xf * scale * vit_gain[...]).astype(BF)

    pair = 2 * WIN
    first = lax.broadcasted_iota(jnp.int32, (WIN, pair), 1) < WIN
    fold = (HS**-0.5) * 1.4426950408889634

    none = jnp.zeros((pair, pair), BF)

    def arrived(d):
        @pl.when(step == 0)
        def _():
            for copy in moves(info, w_refs, w, sem)[d]:
                copy.wait()

    def pack(d, slot):
        mine = w[pl.ds(pl.multiple_of((t ^ d) * rows, rows), rows), :]
        packed[slot] = jnp.dot(mine, nrm[...], preferred_element_type=F32).astype(BF)

    def heads_of(d, more):
        slot = lax.rem(d, 2)
        now = packed.at[slot]
        scores = []
        for h in range(heads):
            q, k = (now[(3 * h + n) * HS : (3 * h + n + 1) * HS, :] for n in range(2))
            s = lax.dot_general(k, q, (((0,), (0,)), ((), ())), preferred_element_type=F32)
            for n in range(cols // pair):
                at = n * pair
                s0, s1 = s[at : at + WIN, at : at + pair], s[at + WIN : at + pair, at : at + pair]
                scores.append(jnp.where(first, s0, s1) * fold)
        if more:
            pack(d + 1, 1 - slot)
        probs = []
        for s in scores:
            p = jnp.exp2(s - jnp.max(s, axis=0, keepdims=True))
            p = p * (1.0 / jnp.sum(p, axis=0, keepdims=True))
            probs.append(
                jnp.concatenate([jnp.where(first, p, 0.0), jnp.where(first, 0.0, p)]).astype(BF)
            )
        for h in range(heads):
            v = now[(3 * h + 2) * HS : (3 * h + 3) * HS, :]
            p = jnp.concatenate(
                [
                    jnp.concatenate([probs[2 * h], none], axis=1),
                    jnp.concatenate([none, probs[2 * h + 1]], axis=1),
                ]
            )
            m = jnp.dot(v, p, preferred_element_type=F32)
            at = pl.multiple_of((t ^ d) * heads * HS, heads * HS) + h * HS
            mixed[pl.ds(at, HS), :] = m.astype(BF)

    def one(d, carry):
        for later in range(1, tp):
            pl.when(d + 1 == later)(functools.partial(arrived, later))
        heads_of(d, True)
        return carry

    arrived(0)
    pack(0, 0)
    lax.fori_loop(0, tp - 1, one, 0)
    heads_of(jnp.int32(tp - 1), False)

    width = 256
    sums = jnp.zeros((cols, 1), F32)
    for n in range(DV // width):
        part = slice(n * width, (n + 1) * width)
        proj = lax.dot_general(
            mixed[...],
            w[first_proj : first_proj + DV, part],
            (((0,), (0,)), ((), ())),
            preferred_element_type=F32,
        )
        y = (xs[part, :].T.astype(F32) + proj).astype(BF)
        vit[:, part] = y
        yf = y.astype(F32)
        sums = sums + jnp.sum(yf * yf, axis=1, keepdims=True)
    scale = lax.rsqrt(sums * (1.0 / DV) + 1e-6)
    merged = (vit[...].astype(F32) * scale * merge_gain[...]).astype(BF)
    per = WIN // MERGE
    for w_at in range(cols // WIN):
        for c in range(MERGE):
            at = w_at * WIN + c * per
            out[c, 0, w_at * per : (w_at + 1) * per] = merged[at : at + per, :]


def attend(tp, info, pieces, weights, moves, count, vit_gain, merge_gain, blocks, buf):
    nb, feats, cols = pieces[0].shape
    per = cols // MERGE
    x_spec = pl.BlockSpec((1, feats, cols), lambda i, s: (i, 0, 0))
    anywhere = pl.BlockSpec(memory_space=pl.ANY)
    ins = [*pieces, *weights, vit_gain, merge_gain]
    specs = [x_spec] * tp + [anywhere] * len(weights)
    specs += [pl.BlockSpec((DV, 1), lambda i, s: (0, 0)), pl.BlockSpec((1, DV), lambda i, s: (0, 0))]
    alias = {}
    if buf is not None:
        ins.append(buf)
        specs.append(anywhere)
        alias = {len(ins): 0}
    return pl.pallas_call(
        functools.partial(attend_kernel, tp, moves, len(weights), buf is not None),
        out_shape=jax.ShapeDtypeStruct((MERGE, blocks, per, DV), BF),
        grid_spec=pltpu.PrefetchScalarGridSpec(
            num_scalar_prefetch=1,
            grid=(nb,),
            in_specs=specs,
            out_specs=pl.BlockSpec((MERGE, 1, per, DV), lambda i, s: (0, s[2 + i], 0, 0)),
            scratch_shapes=[
                pltpu.VMEM((4 * DV, DV), BF),
                pltpu.VMEM((DV, cols), BF),
                pltpu.VMEM((DV, cols), BF),
                pltpu.VMEM((2, 3 * DV // tp, cols), BF),
                pltpu.VMEM((DV, cols), BF),
                pltpu.VMEM((cols, DV), BF),
                pltpu.SemaphoreType.DMA((count,)),
            ],
        ),
        input_output_aliases=alias,
        compiler_params=pltpu.CompilerParams(
            vmem_limit_bytes=48 * MIB, dimension_semantics=("arbitrary",)
        ),
        cost_estimate=pl.CostEstimate(
            flops=nb * cols * DV * DV * 10,
            bytes_accessed=14 * MIB,
            transcendentals=nb * cols * cols * HV,
        ),
        name="attend",
    )(info, *ins)


def project_kernel(moves, position, nw, info, *refs):
    merged = refs[0]
    w_refs = refs[1 : 1 + nw]
    w_cache, llm_gain, out = refs[1 + nw : 4 + nw]
    held, slots, cache, acc, scaled, held_sem, slot_sem, cache_sem = refs[4 + nw :]
    units = scaled.shape[1]
    half = units // 2
    rows = held.shape[1]
    depth = slots.shape[0]
    width = min(1024, half)
    chunks = [(h, i) for h in range(2) for i in range(MERGE)]

    def bring(n):
        return moves(info, w_refs, *chunks[n], slots.at[n % depth], slot_sem.at[n % depth])

    def bring_merged(i):
        c = position(info, i)
        return pltpu.make_async_copy(merged.at[c], held.at[c], held_sem.at[i])

    load_cache = pltpu.make_async_copy(w_cache, cache, cache_sem)
    for n in range(depth):
        bring_merged(n).start()
        for copy in bring(n):
            copy.start()
    for n in range(depth, MERGE):
        bring_merged(n).start()
    load_cache.start()
    total = jnp.zeros((rows, 1), F32)
    for n, (h, i) in enumerate(chunks):
        c = position(info, i)
        if h == 0:
            bring_merged(i).wait()
        for copy in bring(n):
            copy.wait()
        slot = n % depth

        def tile(j, carry):
            spot = pl.ds(pl.multiple_of(j * width, width), width)
            d = jnp.dot(held[c], slots[slot, :, spot], preferred_element_type=F32)
            if i == 0:
                acc[:, spot] = d
            else:
                acc[:, spot] += d
            return carry

        lax.fori_loop(0, half // width, tile, 0)
        if n + depth < len(chunks):
            for copy in bring(n + depth):
                copy.start()
        if i == MERGE - 1:
            hidden = acc[...].astype(BF).astype(F32)
            total = total + jnp.sum(hidden * hidden, axis=1, keepdims=True)
            part = slice(h * half, (h + 1) * half)
            scaled[:, part] = (hidden * llm_gain[:, part]).astype(BF)
    load_cache.wait()
    kvw = cache.shape[1]

    span = min(1024, kvw)

    def kv_tile(j, carry):
        spot = pl.ds(pl.multiple_of(j * span, span), span)
        out[:, spot] = jnp.dot(scaled[...], cache[:, spot], preferred_element_type=F32).astype(BF)
        return carry

    lax.fori_loop(0, kvw // span, kv_tile, 0)
    out[:, kvw:] = jnp.broadcast_to(total, (rows, 128)).astype(BF)


def project(info, merged, weights, moves, position, w_cache, llm_gain):
    units, kvw = w_cache.shape
    rows = merged.shape[1] * merged.shape[2]
    anywhere = pl.BlockSpec(memory_space=pl.ANY)
    return pl.pallas_call(
        functools.partial(project_kernel, moves, position, len(weights)),
        out_shape=jax.ShapeDtypeStruct((rows, kvw + 128), BF),
        grid_spec=pltpu.PrefetchScalarGridSpec(
            num_scalar_prefetch=1,
            grid=(1,),
            in_specs=[anywhere] * (len(weights) + 2)
            + [pl.BlockSpec((1, units), lambda i, s: (0, 0))],
            out_specs=pl.BlockSpec((rows, kvw + 128), lambda i, s: (0, 0)),
            scratch_shapes=[
                pltpu.VMEM((MERGE, rows, DV), BF),
                pltpu.VMEM((3, DV, units // 2), BF),
                pltpu.VMEM((units, kvw), BF),
                pltpu.VMEM((rows, units // 2), F32),
                pltpu.VMEM((rows, units), BF),
                pltpu.SemaphoreType.DMA((MERGE,)),
                pltpu.SemaphoreType.DMA((3, 4)),
                pltpu.SemaphoreType.DMA,
            ],
        ),
        compiler_params=pltpu.CompilerParams(
            vmem_limit_bytes=48 * MIB, dimension_semantics=("arbitrary",)
        ),
        cost_estimate=pl.CostEstimate(
            flops=2 * rows * units * (MERGE * DV + kvw),
            bytes_accessed=36 * MIB,
            transcendentals=0,
        ),
        name="project",
    )(info, merged.reshape(MERGE, rows, DV), *weights, w_cache, llm_gain)


def shards(
    patches, route, order, tiles, w_qkv, w_proj, vit_gain, merge_gain, w_merge, llm_gain, w_cache
):
    seq_count = lax.axis_size("seq")
    tp = lax.axis_size("tp")
    s = lax.axis_index("seq").astype(jnp.int32)
    t = lax.axis_index("tp").astype(jnp.int32)
    win_dev = order.shape[1]
    feats = patches.shape[1]
    per_peer = win_dev // seq_count
    tokens = WIN // MERGE
    blocks = win_dev // GROUP
    picks = order[0]
    tile_index = picks // TILE_WIN
    counts = jnp.take(tiles, tile_index // TILE_SLOTS)
    live = (tile_index % TILE_SLOTS < counts).astype(jnp.int32)
    arrange = jnp.argsort(route[:, 0], stable=True)
    live_send = jnp.take(live, arrange).reshape(seq_count, per_peer)
    window = jnp.take(picks, arrange).reshape(seq_count, per_peer)

    def xor(x, d):
        return lax.ppermute(x, "seq", [(i, i ^ d) for i in range(seq_count)])

    def tie(x, after):
        return lax.optimization_barrier((x, after))[0]

    def tp_xor(x, d):
        return lax.ppermute(x, "tp", [(i, i ^ d) for i in range(tp)])

    def spread(x):
        held = {0: x}
        d = tp // 2
        while d:
            held.update({k ^ d: tp_xor(v, d) for k, v in list(held.items())})
            d //= 2
        return [held[d] for d in range(tp)]

    paired = seq_count == 8 and per_peer == GROUP

    source = (
        window[:, :, None, None] * WIN
        + jnp.arange(tokens)[None, None, None, :] * MERGE
        + jnp.arange(MERGE)[None, None, :, None]
    ).reshape(-1)
    pick = (jnp.arange(patches.shape[0])[:, None] == source[None, :]).astype(BF)
    sent = lax.dot_general(
        patches, pick, (((0,), (0,)), ((), ())), preferred_element_type=F32
    ).astype(BF)
    alive = jnp.repeat(live_send.reshape(-1), WIN).astype(BF)
    sent = jnp.concatenate([sent, jnp.broadcast_to(alive, (16, alive.shape[0]))])
    step = per_peer * WIN
    wq_t = w_qkv.T

    full = lax.all_to_all(
        sent.reshape(feats + 16, seq_count, step).transpose(1, 0, 2),
        "seq",
        split_axis=0,
        concat_axis=0,
        tiled=True,
    )
    live_here = full[:, feats, ::WIN]
    full = full[:, :feats].reshape(blocks, GROUP // per_peer, feats, step)
    full = full.transpose(0, 2, 1, 3).reshape(blocks, feats, GROUP * WIN)
    mid = blocks // 2

    if paired:
        share = (wq_t.shape[0] + w_proj.shape[0]) // seq_count
        q_parts = wq_t.shape[0] // share
        mine = jnp.where(
            s < q_parts,
            lax.dynamic_slice_in_dim(wq_t, jnp.minimum(s, q_parts - 1) * share, share),
            lax.dynamic_slice_in_dim(w_proj, jnp.maximum(s - q_parts, 0) * share, share),
        )
        def sides(x):
            return lax.optimization_barrier((xor(x, 2), xor(x, 4)))

        def corners(by_x, by_y):
            half = by_x.shape[0] // 2
            return xor(by_x[:half], 4), xor(by_y[half:], 2)

        def with_cores(pieces):
            return list(pieces) + [xor(v, 1) for v in pieces]

        def parts(rows):
            half = rows // 2
            own = [(0, 0, rows), (2, 0, rows), (4, 0, rows), (6, 0, half), (6, half, rows)]
            return own + [(d ^ 1, lo, hi) for d, lo, hi in own]

        def sides_of_tp(x):
            return lax.optimization_barrier((tp_xor(x, 1), tp_xor(x, 2)))

        quarter = w_merge.shape[0] // 4
        early = xor(w_merge[:quarter], 2), xor(w_merge[:quarter], 4)
        (by1, by2), early = lax.optimization_barrier((sides_of_tp(mine), early))
        others = jnp.concatenate([by1, by2, tp_xor(by2, 1)])
        vit_sides = sides(tie(others, full))
        near = sides_of_tp(full[:mid])
        vit_sides, near, rest = lax.optimization_barrier((vit_sides, near, w_merge[quarter:]))
        far = tp_xor(near[1], 1)
        far, vit_corners = lax.optimization_barrier((far, corners(*vit_sides)))
        vit_weights = [wq_t, w_proj] + with_cores([jnp.concatenate([others, *vit_sides, *vit_corners])])
        merge_sides = sides(rest)
        q_rows, p_rows = wq_t.shape[0], w_proj.shape[0]
        vit_parts = []
        for n, (d, lo, hi) in enumerate(parts(others.shape[0])):
            base = sum(last - first for _, first, last in parts(others.shape[0])[n // 5 * 5 : n])
            for j in range(1, tp):
                top, end = max(lo, (j - 1) * share), min(hi, j * share)
                if top < end:
                    vit_parts.append(
                        (2 + n // 5, d, j, base + top - lo, top - (j - 1) * share, end - top)
                    )
        vit_count = 2 + len(vit_parts)

        def vit_moves(info, refs, w, sem):
            t, s = info[0], info[1]
            copies = [[] for _ in range(tp)]
            copies[0] = [
                pltpu.make_async_copy(
                    refs[0], w.at[pl.ds(pl.multiple_of(t * q_rows, 16), q_rows)], sem.at[0]
                ),
                pltpu.make_async_copy(
                    refs[1], w.at[pl.ds(pl.multiple_of(3 * DV + t * p_rows, 16), p_rows)], sem.at[1]
                ),
            ]
            for at, (n, d, j, source, offset, count) in enumerate(vit_parts):
                part = s ^ d
                q = t ^ j
                row = offset + jnp.where(
                    part < q_parts,
                    q * q_rows + part * share,
                    3 * DV + q * p_rows + (part - q_parts) * share,
                )
                copies[j].append(
                    pltpu.make_async_copy(
                        refs[n].at[source : source + count],
                        w.at[pl.ds(pl.multiple_of(row, 16), count)],
                        sem.at[2 + at],
                    )
                )
            return copies

        def merge_moves(info, refs, h, i, slot, sem):
            s = info[1]
            wide = slot.shape[1]
            rows = slot.shape[0] // 2
            copies = []
            for n, (d, lo, hi) in enumerate(parts(rows)):
                if d // 2 == i:
                    spot = pl.ds(pl.multiple_of(((s ^ d) & 1) * rows + lo, 16), hi - lo)
                    part = refs[n].at[:, h * wide : (h + 1) * wide]
                    copies.append(pltpu.make_async_copy(part, slot.at[spot], sem.at[len(copies)]))
            return copies

        def position(info, i):
            return (info[1] // 2) ^ i

    else:
        vit_weights = [
            lax.all_gather(wq_t, "tp", axis=0, tiled=True),
            lax.all_gather(w_proj, "tp", axis=0, tiled=True),
        ]
        merge_weights = [lax.all_gather(w_merge, "seq", axis=0, tiled=True)]
        vit_count = 2 * tp
        q_rows, p_rows = wq_t.shape[0], w_proj.shape[0]

        def vit_moves(info, refs, w, sem):
            copies = []
            for d in range(tp):
                g = info[0] ^ d
                q_part = pl.ds(pl.multiple_of(g * q_rows, 16), q_rows)
                p_part = pl.ds(pl.multiple_of(g * p_rows, 16), p_rows)
                p_spot = pl.ds(pl.multiple_of(3 * DV + g * p_rows, 16), p_rows)
                copies.append(
                    [
                        pltpu.make_async_copy(refs[0].at[q_part], w.at[q_part], sem.at[2 * d]),
                        pltpu.make_async_copy(refs[1].at[p_part], w.at[p_spot], sem.at[2 * d + 1]),
                    ]
                )
            return copies

        def merge_moves(info, refs, h, i, slot, sem):
            wide = slot.shape[1]
            part = refs[0].at[i * DV : (i + 1) * DV, h * wide : (h + 1) * wide]
            return [pltpu.make_async_copy(part, slot, sem.at[0])]

        def position(info, i):
            return i

    def encode(first, pieces, buf):
        count = pieces[0].shape[0]
        info = jnp.concatenate([jnp.stack([t, s]), first + jnp.arange(count, dtype=jnp.int32)])
        return attend(
            tp, info, pieces, vit_weights, vit_moves, vit_count,
            vit_gain[:, None], merge_gain[None, :], blocks, buf,
        )

    merged = None
    if paired:
        by1, by2 = near
        own = tie(full[mid:], (far, vit_weights[2:]))
        merged = encode(0, [full[:mid], by1, by2, far], None)
        by1, by2 = sides_of_tp(own)
        merged, by2 = lax.optimization_barrier((merged, by2))
        merge_sides = [jnp.concatenate(pair) for pair in zip(early, merge_sides)]
        merge_corners = corners(*merge_sides)
        far, merge_sides = lax.optimization_barrier((tp_xor(by2, 1), merge_sides))
        merged = encode(mid, [full[mid:], by1, by2, far], merged)
        merged, merge_corners = lax.optimization_barrier((merged, merge_corners))
        merge_weights = with_cores([w_merge, *merge_sides, *merge_corners])
    else:
        for first in (0, mid):
            merged = encode(first, spread(full[first : first + mid]), merged)
    partial_value = project(
        jnp.stack([t, s]), merged, merge_weights, merge_moves, position, w_cache, llm_gain[None, :]
    )
    summed = lax.psum_scatter(partial_value, "tp", scatter_dimension=0, tiled=True).astype(F32)
    kvw = w_cache.shape[1]
    cache, total_squares = summed[:, :kvw], summed[:, kvw : kvw + 1]
    share = cache.shape[0]
    live_tokens = jnp.repeat(live_here.reshape(-1), tokens)
    mine = lax.dynamic_slice_in_dim(live_tokens, t * share, share).astype(F32)
    return (cache * lax.rsqrt(total_squares / D + 1e-6) * mine[:, None]).astype(BF)


def solution(mesh):
    return jax.shard_map(
        shards,
        mesh=mesh,
        in_specs=(
            P("seq", "tp"),
            P("seq", None),
            P("seq", None),
            P("seq"),
            P(None, "tp"),
            P("tp", None),
            P(),
            P(),
            P("seq", "tp"),
            P("tp"),
            P("tp", None),
        ),
        out_specs=P(("seq", "tp"), None),
        check_vma=False,
    )
```

```python
import functools

import jax
import jax.numpy as jnp
from jax import lax
from jax.experimental import pallas as pl
from jax.experimental.pallas import tpu as pltpu
from jax.sharding import PartitionSpec as P

DV = 1280
HV = 16
HS = DV // HV
D = 8192
WIN = 64
MERGE = 4
TILE_WIN = 4
TILE_SLOTS = 4
GROUP = 4
F32 = jnp.float32
BF = jnp.bfloat16
MIB = 1024 * 1024


def attend_kernel(tp, moves, nw, aliased, info, *refs):
    pieces = refs[:tp]
    at = tp
    w_refs = refs[at : at + nw]
    vit_gain, merge_gain = refs[at + nw : at + nw + 2]
    at += nw + 2 + int(aliased)
    out = refs[at]
    w, xs, nrm, packed, mixed, vit, sem = refs[at + 1 :]
    t = info[0]
    heads = HV // tp
    rows = packed.shape[1]
    feats = pieces[0].shape[1]
    first_proj = 3 * DV
    cols = xs.shape[1]
    step = pl.program_id(0)

    @pl.when(step == 0)
    def _():
        for part in moves(info, w_refs, w, sem):
            for copy in part:
                copy.start()

    for d, piece in enumerate(pieces):
        xs[pl.ds(pl.multiple_of((t ^ d) * feats, feats), feats), :] = piece[0]

    xf = xs[...].astype(F32)
    scale = lax.rsqrt(jnp.mean(xf * xf, axis=0, keepdims=True) + 1e-6)
    nrm[...] = (xf * scale * vit_gain[...]).astype(BF)

    pair = 2 * WIN
    first = lax.broadcasted_iota(jnp.int32, (WIN, pair), 1) < WIN
    fold = (HS**-0.5) * 1.4426950408889634

    none = jnp.zeros((pair, pair), BF)

    def arrived(d):
        @pl.when(step == 0)
        def _():
            for copy in moves(info, w_refs, w, sem)[d]:
                copy.wait()

    def pack(d, slot):
        mine = w[pl.ds(pl.multiple_of((t ^ d) * rows, rows), rows), :]
        packed[slot] = jnp.dot(mine, nrm[...], preferred_element_type=F32).astype(BF)

    def heads_of(d, more):
        slot = lax.rem(d, 2)
        now = packed.at[slot]
        scores = []
        for h in range(heads):
            q, k = (now[(3 * h + n) * HS : (3 * h + n + 1) * HS, :] for n in range(2))
            s = lax.dot_general(k, q, (((0,), (0,)), ((), ())), preferred_element_type=F32)
            for n in range(cols // pair):
                at = n * pair
                s0, s1 = s[at : at + WIN, at : at + pair], s[at + WIN : at + pair, at : at + pair]
                scores.append(jnp.where(first, s0, s1) * fold)
        if more:
            pack(d + 1, 1 - slot)
        probs = []
        for s in scores:
            p = jnp.exp2(s - jnp.max(s, axis=0, keepdims=True))
            p = p * (1.0 / jnp.sum(p, axis=0, keepdims=True))
            probs.append(
                jnp.concatenate([jnp.where(first, p, 0.0), jnp.where(first, 0.0, p)]).astype(BF)
            )
        for h in range(heads):
            v = now[(3 * h + 2) * HS : (3 * h + 3) * HS, :]
            p = jnp.concatenate(
                [
                    jnp.concatenate([probs[2 * h], none], axis=1),
                    jnp.concatenate([none, probs[2 * h + 1]], axis=1),
                ]
            )
            m = jnp.dot(v, p, preferred_element_type=F32)
            at = pl.multiple_of((t ^ d) * heads * HS, heads * HS) + h * HS
            mixed[pl.ds(at, HS), :] = m.astype(BF)

    def one(d, carry):
        for later in range(1, tp):
            pl.when(d + 1 == later)(functools.partial(arrived, later))
        heads_of(d, True)
        return carry

    arrived(0)
    pack(0, 0)
    lax.fori_loop(0, tp - 1, one, 0)
    heads_of(jnp.int32(tp - 1), False)

    width = 256
    sums = jnp.zeros((cols, 1), F32)
    for n in range(DV // width):
        part = slice(n * width, (n + 1) * width)
        proj = lax.dot_general(
            mixed[...],
            w[first_proj : first_proj + DV, part],
            (((0,), (0,)), ((), ())),
            preferred_element_type=F32,
        )
        y = (xs[part, :].T.astype(F32) + proj).astype(BF)
        vit[:, part] = y
        yf = y.astype(F32)
        sums = sums + jnp.sum(yf * yf, axis=1, keepdims=True)
    scale = lax.rsqrt(sums * (1.0 / DV) + 1e-6)
    merged = (vit[...].astype(F32) * scale * merge_gain[...]).astype(BF)
    per = WIN // MERGE
    for w_at in range(cols // WIN):
        for c in range(MERGE):
            at = w_at * WIN + c * per
            out[c, 0, w_at * per : (w_at + 1) * per] = merged[at : at + per, :]


def attend(tp, info, pieces, weights, moves, count, vit_gain, merge_gain, blocks, buf):
    nb, feats, cols = pieces[0].shape
    per = cols // MERGE
    x_spec = pl.BlockSpec((1, feats, cols), lambda i, s: (i, 0, 0))
    anywhere = pl.BlockSpec(memory_space=pl.ANY)
    ins = [*pieces, *weights, vit_gain, merge_gain]
    specs = [x_spec] * tp + [anywhere] * len(weights)
    specs += [pl.BlockSpec((DV, 1), lambda i, s: (0, 0)), pl.BlockSpec((1, DV), lambda i, s: (0, 0))]
    alias = {}
    if buf is not None:
        ins.append(buf)
        specs.append(anywhere)
        alias = {len(ins): 0}
    return pl.pallas_call(
        functools.partial(attend_kernel, tp, moves, len(weights), buf is not None),
        out_shape=jax.ShapeDtypeStruct((MERGE, blocks, per, DV), BF),
        grid_spec=pltpu.PrefetchScalarGridSpec(
            num_scalar_prefetch=1,
            grid=(nb,),
            in_specs=specs,
            out_specs=pl.BlockSpec((MERGE, 1, per, DV), lambda i, s: (0, s[2 + i], 0, 0)),
            scratch_shapes=[
                pltpu.VMEM((4 * DV, DV), BF),
                pltpu.VMEM((DV, cols), BF),
                pltpu.VMEM((DV, cols), BF),
                pltpu.VMEM((2, 3 * DV // tp, cols), BF),
                pltpu.VMEM((DV, cols), BF),
                pltpu.VMEM((cols, DV), BF),
                pltpu.SemaphoreType.DMA((count,)),
            ],
        ),
        input_output_aliases=alias,
        compiler_params=pltpu.CompilerParams(
            vmem_limit_bytes=48 * MIB, dimension_semantics=("arbitrary",)
        ),
        cost_estimate=pl.CostEstimate(
            flops=nb * cols * DV * DV * 10,
            bytes_accessed=14 * MIB,
            transcendentals=nb * cols * cols * HV,
        ),
        name="attend",
    )(info, *ins)


def project_kernel(moves, position, nw, info, *refs):
    merged = refs[0]
    w_refs = refs[1 : 1 + nw]
    w_cache, llm_gain, out = refs[1 + nw : 4 + nw]
    held, slots, cache, acc, scaled, held_sem, slot_sem, cache_sem = refs[4 + nw :]
    units = scaled.shape[1]
    half = units // 2
    rows = held.shape[1]
    depth = slots.shape[0]
    width = min(1024, half)
    chunks = [(h, i) for h in range(2) for i in range(MERGE)]

    def bring(n):
        return moves(info, w_refs, *chunks[n], slots.at[n % depth], slot_sem.at[n % depth])

    def bring_merged(i):
        c = position(info, i)
        return pltpu.make_async_copy(merged.at[c], held.at[c], held_sem.at[i])

    load_cache = pltpu.make_async_copy(w_cache, cache, cache_sem)
    for n in range(depth):
        bring_merged(n).start()
        for copy in bring(n):
            copy.start()
    for n in range(depth, MERGE):
        bring_merged(n).start()
    load_cache.start()
    total = jnp.zeros((rows, 1), F32)
    for n, (h, i) in enumerate(chunks):
        c = position(info, i)
        if h == 0:
            bring_merged(i).wait()
        for copy in bring(n):
            copy.wait()
        slot = n % depth

        def tile(j, carry):
            spot = pl.ds(pl.multiple_of(j * width, width), width)
            d = jnp.dot(held[c], slots[slot, :, spot], preferred_element_type=F32)
            if i == 0:
                acc[:, spot] = d
            else:
                acc[:, spot] += d
            return carry

        lax.fori_loop(0, half // width, tile, 0)
        if n + depth < len(chunks):
            for copy in bring(n + depth):
                copy.start()
        if i == MERGE - 1:
            hidden = acc[...].astype(BF).astype(F32)
            total = total + jnp.sum(hidden * hidden, axis=1, keepdims=True)
            part = slice(h * half, (h + 1) * half)
            scaled[:, part] = (hidden * llm_gain[:, part]).astype(BF)
    load_cache.wait()
    kvw = cache.shape[1]

    span = min(1024, kvw)

    def kv_tile(j, carry):
        spot = pl.ds(pl.multiple_of(j * span, span), span)
        out[:, spot] = jnp.dot(scaled[...], cache[:, spot], preferred_element_type=F32).astype(BF)
        return carry

    lax.fori_loop(0, kvw // span, kv_tile, 0)
    out[:, kvw:] = jnp.broadcast_to(total, (rows, 128)).astype(BF)


def project(info, merged, weights, moves, position, w_cache, llm_gain):
    units, kvw = w_cache.shape
    rows = merged.shape[1] * merged.shape[2]
    anywhere = pl.BlockSpec(memory_space=pl.ANY)
    return pl.pallas_call(
        functools.partial(project_kernel, moves, position, len(weights)),
        out_shape=jax.ShapeDtypeStruct((rows, kvw + 128), BF),
        grid_spec=pltpu.PrefetchScalarGridSpec(
            num_scalar_prefetch=1,
            grid=(1,),
            in_specs=[anywhere] * (len(weights) + 2)
            + [pl.BlockSpec((1, units), lambda i, s: (0, 0))],
            out_specs=pl.BlockSpec((rows, kvw + 128), lambda i, s: (0, 0)),
            scratch_shapes=[
                pltpu.VMEM((MERGE, rows, DV), BF),
                pltpu.VMEM((4, DV, units // 2), BF),
                pltpu.VMEM((units, kvw), BF),
                pltpu.VMEM((rows, units // 2), F32),
                pltpu.VMEM((rows, units), BF),
                pltpu.SemaphoreType.DMA((MERGE,)),
                pltpu.SemaphoreType.DMA((4, 4)),
                pltpu.SemaphoreType.DMA,
            ],
        ),
        compiler_params=pltpu.CompilerParams(
            vmem_limit_bytes=48 * MIB, dimension_semantics=("arbitrary",)
        ),
        cost_estimate=pl.CostEstimate(
            flops=2 * rows * units * (MERGE * DV + kvw),
            bytes_accessed=36 * MIB,
            transcendentals=0,
        ),
        name="project",
    )(info, merged.reshape(MERGE, rows, DV), *weights, w_cache, llm_gain)


def shards(
    patches, route, order, tiles, w_qkv, w_proj, vit_gain, merge_gain, w_merge, llm_gain, w_cache
):
    seq_count = lax.axis_size("seq")
    tp = lax.axis_size("tp")
    s = lax.axis_index("seq").astype(jnp.int32)
    t = lax.axis_index("tp").astype(jnp.int32)
    win_dev = order.shape[1]
    feats = patches.shape[1]
    per_peer = win_dev // seq_count
    tokens = WIN // MERGE
    blocks = win_dev // GROUP
    picks = order[0]
    tile_index = picks // TILE_WIN
    counts = jnp.take(tiles, tile_index // TILE_SLOTS)
    live = (tile_index % TILE_SLOTS < counts).astype(jnp.int32)
    arrange = jnp.argsort(route[:, 0], stable=True)
    live_send = jnp.take(live, arrange).reshape(seq_count, per_peer)
    window = jnp.take(picks, arrange).reshape(seq_count, per_peer)

    def xor(x, d):
        return lax.ppermute(x, "seq", [(i, i ^ d) for i in range(seq_count)])

    def tie(x, after):
        return lax.optimization_barrier((x, after))[0]

    def tp_xor(x, d):
        return lax.ppermute(x, "tp", [(i, i ^ d) for i in range(tp)])

    def spread(x):
        held = {0: x}
        d = tp // 2
        while d:
            held.update({k ^ d: tp_xor(v, d) for k, v in list(held.items())})
            d //= 2
        return [held[d] for d in range(tp)]

    paired = seq_count == 8 and per_peer == GROUP

    source = (
        window[:, :, None, None] * WIN
        + jnp.arange(tokens)[None, None, None, :] * MERGE
        + jnp.arange(MERGE)[None, None, :, None]
    ).reshape(-1)
    pick = (jnp.arange(patches.shape[0])[:, None] == source[None, :]).astype(BF)
    sent = lax.dot_general(
        patches, pick, (((0,), (0,)), ((), ())), preferred_element_type=F32
    ).astype(BF)
    alive = jnp.repeat(live_send.reshape(-1), WIN).astype(BF)
    sent = jnp.concatenate([sent, jnp.broadcast_to(alive, (16, alive.shape[0]))])
    step = per_peer * WIN
    wq_t = w_qkv.T

    full = lax.all_to_all(
        sent.reshape(feats + 16, seq_count, step).transpose(1, 0, 2),
        "seq",
        split_axis=0,
        concat_axis=0,
        tiled=True,
    )
    live_here = full[:, feats, ::WIN]
    full = full[:, :feats].reshape(blocks, GROUP // per_peer, feats, step)
    full = full.transpose(0, 2, 1, 3).reshape(blocks, feats, GROUP * WIN)
    mid = blocks // 2

    if paired:
        share = (wq_t.shape[0] + w_proj.shape[0]) // seq_count
        q_parts = wq_t.shape[0] // share
        mine = jnp.where(
            s < q_parts,
            lax.dynamic_slice_in_dim(wq_t, jnp.minimum(s, q_parts - 1) * share, share),
            lax.dynamic_slice_in_dim(w_proj, jnp.maximum(s - q_parts, 0) * share, share),
        )
        def sides(x):
            return lax.optimization_barrier((xor(x, 2), xor(x, 4)))

        def corners(by_x, by_y):
            half = by_x.shape[0] // 2
            return xor(by_x[:half], 4), xor(by_y[half:], 2)

        def with_cores(pieces):
            return list(pieces) + [xor(v, 1) for v in pieces]

        def parts(rows):
            half = rows // 2
            own = [(0, 0, rows), (2, 0, rows), (4, 0, rows), (6, 0, half), (6, half, rows)]
            return own + [(d ^ 1, lo, hi) for d, lo, hi in own]

        def sides_of_tp(x):
            return lax.optimization_barrier((tp_xor(x, 1), tp_xor(x, 2)))

        quarter = w_merge.shape[0] // 4
        early = xor(w_merge[:quarter], 2), xor(w_merge[:quarter], 4)
        (by1, by2), early = lax.optimization_barrier((sides_of_tp(mine), early))
        others = jnp.concatenate([by1, by2, tp_xor(by2, 1)])
        vit_sides = sides(tie(others, full))
        near = sides_of_tp(full[:mid])
        vit_sides, near, rest = lax.optimization_barrier((vit_sides, near, w_merge[quarter:]))
        far = tp_xor(near[1], 1)
        far, vit_corners = lax.optimization_barrier((far, corners(*vit_sides)))
        vit_weights = [wq_t, w_proj] + with_cores([jnp.concatenate([others, *vit_sides, *vit_corners])])
        merge_sides = sides(rest)
        q_rows, p_rows = wq_t.shape[0], w_proj.shape[0]
        vit_parts = []
        for n, (d, lo, hi) in enumerate(parts(others.shape[0])):
            base = sum(last - first for _, first, last in parts(others.shape[0])[n // 5 * 5 : n])
            for j in range(1, tp):
                top, end = max(lo, (j - 1) * share), min(hi, j * share)
                if top < end:
                    vit_parts.append(
                        (2 + n // 5, d, j, base + top - lo, top - (j - 1) * share, end - top)
                    )
        vit_count = 2 + len(vit_parts)

        def vit_moves(info, refs, w, sem):
            t, s = info[0], info[1]
            copies = [[] for _ in range(tp)]
            copies[0] = [
                pltpu.make_async_copy(
                    refs[0], w.at[pl.ds(pl.multiple_of(t * q_rows, 16), q_rows)], sem.at[0]
                ),
                pltpu.make_async_copy(
                    refs[1], w.at[pl.ds(pl.multiple_of(3 * DV + t * p_rows, 16), p_rows)], sem.at[1]
                ),
            ]
            for at, (n, d, j, source, offset, count) in enumerate(vit_parts):
                part = s ^ d
                q = t ^ j
                row = offset + jnp.where(
                    part < q_parts,
                    q * q_rows + part * share,
                    3 * DV + q * p_rows + (part - q_parts) * share,
                )
                copies[j].append(
                    pltpu.make_async_copy(
                        refs[n].at[source : source + count],
                        w.at[pl.ds(pl.multiple_of(row, 16), count)],
                        sem.at[2 + at],
                    )
                )
            return copies

        def merge_moves(info, refs, h, i, slot, sem):
            s = info[1]
            wide = slot.shape[1]
            rows = slot.shape[0] // 2
            copies = []
            for n, (d, lo, hi) in enumerate(parts(rows)):
                if d // 2 == i:
                    spot = pl.ds(pl.multiple_of(((s ^ d) & 1) * rows + lo, 16), hi - lo)
                    part = refs[n].at[:, h * wide : (h + 1) * wide]
                    copies.append(pltpu.make_async_copy(part, slot.at[spot], sem.at[len(copies)]))
            return copies

        def position(info, i):
            return (info[1] // 2) ^ i

    else:
        vit_weights = [
            lax.all_gather(wq_t, "tp", axis=0, tiled=True),
            lax.all_gather(w_proj, "tp", axis=0, tiled=True),
        ]
        merge_weights = [lax.all_gather(w_merge, "seq", axis=0, tiled=True)]
        vit_count = 2 * tp
        q_rows, p_rows = wq_t.shape[0], w_proj.shape[0]

        def vit_moves(info, refs, w, sem):
            copies = []
            for d in range(tp):
                g = info[0] ^ d
                q_part = pl.ds(pl.multiple_of(g * q_rows, 16), q_rows)
                p_part = pl.ds(pl.multiple_of(g * p_rows, 16), p_rows)
                p_spot = pl.ds(pl.multiple_of(3 * DV + g * p_rows, 16), p_rows)
                copies.append(
                    [
                        pltpu.make_async_copy(refs[0].at[q_part], w.at[q_part], sem.at[2 * d]),
                        pltpu.make_async_copy(refs[1].at[p_part], w.at[p_spot], sem.at[2 * d + 1]),
                    ]
                )
            return copies

        def merge_moves(info, refs, h, i, slot, sem):
            wide = slot.shape[1]
            part = refs[0].at[i * DV : (i + 1) * DV, h * wide : (h + 1) * wide]
            return [pltpu.make_async_copy(part, slot, sem.at[0])]

        def position(info, i):
            return i

    def encode(first, pieces, buf):
        count = pieces[0].shape[0]
        info = jnp.concatenate([jnp.stack([t, s]), first + jnp.arange(count, dtype=jnp.int32)])
        return attend(
            tp, info, pieces, vit_weights, vit_moves, vit_count,
            vit_gain[:, None], merge_gain[None, :], blocks, buf,
        )

    merged = None
    if paired:
        by1, by2 = near
        own = tie(full[mid:], (far, vit_weights[2:]))
        merged = encode(0, [full[:mid], by1, by2, far], None)
        by1, by2 = sides_of_tp(own)
        merged, by2 = lax.optimization_barrier((merged, by2))
        merge_sides = [jnp.concatenate(pair) for pair in zip(early, merge_sides)]
        merge_corners = corners(*merge_sides)
        far, merge_sides = lax.optimization_barrier((tp_xor(by2, 1), merge_sides))
        merged = encode(mid, [full[mid:], by1, by2, far], merged)
        merged, merge_corners = lax.optimization_barrier((merged, merge_corners))
        merge_weights = with_cores([w_merge, *merge_sides, *merge_corners])
    else:
        for first in (0, mid):
            merged = encode(first, spread(full[first : first + mid]), merged)
    partial_value = project(
        jnp.stack([t, s]), merged, merge_weights, merge_moves, position, w_cache, llm_gain[None, :]
    )
    summed = lax.psum_scatter(partial_value, "tp", scatter_dimension=0, tiled=True).astype(F32)
    kvw = w_cache.shape[1]
    cache, total_squares = summed[:, :kvw], summed[:, kvw : kvw + 1]
    share = cache.shape[0]
    live_tokens = jnp.repeat(live_here.reshape(-1), tokens)
    mine = lax.dynamic_slice_in_dim(live_tokens, t * share, share).astype(F32)
    return (cache * lax.rsqrt(total_squares / D + 1e-6) * mine[:, None]).astype(BF)


def solution(mesh):
    return jax.shard_map(
        shards,
        mesh=mesh,
        in_specs=(
            P("seq", "tp"),
            P("seq", None),
            P("seq", None),
            P("seq"),
            P(None, "tp"),
            P("tp", None),
            P(),
            P(),
            P("seq", "tp"),
            P("tp"),
            P("tp", None),
        ),
        out_specs=P(("seq", "tp"), None),
        check_vma=False,
    )
```
